32 devices in a mesh: dp: 8 (over y, x, core), mp: 4 (over z).
Axes of the slice: x: 2, y: 2, z: 4, core: 2. Of those that a mesh axis runs over, the one named last changes fastest.
Arguments:
- tokens: bfloat16 [320, 48, 1024], P('mp', 'dp'), may hold values from -6 to 6
- counts: int32 [48], P('dp'), may hold values from 1 to 256, as said below
- norm_gains: float32 [2, 1024], replicated, may hold values from 0.1 to 1.9
- norm_shifts: float32 [2, 1024], replicated, may hold values from -1 to 1
- qkv_weight: bfloat16 [3, 1024, 1024], P(None, 'dp', 'mp'), may hold values from -0.1875 to 0.1875
- qkv_bias: float32 [2, 1024], P(None, 'mp'), may hold values from -1.5 to 1.5
- proj_weight: bfloat16 [1024, 1024], P('mp', 'dp'), may hold values from -2 to 2
- out_biases: float32 [2, 1024], replicated, may hold values from -1.5 to 1.5
- up_weight: bfloat16 [1024, 4096], P('dp', 'mp'), may hold values from -0.1875 to 0.1875
- up_bias: float32 [4096], P('mp'), may hold values from -1.5 to 1.5
- down_weight: bfloat16 [4096, 1024], P('mp', 'dp'), may hold values from -0.09375 to 0.09375
- cotangent: bfloat16 [320, 48, 1024], P('mp', 'dp'), may hold values from -6 to 6
Outputs:
- block_out: bfloat16 [320, 48, 1024], P('mp', 'dp')
- input_grad: bfloat16 [320, 48, 1024], P('mp', 'dp')
- gains_grad: float32 [2, 1024], replicated
- shifts_grad: float32 [2, 1024], replicated
- qkv_grad: float32 [3, 1024, 1024], P(None, 'dp', 'mp')
- bias_grad: float32 [2, 1024], P(None, 'mp')
- proj_grad: float32 [1024, 1024], P('mp', 'dp')
- outbias_grad: float32 [2, 1024], replicated
- up_grad: float32 [1024, 4096], P('dp', 'mp')
- upbias_grad: float32 [4096], P('mp')
- down_grad: float32 [4096, 1024], P('mp', 'dp')
The draws below stay inside these ranges and needn't reach their ends.
Inputs may be any that keep to these rules, and one draw needn't show every extreme that they name: `counts`: in each aligned block of 6 images one image has exactly 256 kept tokens.
All inputs are finite; a program needn't handle non-finite values.
Results may differ from the reference program's by a relative error of at most 0.012.
The reference program's roundings to bfloat16 on the way count: a program that leaves them out, or rounds other values in their place, can miss the bound.
Values may be sent and summed in bfloat16 or wider, within the bound.
No kernel may reach another device: no remote copies, remote signals or barrier semaphores. Data moves between devices by JAX's collectives and lax.ppermute only.
A program may use at most 128 MiB of HBM per device.

```python
import jax
import jax.numpy as jnp
from jax import lax

D = 1024
HEADS = 16
HEAD = 64
FF = 4096
BUF = 64
KEPT = 256
IMG_DEV = 6
SLOTS = 320
IMAGES = 48
N_DP = 8


def draw_counts(key, part):
    key = jax.random.fold_in(key, 7)
    first_key, second_key = jax.random.split(key)
    base_counts = jax.random.randint(first_key, (IMAGES,), 1, KEPT + 1)
    chosen = jax.random.randint(second_key, (IMAGES // IMG_DEV,), 0, IMG_DEV)
    image_ids = jnp.arange(IMAGES)
    is_full = image_ids % IMG_DEV == chosen[image_ids // IMG_DEV]
    return jnp.where(is_full, KEPT, base_counts).astype(jnp.int32)


def with_spikes(entries, own_key, source, target, blocks, factor):
    owner, partner = [(jnp.arange(entries.shape[position]) // (entries.shape[position] // blocks)).reshape([-1 if axis == position else 1 for axis in range(entries.ndim)]) for position in (source, target)]
    chosen = jax.random.permutation(own_key, blocks)[partner]
    strong = (owner == chosen) | (owner == (partner + blocks // 2) % blocks)
    return jnp.where(strong, factor * entries, entries)


def block_levels(own_key, extent, pieces, least, top_value):
    def one(dim, shards_of):
        steps = jax.random.uniform(jax.random.fold_in(jax.random.fold_in(own_key, 6), dim), (shards_of,), jnp.float32, least / len(pieces), top_value / len(pieces))
        return jnp.repeat(jnp.exp(steps), extent[dim] // shards_of).reshape((-1,) + (1,) * (len(extent) - dim - 1))

    factor_of = one(*pieces[0])
    for cut in pieces[1:]:
        factor_of = factor_of * one(*cut)
    return factor_of


def scatter_about(rng, shape, scale, limit, pieces=(), kind=jnp.bfloat16):
    loudness = block_levels(rng, shape, pieces, -0.22, 0.18) if pieces else 1.0
    drawn = jax.random.normal(rng, shape, jnp.float32) * scale * loudness
    return jnp.minimum(jnp.maximum(drawn, -limit), limit).astype(kind)


def gaussian_with(stream_key, extent, scale, bound, cuts, heavy, kind=jnp.bfloat16):
    array = scale * jax.random.normal(stream_key, extent, jnp.float32)
    if cuts:
        array = array * block_levels(stream_key, extent, cuts, -0.22, 0.18)
    return jnp.clip(with_spikes(array, jax.random.fold_in(stream_key, 3), *heavy), -bound, bound).astype(kind)


def setup_inputs(seed: int = 0) -> dict:
    key_list = jax.random.split(jax.random.key(seed), 13)
    return {
        "tokens": gaussian_with(key_list[0], (SLOTS, IMAGES, D), 1.0, 6.0, ((0, 4), (1, 8)), (1, 2, 8, 2.0)),
        "counts": draw_counts(jax.random.fold_in(key_list[12], 71), 0),
        "norm_gains": jnp.clip(1.0 + 0.18 * jax.random.normal(key_list[2], (2, D), jnp.float32), 0.1, 1.9),
        "norm_shifts": scatter_about(key_list[3], (2, D), 0.2, 1.0, (), jnp.float32),
        "qkv_weight": scatter_about(key_list[4], (3, D, D), D ** -0.5, 0.1875, ((1, 8), (2, 4))),
        "qkv_bias": scatter_about(key_list[5], (2, D), 0.3, 1.5, ((1, 4),), jnp.float32),
        "proj_weight": scatter_about(key_list[6], (D, D), (max(D // 128, 1)) ** -0.5, 2.0, ((0, 4), (1, 8))),
        "out_biases": scatter_about(key_list[7], (2, D), 0.3, 1.5, (), jnp.float32),
        "up_weight": scatter_about(key_list[8], (D, FF), D ** -0.5, 0.1875, ((0, 8), (1, 4))),
        "up_bias": scatter_about(key_list[9], (FF,), 0.3, 1.5, ((0, 4),), jnp.float32),
        "down_weight": scatter_about(key_list[10], (FF, D), FF ** -0.5, 0.09375, ((0, 4), (1, 8))),
        "cotangent": gaussian_with(key_list[11], (SLOTS, IMAGES, D), 1.0, 6.0, ((0, 4), (1, 8)), (1, 2, 8, 2.0)),
    }


@jax.custom_vjp
def low(v):
    return lax.optimization_barrier(v.astype(jnp.bfloat16)).astype(jnp.float32)

@jax.custom_vjp
def low_back(v):
    return v

def low_keep(v):
    return (low(v), None)

def low_pass(kept, grad):
    return (grad,)

def back_keep(v):
    return (v, None)

def back_low(kept, grad):
    return (low(grad),)
low.defvjp(low_keep, low_pass)
low_back.defvjp(back_keep, back_low)
epsilon = 1e-06
masked_score = -1e+30
highest = lax.Precision.HIGHEST

def layer_norm(values, scales, shifts):
    average = lax.optimization_barrier(jnp.mean(values, axis=-1, keepdims=True))
    centred = values - average
    spread = lax.optimization_barrier(jnp.mean(centred * centred, axis=-1, keepdims=True))
    return centred * lax.rsqrt(spread + epsilon) * scales + shifts

def layer_forward(valid_mask, tokens32, weight_set):
    norm_gains, norm_shifts, qkv_weight, qkv_bias, proj_weight, out_biases, up_weight, up_bias, down_weight = weight_set
    slot_count, images, model_width = tokens32.shape
    normed_one = low(layer_norm(tokens32, norm_gains[0], norm_shifts[0]))
    projected = jnp.einsum('sbd,tde->tsbe', normed_one, qkv_weight, precision=highest)
    bias_rows = jnp.stack([qkv_bias[0], jnp.zeros_like(qkv_bias[0]), qkv_bias[1]])
    qkv_all = low(low_back(projected + bias_rows[:, None, None, :]))
    qkv_heads = qkv_all.reshape(3, slot_count, images, HEADS, HEAD)
    scores = jnp.einsum('qbhe,kbhe->bhqk', qkv_heads[0], qkv_heads[1], precision=highest) * HEAD ** (-0.5)
    scores = low_back(scores)
    allowed = jnp.transpose(valid_mask)[:, None, None, :] > 0.5
    scores = jnp.where(allowed, scores, masked_score)
    top_score = lax.optimization_barrier(jnp.max(scores, axis=-1, keepdims=True))
    powers = jnp.exp(scores - top_score)
    attn_weights = low(powers / lax.optimization_barrier(jnp.sum(powers, axis=-1, keepdims=True)))
    mixture = jnp.einsum('bhqk,kbhe->qbhe', attn_weights, qkv_heads[2], precision=highest)
    mixture = low(low_back(mixture.reshape(slot_count, images, model_width)))
    attended = low_back(jnp.einsum('sbe,ed->sbd', mixture, proj_weight, precision=highest)) + out_biases[0]
    hidden = tokens32 + attended
    normed_two = low(layer_norm(hidden, norm_gains[1], norm_shifts[1]))
    up_pre = low_back(jnp.einsum('sbd,df->sbf', normed_two, up_weight, precision=highest) + up_bias)
    up_act = low(jax.nn.gelu(up_pre, approximate=False))
    branch = low_back(jnp.einsum('sbf,fd->sbd', up_act, down_weight, precision=highest)) + out_biases[1]
    return (hidden + branch) * valid_mask[:, :, None]

def reference(tokens, counts, norm_gains, norm_shifts, qkv_weight, qkv_bias, proj_weight, out_biases, up_weight, up_bias, down_weight, cotangent):
    slot_ids = jnp.arange(SLOTS, dtype=jnp.int32)
    valid_all = (slot_ids[:, None] < BUF + counts[None, :]).astype(jnp.float32)
    params = (norm_gains, norm_shifts, qkv_weight.astype(jnp.float32), qkv_bias, proj_weight.astype(jnp.float32), out_biases, up_weight.astype(jnp.float32), up_bias, down_weight.astype(jnp.float32))

    def one_group(totals, group_index):
        offset = (group_index * IMG_DEV).astype(jnp.int32)
        group_tokens = lax.dynamic_slice_in_dim(tokens, offset, IMG_DEV, 1).astype(jnp.float32)
        group_cot = lax.dynamic_slice_in_dim(cotangent, offset, IMG_DEV, 1).astype(jnp.float32)
        group_valid = lax.dynamic_slice_in_dim(valid_all, offset, IMG_DEV, 1)
        result, pullback = jax.vjp(lambda token_rows, weight_set: layer_forward(group_valid, token_rows, weight_set), group_tokens, params)
        grads_in, grads_params = pullback(group_cot)
        totals = jax.tree.map(jnp.add, totals, grads_params)
        return (totals, (result.astype(jnp.bfloat16), grads_in.astype(jnp.bfloat16)))
    initial = jax.tree.map(jnp.zeros_like, params)
    totals, stacked = lax.scan(one_group, initial, jnp.arange(N_DP, dtype=jnp.int32))
    outputs, input_grads = stacked
    block_out = jnp.moveaxis(outputs, 0, 1).reshape(SLOTS, IMG_DEV * N_DP, D)
    input_grad = jnp.moveaxis(input_grads, 0, 1).reshape(SLOTS, IMG_DEV * N_DP, D)
    return (block_out, input_grad, totals[0], totals[1], totals[2], totals[3], totals[4], totals[5], totals[6], totals[7], totals[8])
```

```python
import jax
import jax.numpy as jnp
from jax import lax
from jax.sharding import PartitionSpec as P

HEAD = 64
BUF = 64
BF = jnp.bfloat16
F32 = jnp.float32

epsilon = 1e-06
masked_score = -1e30


def swap(x, axis, bits):
    n = lax.axis_size(axis)
    return lax.ppermute(x, axis, [(i, i ^ bits) for i in range(n)])


def gather_q(own):
    n_q = lax.axis_size("dp") // 2
    if n_q != 4:
        blocks = own[None]
        bit = 1
        while bit < n_q:
            blocks = jnp.concatenate([blocks, swap(blocks, "dp", 2 * bit)])
            bit *= 2
        return blocks
    half = own.shape[0] // 2
    one = swap(own, "dp", 2)
    two = swap(own, "dp", 4)
    three = jnp.concatenate([swap(one[:half], "dp", 4), swap(two[half:], "dp", 2)])
    return jnp.stack([own, one, two, three])


def add(*parts):
    total = parts[0].astype(F32)
    for part in parts[1:]:
        total = total + part.astype(F32)
    return total.astype(parts[0].dtype)


def scatter_q(parts):
    n_q = lax.axis_size("dp") // 2
    if n_q != 4:
        bit = n_q // 2
        while bit >= 1:
            parts = add(parts[:bit], swap(parts[bit:], "dp", 2 * bit))
            bit //= 2
        return parts[0]
    half = parts.shape[1] // 2
    into_one = swap(parts[3][:half], "dp", 4)
    into_two = swap(parts[3][half:], "dp", 2)
    one = jnp.concatenate([add(parts[1][:half], into_one), parts[1][half:]])
    two = jnp.concatenate([parts[2][:half], add(parts[2][half:], into_two)])
    return add(parts[0], swap(one, "dp", 2), swap(two, "dp", 4))


def gather_z(own):
    two = swap(own, "mp", 2)
    one = swap(own, "mp", 1)
    three = swap(two, "mp", 1)
    return jnp.stack([own, one, two, three])


def scatter_z(parts):
    into_two = swap(parts[3], "mp", 1)
    return add(parts[0], swap(parts[1], "mp", 1), swap(add(parts[2], into_two), "mp", 2))


def ordered_pair(own, other, core):
    return jnp.stack([jnp.where(core == 0, own, other), jnp.where(core == 0, other, own)])


def image_routes(n_dp, n_mp, odd):
    pairs = []
    for plane in range(n_dp // 2):
        for core in range(2):
            for z in range(n_mp):
                shift = 2 * core + odd
                worker = (plane * 2 + core) * n_mp + z
                holder = (plane * 2 + (z >> 1)) * n_mp + (z ^ shift)
                pairs.append((holder, worker))
    return pairs


def to_images(x, core, z):
    n_dp, n_mp = lax.axis_size("dp"), lax.axis_size("mp")
    slots, images, width = x.shape
    groups = jnp.transpose(x, (1, 0, 2)).reshape(2, images // 2, slots, width)
    got = []
    for odd in (0, 1):
        which = (z ^ odd) & 1
        send = lax.dynamic_index_in_dim(groups, which, 0, False)
        got.append(lax.ppermute(send, ("dp", "mp"), image_routes(n_dp, n_mp, odd)))
    return jnp.stack(got, 1)


def from_images(y, core, z):
    n_dp, n_mp = lax.axis_size("dp"), lax.axis_size("mp")
    back = []
    for odd in (0, 1):
        routes = [(b, a) for a, b in image_routes(n_dp, n_mp, odd)]
        back.append(lax.ppermute(y[:, odd], ("dp", "mp"), routes))
    flip = (z & 1) == 1
    groups = jnp.concatenate([jnp.where(flip, back[1], back[0]), jnp.where(flip, back[0], back[1])])
    return jnp.transpose(groups, (1, 0, 2))


def layer_norm(values, scales, shifts):
    average = jnp.mean(values, axis=-1, keepdims=True)
    centred = values - average
    spread = jnp.mean(centred * centred, axis=-1, keepdims=True)
    inv = lax.rsqrt(spread + epsilon)
    n = centred * inv
    return n * scales + shifts, n, inv


def layer_norm_back(n, inv, scales, grad):
    e = grad * scales
    mean_e = jnp.mean(e, axis=-1, keepdims=True)
    mean_en = jnp.mean(e * n, axis=-1, keepdims=True)
    return (e - mean_e - n * mean_en) * inv


def gelu_parts(inputs):
    normal_cdf = 0.5 * (1.0 + lax.erf(inputs * 0.7071067811865476))
    density = jnp.exp(-0.5 * inputs * inputs) * 0.3989422804014327
    return inputs * normal_cdf, normal_cdf + inputs * density


def local(
    tokens,
    counts,
    norm_gains,
    norm_shifts,
    qkv_weight,
    qkv_bias,
    proj_weight,
    out_biases,
    up_weight,
    up_bias,
    down_weight,
    cotangent,
):
    slots, images, width = tokens.shape
    n_dp, n_mp = lax.axis_size("dp"), lax.axis_size("mp")
    n_q = n_dp // 2
    wq = width // n_q
    dp, z = lax.axis_index("dp"), lax.axis_index("mp")
    q, core = dp >> 1, dp & 1
    own_images = images // 2
    all_slots = slots * n_mp
    rows = own_images * all_slots

    def rel(v):
        blocks = [lax.dynamic_slice_in_dim(v, (q ^ j) * wq, wq, v.ndim - 1) for j in range(n_q)]
        return jnp.concatenate(blocks, -1)

    def half_of(v, which, axis):
        size = v.shape[axis] // 2
        return lax.dynamic_slice_in_dim(v, which * size, size, axis)

    att = jnp.concatenate([qkv_weight, jnp.transpose(proj_weight)[None]])
    ffn = jnp.stack([up_weight, jnp.transpose(down_weight)])
    att_own = ordered_pair(half_of(att, core, 2), swap(half_of(att, 1 - core, 2), "dp", 1), core)
    att_own = jnp.transpose(att_own, (1, 0, 2, 3)).reshape(4, wq, -1)
    ffn_own = ordered_pair(half_of(ffn, core, 2), swap(half_of(ffn, 1 - core, 2), "dp", 1), core)
    ffn_own = jnp.transpose(ffn_own, (1, 0, 2, 3)).reshape(2, wq, -1)
    bias_own = jnp.concatenate(
        [half_of(qkv_bias, core, 1), half_of(up_bias, core, 0).reshape(-1, 128)]
    )
    bias_all = gather_z(bias_own)
    att_all = gather_q(gather_z(att_own))
    ffn_z = gather_z(ffn_own)
    ffn_all = [gather_q(ffn_z[:2]), gather_q(ffn_z[2:])]

    def whole_rows(v):
        got = to_images(rel(v), core, z)
        pair = ordered_pair(got, swap(got, "dp", 1), core)
        return jnp.transpose(pair, (1, 0, 2, 3, 4)).reshape(rows, width)

    other_counts = swap(counts, "dp", 1)
    source = z >> 1
    counts_here = jnp.where(source == core, counts, other_counts)
    counts_here = lax.dynamic_slice_in_dim(counts_here, (z & 1) * own_images, own_images, 0)
    slot_of = (z ^ jnp.arange(n_mp, dtype=jnp.int32))[:, None] * slots + jnp.arange(slots, dtype=jnp.int32)
    valid = (slot_of.reshape(1, -1) < BUF + counts_here[:, None])
    keep_mine = (z * slots + jnp.arange(slots, dtype=jnp.int32))[:, None] < BUF + counts[None, :]

    x = whole_rows(tokens)
    go = whole_rows(jnp.where(keep_mine[:, :, None], cotangent, jnp.zeros_like(cotangent)))
    gains, shifts, out_b = rel(norm_gains), rel(norm_shifts), rel(out_biases)

    x32 = x.astype(F32)
    n1f, hat1, inv1 = layer_norm(x32, gains[0], shifts[0])
    n1 = n1f.astype(BF)
    n_i, he = att_all.shape[1], att_all.shape[-1]
    heads = n_i * he // HEAD
    w_att = jnp.transpose(att_all, (2, 0, 3, 1, 4)).reshape(4, width, n_i * he)
    bias_rows = jnp.stack([bias_all[:, 0], jnp.zeros_like(bias_all[:, 0]), bias_all[:, 1]]).reshape(3, 1, -1)
    qkv = (jnp.einsum("rd,tde->tre", n1, w_att[:3], preferred_element_type=F32) + bias_rows).astype(BF)
    qkv = qkv.reshape(3, own_images, all_slots, heads, HEAD)
    factor = HEAD ** (-0.5)
    scores = jnp.einsum("bqhe,bkhe->bhqk", qkv[0], qkv[1], preferred_element_type=F32) * factor
    scores = jnp.where(valid[:, None, None, :], scores, masked_score)
    top = jnp.max(scores, axis=-1, keepdims=True)
    powers = jnp.exp(scores - top)
    probs = powers / jnp.sum(powers, axis=-1, keepdims=True)
    probs_low = probs.astype(BF)
    mixture = jnp.einsum("bhqk,bkhe->bqhe", probs_low, qkv[2], preferred_element_type=F32)
    mixture = mixture.astype(BF).reshape(rows, heads * HEAD)

    part = jnp.einsum("re,de->rd", mixture, w_att[3], preferred_element_type=F32).astype(BF)
    hidden = x32 + add(part.astype(F32), swap(part, "dp", 1)) + out_b[0]
    n2f, hat2, inv2 = layer_norm(hidden, gains[1], shifts[1])
    n2 = n2f.astype(BF)

    branch = 0.0
    gn2 = 0.0
    ffn_grads = []
    upbias_parts = []
    for group in (0, 1):
        w = ffn_all[group]
        w = jnp.transpose(w, (2, 0, 3, 1, 4)).reshape(2, width, -1)
        bias = bias_all[2 * group : 2 * group + 2, 2:].reshape(-1)
        up_pre = jnp.einsum("rd,df->rf", n2, w[0], preferred_element_type=F32) + bias
        act, slope = gelu_parts(up_pre)
        act = act.astype(BF)
        branch = branch + jnp.einsum("rf,df->rd", act, w[1], preferred_element_type=F32)
        grad_act = jnp.einsum("rd,df->rf", go, w[1], preferred_element_type=F32)
        grad_pre = (grad_act * slope).astype(BF)
        gn2 = gn2 + jnp.einsum("rf,df->rd", grad_pre, w[0], preferred_element_type=F32)
        up_g = jnp.einsum("rd,rf->df", n2, grad_pre, preferred_element_type=F32).astype(BF)
        down_g = jnp.einsum("rd,rf->df", go, act, preferred_element_type=F32).astype(BF)
        upbias_parts.append(jnp.sum(grad_pre.astype(F32), 0))
        g = jnp.stack([up_g, down_g]).reshape(2, n_q, wq, 2, -1)
        ffn_grads.append(scatter_q(jnp.transpose(g, (1, 3, 0, 2, 4))))
    ffn_grad = scatter_z(jnp.concatenate(ffn_grads))

    row_half = lambda v, which: half_of(v.reshape(own_images, n_mp, slots, width), which, 1)
    branch = branch.astype(BF)
    mine = row_half(branch, core).astype(F32)
    theirs = swap(row_half(branch, 1 - core), "dp", 1).astype(F32)
    out_half = row_half(hidden, core) + mine + theirs + out_b[1]
    block_out = from_images(rel(out_half.astype(BF)), core, z)
    block_out = jnp.where(keep_mine[:, :, None], block_out, jnp.zeros_like(block_out))

    gn2 = gn2.astype(BF)
    gn2 = gn2.astype(F32) + swap(gn2, "dp", 1).astype(F32)
    grad_hidden = go.astype(F32) + layer_norm_back(hat2, inv2, gains[1], gn2)
    gain_two, shift_two = jnp.sum(gn2 * hat2, 0), jnp.sum(gn2, 0)
    gh = grad_hidden.astype(BF)
    proj_g = jnp.einsum("rd,re->de", gh, mixture, preferred_element_type=F32).astype(BF)
    grad_mix = jnp.einsum("rd,de->re", gh, w_att[3], preferred_element_type=F32).astype(BF)
    grad_mix = grad_mix.reshape(own_images, all_slots, heads, HEAD)
    grad_probs = jnp.einsum("bqhe,bkhe->bhqk", grad_mix, qkv[2], preferred_element_type=F32)
    row_dot = jnp.sum(probs * grad_probs, axis=-1, keepdims=True)
    grad_scores = (probs * (grad_probs - row_dot)).astype(BF)
    grad_q = jnp.einsum("bhqk,bkhe->bqhe", grad_scores, qkv[1], preferred_element_type=F32) * factor
    grad_k = jnp.einsum("bhqk,bqhe->bkhe", grad_scores, qkv[0], preferred_element_type=F32) * factor
    grad_v = jnp.einsum("bhqk,bqhe->bkhe", probs_low, grad_mix, preferred_element_type=F32)
    grad_qkv = jnp.stack([grad_q, grad_k, grad_v]).astype(BF).reshape(3, rows, heads * HEAD)
    qkv_g = jnp.einsum("rd,tre->tde", n1, grad_qkv, preferred_element_type=F32).astype(BF)
    bias_part = jnp.stack([jnp.sum(grad_qkv[0].astype(F32), 0), jnp.sum(grad_qkv[2].astype(F32), 0)])
    att_g = jnp.concatenate([qkv_g, proj_g[None]]).reshape(4, n_q, wq, n_i, he)
    att_grad = scatter_z(scatter_q(jnp.transpose(att_g, (1, 3, 0, 2, 4))))

    gn1 = jnp.einsum("tre,tde->rd", grad_qkv, w_att[:3], preferred_element_type=F32).astype(BF)
    gn1 = row_half(gn1, core).astype(F32) + swap(row_half(gn1, 1 - core), "dp", 1).astype(F32)
    my_hat1, my_inv1 = row_half(hat1, core), half_of(inv1.reshape(own_images, n_mp, slots, 1), core, 1)
    input_half = row_half(grad_hidden, core) + layer_norm_back(my_hat1, my_inv1, gains[0], gn1)
    gain_one, shift_one = jnp.sum(gn1 * my_hat1, (0, 1, 2)), jnp.sum(gn1, (0, 1, 2))
    input_grad = from_images(rel(input_half.astype(BF)), core, z)

    def own_shard(grad, last):
        kinds = grad.shape[0]
        pair = grad.reshape(kinds, 2, wq // 2, last // 2)
        keep = lax.dynamic_index_in_dim(pair, core, 1, False)
        got = swap(lax.dynamic_index_in_dim(pair, 1 - core, 1, False), "dp", 1)
        both = ordered_pair(keep, got, core)
        return jnp.transpose(both, (1, 2, 0, 3)).reshape(kinds, wq // 2, last).astype(F32)

    att_shard = own_shard(att_grad, 2 * he)
    ffn_shard = own_shard(ffn_grad, 2 * ffn_own.shape[-1])
    qkv_owned, proj_owned = att_shard[:3], jnp.transpose(att_shard[3])
    up_owned, down_owned = ffn_shard[0], jnp.transpose(ffn_shard[1])

    fh = ffn_own.shape[-1]
    wide_up = jnp.zeros((n_mp, 2, fh), F32)
    wide_bias = jnp.zeros((2, n_mp, 2, he), F32)
    ups = jnp.concatenate(upbias_parts).reshape(n_mp, fh)
    biases = bias_part.reshape(2, n_mp, he)
    for i in range(n_mp):
        wide_up = lax.dynamic_update_slice(wide_up, ups[i][None, None], (z ^ i, core, 0))
        wide_bias = lax.dynamic_update_slice(wide_bias, biases[:, i][:, None, None], (0, z ^ i, core, 0))
    go_half = row_half(go, core).astype(F32)
    gh_half = row_half(grad_hidden, core)
    small = rel(
        jnp.stack(
            [
                gain_one,
                gain_two * 0.5,
                shift_one,
                shift_two * 0.5,
                jnp.sum(gh_half, (0, 1, 2)),
                jnp.sum(go_half, (0, 1, 2)),
            ]
        )
    )
    small, wide_bias, wide_up = lax.psum((small, wide_bias, wide_up), ("dp", "mp"))
    bias_grad = lax.dynamic_index_in_dim(wide_bias, z, 1, False).reshape(2, -1)
    upbias_grad = lax.dynamic_index_in_dim(wide_up, z, 0, False).reshape(-1)
    return (
        block_out,
        input_grad,
        small[0:2],
        small[2:4],
        qkv_owned,
        bias_grad,
        proj_owned,
        small[4:6],
        up_owned,
        upbias_grad,
        down_owned,
    )


def solution(mesh):
    return jax.shard_map(
        local,
        mesh=mesh,
        in_specs=(
            P("mp", "dp", None),
            P("dp"),
            P(),
            P(),
            P(None, "dp", "mp"),
            P(None, "mp"),
            P("mp", "dp"),
            P(),
            P("dp", "mp"),
            P("mp"),
            P("mp", "dp"),
            P("mp", "dp", None),
        ),
        out_specs=(
            P("mp", "dp", None),
            P("mp", "dp", None),
            P(),
            P(),
            P(None, "dp", "mp"),
            P(None, "mp"),
            P("mp", "dp"),
            P(),
            P("dp", "mp"),
            P("mp"),
            P("mp", "dp"),
        ),
        check_vma=False,
    )
```

```python
import functools

import jax
import jax.numpy as jnp
from jax import lax
from jax.experimental import pallas as pl
from jax.experimental.pallas import tpu as pltpu
from jax.sharding import PartitionSpec as P

HEAD = 64
BUF = 64
BF = jnp.bfloat16
F32 = jnp.float32
epsilon = 1e-06
masked_score = -1e30
MIB = 1 << 20
NT = (((1,), (1,)), ((), ()))
NN = (((1,), (0,)), ((), ()))
TN = (((0,), (0,)), ((), ()))
factor = HEAD ** (-0.5)
VMEM_SPEC = pl.BlockSpec(memory_space=pltpu.VMEM)
ANY_SPEC = pl.BlockSpec(memory_space=pl.ANY)


def mm(a, b, dims=NN):
    return lax.dot_general(a, b, dims, preferred_element_type=F32)


def normalise(values):
    average = jnp.mean(values, axis=-1, keepdims=True)
    centred = values - average
    spread = jnp.mean(centred * centred, axis=-1, keepdims=True)
    inv = lax.rsqrt(spread + epsilon)
    return centred * inv, inv


def norm_back(n, inv, scales, grad):
    e = grad * scales
    mean_e = jnp.mean(e, axis=-1, keepdims=True)
    mean_en = jnp.mean(e * n, axis=-1, keepdims=True)
    return (e - mean_e - n * mean_en) * inv


def gelu_parts(inputs):
    normal_cdf = 0.5 + 0.5 * lax.erf(inputs * 0.7071067811865476)
    density = jnp.exp(-0.5 * inputs * inputs) * 0.3989422804014327
    return inputs * normal_cdf, normal_cdf + inputs * density


def for_each(count, step):
    if count <= 4:
        for index in range(count):
            step(index)
    else:
        pl.loop(0, count)(step)


def copy_att(parts, refs, w_scr, sem, kinds, n_i):
    for (j0, i0), ref in zip(parts, refs):
        nj, ni, _, wq, he = ref.shape

        def one(jj, ref=ref, j0=j0, i0=i0, ni=ni, wq=wq, he=he):
            rows = pl.ds(pl.multiple_of((j0 + jj) * wq, wq), wq) if not isinstance(jj, int) else pl.ds((j0 + jj) * wq, wq)
            for ii in range(ni):
                for t in range(kinds):
                    pltpu.make_async_copy(
                        ref.at[jj, ii, t], w_scr.at[rows, pl.ds((t * n_i + i0 + ii) * he, he)], sem
                    ).start()

        for_each(nj, one)
    pltpu.make_async_copy(w_scr, w_scr, sem).wait()


def att_fwd_kernel(parts, n_i, x_ref, g_ref, c_ref, bias_ref, valid_ref, *rest):
    w_refs = rest[: len(parts)]
    n1_ref, qkv_ref, mix_ref, part_ref, w_scr, m_scr, sem = rest[len(parts) :]
    he = 2 * HEAD

    @pl.when(pl.program_id(0) == 0)
    def _():
        copy_att(parts, w_refs, w_scr, sem, 4, n_i)

    hat, _ = normalise(x_ref[0].astype(F32))
    n1 = (hat * g_ref[...] + c_ref[...]).astype(BF)
    n1_ref[...] = n1
    for t in range(3):
        cols = pl.ds(t * n_i * he, n_i * he)
        res = (mm(n1, w_scr[:, cols]) + bias_ref[:, cols]).astype(BF)
        for i in range(n_i):
            qkv_ref[t * n_i + i] = res[:, i * he : (i + 1) * he]
    bias = jnp.where(valid_ref[0] > 0.5, 0.0, masked_score)
    lane = lax.broadcasted_iota(jnp.int32, (1, he), 1)
    low_half = lane < HEAD
    for i in range(n_i):
        q2, k2, v2 = qkv_ref[i], qkv_ref[n_i + i], qkv_ref[2 * n_i + i]
        outs = []
        for h in range(2):
            qm = jnp.where(low_half if h == 0 else ~low_half, q2, jnp.zeros_like(q2))
            s = mm(qm, k2, NT) * factor + bias
            top = jnp.max(s, axis=-1, keepdims=True)
            p = jnp.exp(s - top)
            w = (p / jnp.sum(p, axis=-1, keepdims=True)).astype(BF)
            outs.append(mm(w, v2))
        mixed = jnp.where(low_half, outs[0], outs[1]).astype(BF)
        m_scr[:, i * he : (i + 1) * he] = mixed
    mix_ref[...] = m_scr[...]
    part_ref[...] = mm(m_scr[...], w_scr[:, 3 * n_i * he :], NT).astype(BF)


def att_forward(x, gain, shift, bias, valid, parts, arrays, cost=True):
    images, slots, width = x.shape
    n_i = 4
    he = 2 * HEAD
    rows = images * slots
    row_block = lambda last: pl.BlockSpec((slots, last), lambda a: (a, 0))
    whole = lambda *shape: pl.BlockSpec(shape, lambda a: (0,) * len(shape))
    return pl.pallas_call(
        functools.partial(att_fwd_kernel, parts, n_i),
        grid=(images,),
        in_specs=[
            pl.BlockSpec((1, slots, width), lambda a: (a, 0, 0)),
            whole(1, width),
            whole(1, width),
            whole(1, 3 * n_i * he),
            pl.BlockSpec((1, 1, slots), lambda a: (a, 0, 0)),
        ]
        + [ANY_SPEC] * len(arrays),
        out_specs=[
            row_block(width),
            pl.BlockSpec((3 * n_i, slots, he), lambda a: (0, a, 0)),
            row_block(n_i * he),
            row_block(width),
        ],
        out_shape=[
            jax.ShapeDtypeStruct((rows, width), BF),
            jax.ShapeDtypeStruct((3 * n_i, rows, he), BF),
            jax.ShapeDtypeStruct((rows, n_i * he), BF),
            jax.ShapeDtypeStruct((rows, width), BF),
        ],
        scratch_shapes=[
            pltpu.VMEM((width, 4 * n_i * he), BF),
            pltpu.VMEM((slots, n_i * he), BF),
            pltpu.SemaphoreType.DMA,
        ],
        compiler_params=pltpu.CompilerParams(vmem_limit_bytes=32 * MIB),
        cost_estimate=pl.CostEstimate(flops=8_000_000_000, bytes_accessed=20_000_000, transcendentals=2_500_000),
        name="att_forward",
    )(x, gain, shift, bias, valid, *arrays)


def ffn_kernel(
    parts, n_i, last, x_ref, pa_ref, pb_ref, b_ref, g_ref, c_ref, go_ref, upb_ref, *rest
):
    w_refs = rest[: len(parts)]
    hidden_ref, branch_ref, gn2_ref, grads_ref, upg_ref = rest[len(parts) : len(parts) + 5]
    n2, n2t, got, acc_b, acc_g, wbuf, gbuf, act_s, pre_s, wsem, gsem = rest[len(parts) + 5 :]
    rows, width = x_ref.shape
    fh = last
    n_j, _, _, wq, _ = grads_ref.shape

    def fetch(i, slot):
        for (j0, i0), ref in zip(parts, w_refs):
            nj, ni = ref.shape[:2]
            if not i0 <= i < i0 + ni:
                continue

            def one(jj, ref=ref, j0=j0, i0=i0):
                start = (j0 + jj) * wq
                rws = pl.ds(start if isinstance(jj, int) else pl.multiple_of(start, wq), wq)
                for kind in range(2):
                    pltpu.make_async_copy(
                        ref.at[jj, i - i0, kind], wbuf.at[slot, kind, rws], wsem.at[slot]
                    ).start()

            for_each(nj, one)

    def fetched(slot):
        pltpu.make_async_copy(wbuf.at[slot], wbuf.at[slot], wsem.at[slot]).wait()

    def put(i, slot):
        def one(jj):
            start = jj * wq
            rws = pl.ds(start if isinstance(jj, int) else pl.multiple_of(start, wq), wq)
            for kind in range(2):
                pltpu.make_async_copy(
                    gbuf.at[slot, kind, rws], grads_ref.at[jj, i, kind], gsem.at[slot]
                ).start()

        for_each(n_j, one)

    def stored(slot):
        pltpu.make_async_copy(gbuf.at[slot], gbuf.at[slot], gsem.at[slot]).wait()

    fetch(0, 0)
    block = 192

    @pl.loop(0, rows // block)
    def _(r):
        rw = pl.ds(pl.multiple_of(r * block, block), block)
        h = (
            x_ref[rw, :].astype(F32)
            + (pa_ref[rw, :].astype(F32) + pb_ref[rw, :].astype(F32))
            + b_ref[...]
        )
        hidden_ref[rw, :] = h
        hat, _ = normalise(h)
        n2[rw, :] = (hat * g_ref[...] + c_ref[...]).astype(BF)

    n2t[...] = n2[...].T
    got[...] = go_ref[...].T
    rb = rows // 3
    for i in range(n_i):
        slot = i % 2
        if i + 1 < n_i:
            fetch(i + 1, 1 - slot)
        fetched(slot)

        @pl.loop(0, 3)
        def _(r, i=i, slot=slot):
            rw = pl.ds(pl.multiple_of(r * rb, rb), rb)
            u, w = wbuf[slot, 0], wbuf[slot, 1]
            up = mm(n2[rw, :], u) + upb_ref[i : i + 1, :]
            act, slope = gelu_parts(up)
            act = act.astype(BF)
            act_s[rw, :] = act
            pre = (mm(go_ref[rw, :], w) * slope).astype(BF)
            pre_s[rw, :] = pre
            down = mm(act, w, NT)
            back = mm(pre, u, NT)
            if i == 0:
                acc_b[rw, :] = down
                acc_g[rw, :] = back
            elif i < n_i - 1:
                acc_b[rw, :] += down
                acc_g[rw, :] += back
            else:
                branch_ref[rw, :] = (acc_b[rw, :] + down).astype(BF)
                gn2_ref[rw, :] = (acc_g[rw, :] + back).astype(BF)

        upg_ref[i : i + 1, :] = jnp.sum(pre_s[...].astype(F32), axis=0, keepdims=True)
        if i >= 2:
            stored(slot)
        gbuf[slot, 0] = mm(n2t[...], pre_s[...]).astype(BF)
        gbuf[slot, 1] = mm(got[...], act_s[...]).astype(BF)
        put(i, slot)
    stored((n_i - 2) % 2)
    stored((n_i - 1) % 2)


def ffn(x, pa, pb, b0, gain, shift, go, upb, n_j, parts, arrays):
    rows, width = x.shape
    n_i, fh = upb.shape
    wq = width // n_j
    return pl.pallas_call(
        functools.partial(ffn_kernel, parts, n_i, fh),
        in_specs=[VMEM_SPEC] * 8 + [ANY_SPEC] * len(arrays),
        out_specs=[VMEM_SPEC] * 3 + [ANY_SPEC, VMEM_SPEC],
        out_shape=[
            jax.ShapeDtypeStruct((rows, width), F32),
            jax.ShapeDtypeStruct((rows, width), BF),
            jax.ShapeDtypeStruct((rows, width), BF),
            jax.ShapeDtypeStruct((n_j, n_i, 2, wq, fh), BF),
            jax.ShapeDtypeStruct((n_i, fh), F32),
        ],
        scratch_shapes=[
            pltpu.VMEM((rows, width), BF),
            pltpu.VMEM((width, rows), BF),
            pltpu.VMEM((width, rows), BF),
            pltpu.VMEM((rows, width), F32),
            pltpu.VMEM((rows, width), F32),
            pltpu.VMEM((2, 2, width, fh), BF),
            pltpu.VMEM((2, 2, width, fh), BF),
            pltpu.VMEM((rows, fh), BF),
            pltpu.VMEM((rows, fh), BF),
            pltpu.SemaphoreType.DMA((2,)),
            pltpu.SemaphoreType.DMA((2,)),
        ],
        compiler_params=pltpu.CompilerParams(vmem_limit_bytes=56 * MIB),
        cost_estimate=pl.CostEstimate(flops=36_000_000_000, bytes_accessed=30_000_000, transcendentals=4_000_000),
        name="ffn",
    )(x, pa, pb, b0, gain, shift, go, upb, *arrays)


def att_bwd_kernel(
    parts, n_i, hid_ref, ga_ref, gb_ref, g_ref, go_ref, n1_ref, qkv_ref, mix_ref, valid_ref, *rest
):
    w_refs = rest[: len(parts)]
    gh_ref, gn1_ref, grads_ref, bias_ref, sums_ref = rest[len(parts) : len(parts) + 5]
    ghb, gmix, gq, w_scr, gbuf, sem, gsem = rest[len(parts) + 5 :]
    rows, width = hid_ref.shape
    he = 2 * HEAD
    images = valid_ref.shape[0]
    slots = rows // images
    n_j, _, _, wq, _ = grads_ref.shape
    copy_att(parts, w_refs, w_scr, sem, 4, n_i)
    block = 192
    proj_cols = pl.ds(3 * n_i * he, n_i * he)
    sums_ref[...] = jnp.zeros_like(sums_ref)

    @pl.loop(0, rows // block)
    def _(r):
        rw = pl.ds(pl.multiple_of(r * block, block), block)
        hat, inv = normalise(hid_ref[rw, :])
        grad = ga_ref[rw, :].astype(F32) + gb_ref[rw, :].astype(F32)
        gout = go_ref[rw, :].astype(F32)
        gh = gout + norm_back(hat, inv, g_ref[...], grad)
        gh_ref[rw, :] = gh
        low = gh.astype(BF)
        ghb[rw, :] = low
        sums_ref[0:1, :] += jnp.sum(grad * hat, axis=0, keepdims=True)
        sums_ref[1:2, :] += jnp.sum(grad, axis=0, keepdims=True)
        sums_ref[2:3, :] += jnp.sum(gh, axis=0, keepdims=True)
        sums_ref[3:4, :] += jnp.sum(gout, axis=0, keepdims=True)
        res = mm(low, w_scr[:, proj_cols]).astype(BF)
        for i in range(n_i):
            gmix[i, rw, :] = res[:, i * he : (i + 1) * he]

    def put(kind):
        def one(jj):
            start = jj * wq
            rws = pl.ds(start if isinstance(jj, int) else pl.multiple_of(start, wq), wq)
            for i in range(n_i):
                pltpu.make_async_copy(
                    gbuf.at[kind, rws, pl.ds(i * he, he)], grads_ref.at[jj, i, kind], gsem.at[kind]
                ).start()

        for_each(n_j, one)

    gbuf[3] = mm(ghb[...].T, mix_ref[...]).astype(BF)
    put(3)
    lane = lax.broadcasted_iota(jnp.int32, (1, he), 1)
    low_half = lane < HEAD

    @pl.loop(0, images)
    def _(a):
        rw = pl.ds(pl.multiple_of(a * slots, slots), slots)
        bias = jnp.where(valid_ref[a] > 0.5, 0.0, masked_score)
        for i in range(n_i):
            q2, k2, v2 = qkv_ref[i, rw, :], qkv_ref[n_i + i, rw, :], qkv_ref[2 * n_i + i, rw, :]
            g2 = gmix[i, rw, :]
            dq, dk, dv = [], [], []
            for h in range(2):
                here = low_half if h == 0 else ~low_half
                qm = jnp.where(here, q2, jnp.zeros_like(q2))
                gm = jnp.where(here, g2, jnp.zeros_like(g2))
                st = mm(k2, qm, NT) * factor + bias
                top = jnp.max(st, axis=0, keepdims=True)
                p = jnp.exp(st - top)
                p = p / jnp.sum(p, axis=0, keepdims=True)
                dpt = mm(v2, gm, NT)
                dot = jnp.sum(p * dpt, axis=0, keepdims=True)
                ds = (p * (dpt - dot)).astype(BF)
                dk.append(mm(ds, q2))
                dv.append(mm(p.astype(BF), g2))
                dq.append(mm(ds, k2, TN))
            gq[rw, i * he : (i + 1) * he] = (jnp.where(low_half, dq[0], dq[1]) * factor).astype(BF)
            gq[rw, (n_i + i) * he : (n_i + i + 1) * he] = (
                jnp.where(low_half, dk[0], dk[1]) * factor
            ).astype(BF)
            gq[rw, (2 * n_i + i) * he : (2 * n_i + i + 1) * he] = jnp.where(
                low_half, dv[0], dv[1]
            ).astype(BF)

    n1t = n1_ref[...].T
    for t in range(3):
        cols = pl.ds(t * n_i * he, n_i * he)
        gbuf[t] = mm(n1t, gq[:, cols]).astype(BF)
        put(t)
    bias_ref[...] = jnp.sum(gq[...].astype(F32), axis=0, keepdims=True)
    rb = rows // 3

    @pl.loop(0, 3)
    def _(r):
        rw = pl.ds(pl.multiple_of(r * rb, rb), rb)
        gn1_ref[rw, :] = mm(gq[rw, :], w_scr[:, : 3 * n_i * he], NT).astype(BF)

    for kind in range(4):
        pltpu.make_async_copy(gbuf.at[kind], gbuf.at[kind], gsem.at[kind]).wait()


def att_backward(hidden, ga, gb, gain, go, n1, qkv, mix, valid_t, n_j, parts, arrays):
    rows, width = hidden.shape
    n_i, he = 4, 2 * HEAD
    wq = width // n_j
    return pl.pallas_call(
        functools.partial(att_bwd_kernel, parts, n_i),
        in_specs=[VMEM_SPEC] * 9 + [ANY_SPEC] * len(arrays),
        out_specs=[VMEM_SPEC] * 2 + [ANY_SPEC] + [VMEM_SPEC] * 2,
        out_shape=[
            jax.ShapeDtypeStruct((rows, width), F32),
            jax.ShapeDtypeStruct((rows, width), BF),
            jax.ShapeDtypeStruct((n_j, n_i, 4, wq, he), BF),
            jax.ShapeDtypeStruct((1, 3 * n_i * he), F32),
            jax.ShapeDtypeStruct((8, width), F32),
        ],
        scratch_shapes=[
            pltpu.VMEM((rows, width), BF),
            pltpu.VMEM((n_i, rows, he), BF),
            pltpu.VMEM((rows, 3 * n_i * he), BF),
            pltpu.VMEM((width, 4 * n_i * he), BF),
            pltpu.VMEM((4, width, n_i * he), BF),
            pltpu.SemaphoreType.DMA,
            pltpu.SemaphoreType.DMA((4,)),
        ],
        compiler_params=pltpu.CompilerParams(vmem_limit_bytes=56 * MIB),
        cost_estimate=pl.CostEstimate(flops=20_000_000_000, bytes_accessed=40_000_000, transcendentals=2_500_000),
        name="att_backward",
    )(hidden, ga, gb, gain, go, n1, qkv, mix, valid_t, *arrays)


def swap(x, axis, bits):
    n = lax.axis_size(axis)
    return lax.ppermute(x, axis, [(i, i ^ bits) for i in range(n)])


def gather_q(own):
    n_q = lax.axis_size("dp") // 2
    if n_q != 4:
        blocks = own[None]
        bit = 1
        while bit < n_q:
            blocks = jnp.concatenate([blocks, swap(blocks, "dp", 2 * bit)])
            bit *= 2
        return [(0, 0)], [blocks]
    half = own.shape[0] // 2
    one = swap(own, "dp", 2)
    two = swap(own, "dp", 4)
    three_a = swap(one[:half], "dp", 4)
    three_b = swap(two[half:], "dp", 2)
    places = [(0, 0), (1, 0), (2, 0), (3, 0), (3, half)]
    return places, [v[None] for v in (own, one, two, three_a, three_b)]


def add(*parts):
    total = parts[0].astype(F32)
    for part in parts[1:]:
        total = total + part.astype(F32)
    return total.astype(parts[0].dtype)


def scatter_q(parts):
    n_q = lax.axis_size("dp") // 2
    if n_q != 4:
        bit = n_q // 2
        while bit >= 1:
            parts = add(parts[:bit], swap(parts[bit:], "dp", 2 * bit))
            bit //= 2
        return parts[0]
    half = parts.shape[1] // 2
    into_one = swap(parts[3, :half], "dp", 4)
    into_two = swap(parts[3, half:], "dp", 2)
    one = jnp.concatenate([add(parts[1, :half], into_one), parts[1, half:]])
    two = jnp.concatenate([parts[2, :half], add(parts[2, half:], into_two)])
    return add(parts[0], swap(one, "dp", 2), swap(two, "dp", 4))


def gather_z(own):
    two = swap(own, "mp", 2)
    one = swap(own, "mp", 1)
    three = swap(two, "mp", 1)
    return jnp.stack([own, one, two, three])


def scatter_z(parts):
    into_two = swap(parts[3], "mp", 1)
    return add(parts[0], swap(parts[1], "mp", 1), swap(add(parts[2], into_two), "mp", 2))


def ordered_pair(own, other, core, axis=0):
    return jnp.stack(
        [jnp.where(core == 0, own, other), jnp.where(core == 0, other, own)], axis
    )


def image_routes(n_dp, n_mp, odd):
    pairs = []
    for plane in range(n_dp // 2):
        for core in range(2):
            for z in range(n_mp):
                shift = 2 * core + odd
                worker = (plane * 2 + core) * n_mp + z
                holder = (plane * 2 + (z >> 1)) * n_mp + (z ^ shift)
                pairs.append((holder, worker))
    return pairs


def to_images(x, z):
    n_dp, n_mp = lax.axis_size("dp"), lax.axis_size("mp")
    slots, images, width = x.shape
    groups = jnp.transpose(x, (1, 0, 2)).reshape(2, images // 2, slots, width)
    got = []
    for odd in (0, 1):
        send = lax.dynamic_index_in_dim(groups, (z ^ odd) & 1, 0, False)
        got.append(lax.ppermute(send, ("dp", "mp"), image_routes(n_dp, n_mp, odd)))
    return jnp.stack(got, 1)


def from_images(y, z):
    n_dp, n_mp = lax.axis_size("dp"), lax.axis_size("mp")
    back = []
    for odd in (0, 1):
        routes = [(b, a) for a, b in image_routes(n_dp, n_mp, odd)]
        back.append(lax.ppermute(y[:, odd], ("dp", "mp"), routes))
    flip = (z & 1) == 1
    groups = jnp.concatenate([jnp.where(flip, back[1], back[0]), jnp.where(flip, back[0], back[1])])
    return jnp.transpose(groups, (1, 0, 2))


def local(
    tokens,
    counts,
    norm_gains,
    norm_shifts,
    qkv_weight,
    qkv_bias,
    proj_weight,
    out_biases,
    up_weight,
    up_bias,
    down_weight,
    cotangent,
):
    slots, images, width = tokens.shape
    n_dp, n_mp = lax.axis_size("dp"), lax.axis_size("mp")
    n_q = n_dp // 2
    wq = width // n_q
    dp, z = lax.axis_index("dp"), lax.axis_index("mp")
    q, core = dp >> 1, dp & 1
    own_images = images // 2
    all_slots = slots * n_mp
    rows = own_images * all_slots

    def rel(v):
        blocks = [lax.dynamic_slice_in_dim(v, (q ^ j) * wq, wq, v.ndim - 1) for j in range(n_q)]
        return jnp.concatenate(blocks, -1)

    def half_of(v, which, axis):
        size = v.shape[axis] // 2
        return lax.dynamic_slice_in_dim(v, which * size, size, axis)

    att = jnp.concatenate([qkv_weight, jnp.transpose(proj_weight)[None]])
    ffn_w = jnp.stack([up_weight, jnp.transpose(down_weight)])

    def paired(v):
        got = swap(half_of(v, 1 - core, 2), "dp", 1)
        both = ordered_pair(half_of(v, core, 2), got, core, 1)
        return both.reshape(v.shape[0], wq, -1)

    att_own, ffn_own = paired(att), paired(ffn_w)
    he, fh = att_own.shape[-1], ffn_own.shape[-1]
    bias_own = jnp.concatenate(
        [half_of(qkv_bias, core, 1), half_of(up_bias, core, 0).reshape(-1, he)]
    )
    bias_all = gather_z(bias_own)
    att_places, att_parts = gather_q(gather_z(att_own))

    def whole_rows(v):
        got = to_images(rel(v), z)
        return ordered_pair(got, swap(got, "dp", 1), core, 1).reshape(rows, width)

    other_counts = swap(counts, "dp", 1)
    counts_here = jnp.where((z >> 1) == core, counts, other_counts)
    counts_here = lax.dynamic_slice_in_dim(counts_here, (z & 1) * own_images, own_images, 0)
    slot_ids = jnp.arange(slots, dtype=jnp.int32)
    slot_of = (z ^ jnp.arange(n_mp, dtype=jnp.int32))[:, None] * slots + slot_ids
    valid = (slot_of.reshape(1, -1) < BUF + counts_here[:, None]).astype(F32)
    keep_mine = ((z * slots + slot_ids)[:, None] < BUF + counts[None, :])[:, :, None]

    x = whole_rows(tokens)
    gains, shifts, out_b = rel(norm_gains), rel(norm_shifts), rel(out_biases)
    n_i = n_mp
    bias_rows = jnp.concatenate(
        [bias_all[:, 0].reshape(1, -1), jnp.zeros((1, n_i * he), F32), bias_all[:, 1].reshape(1, -1)], 1
    )
    n1, qkv, mix, part = att_forward(
        x.reshape(own_images, all_slots, width),
        gains[0:1],
        shifts[0:1],
        bias_rows,
        valid[:, None],
        att_places,
        att_parts,
    )

    ffn_z = gather_z(ffn_own)
    ffn_places, ffn_parts = [], []
    for i0 in (0, 2):
        places, arrays = gather_q(ffn_z[i0 : i0 + 2])
        ffn_places += [(j, i + i0) for j, i in places]
        ffn_parts += arrays
    go = whole_rows(jnp.where(keep_mine, cotangent, jnp.zeros_like(cotangent)))
    hidden, branch, gn2, ffn_g, upg = ffn(
        x,
        part,
        swap(part, "dp", 1),
        out_b[0:1],
        gains[1:2],
        shifts[1:2],
        go,
        bias_all[:, 2:].reshape(n_i, fh),
        n_q,
        ffn_places,
        ffn_parts,
    )
    gn2_other = swap(gn2, "dp", 1)
    gh, gn1, att_g, bias_sum, sums = att_backward(
        hidden,
        gn2,
        gn2_other,
        gains[1:2],
        go,
        n1,
        qkv,
        mix,
        valid[:, :, None],
        n_q,
        att_places,
        att_parts,
    )
    ffn_grad = scatter_z(
        jnp.concatenate([scatter_q(ffn_g[:, :2]), scatter_q(ffn_g[:, 2:])])
    )

    row_half = lambda v, which: half_of(v.reshape(own_images, n_mp, slots, width), which, 1)
    theirs = swap(row_half(branch, 1 - core), "dp", 1).astype(F32)
    out_half = row_half(hidden, core) + row_half(branch, core).astype(F32) + theirs + out_b[1]
    block_out = from_images(rel(out_half.astype(BF)), z)
    block_out = jnp.where(keep_mine, block_out, jnp.zeros_like(block_out))

    att_grad = scatter_z(scatter_q(att_g))
    gn1 = row_half(gn1, core).astype(F32) + swap(row_half(gn1, 1 - core), "dp", 1).astype(F32)
    hat1, inv1 = normalise(row_half(x, core).astype(F32))
    input_half = row_half(gh, core) + norm_back(hat1, inv1, gains[0], gn1)
    gain_one, shift_one = jnp.sum(gn1 * hat1, (0, 1, 2)), jnp.sum(gn1, (0, 1, 2))
    input_grad = from_images(rel(input_half.astype(BF)), z)

    def own_shard(grad):
        kinds, _, last = grad.shape
        pair = grad.reshape(kinds, 2, wq // 2, last)
        keep = lax.dynamic_index_in_dim(pair, core, 1, False)
        got = swap(lax.dynamic_index_in_dim(pair, 1 - core, 1, False), "dp", 1)
        return ordered_pair(keep, got, core, 2).reshape(kinds, wq // 2, 2 * last).astype(F32)

    att_shard, ffn_shard = own_shard(att_grad), own_shard(ffn_grad)
    qkv_owned, proj_owned = att_shard[:3], jnp.transpose(att_shard[3])
    up_owned, down_owned = ffn_shard[0], jnp.transpose(ffn_shard[1])

    wide_up = jnp.zeros((n_mp, 2, fh), F32)
    wide_bias = jnp.zeros((2, n_mp, 2, he), F32)
    biases = bias_sum.reshape(3, n_i, he)[0::2]
    for i in range(n_i):
        wide_up = lax.dynamic_update_slice(wide_up, upg[i][None, None], (z ^ i, core, 0))
        wide_bias = lax.dynamic_update_slice(wide_bias, biases[:, i][:, None, None], (0, z ^ i, core, 0))
    small = rel(
        jnp.concatenate(
            [gain_one[None], sums[0:1] * 0.5, shift_one[None], sums[1:2] * 0.5, sums[2:4] * 0.5]
        )
    )
    small, wide_bias, wide_up = lax.psum((small, wide_bias, wide_up), ("dp", "mp"))
    bias_grad = lax.dynamic_index_in_dim(wide_bias, z, 1, False).reshape(2, -1)
    upbias_grad = lax.dynamic_index_in_dim(wide_up, z, 0, False).reshape(-1)
    return (
        block_out,
        input_grad,
        small[0:2],
        small[2:4],
        qkv_owned,
        bias_grad,
        proj_owned,
        small[4:6],
        up_owned,
        upbias_grad,
        down_owned,
    )


def solution(mesh):
    split = P("mp", "dp", None)
    return jax.shard_map(
        local,
        mesh=mesh,
        in_specs=(
            split,
            P("dp"),
            P(),
            P(),
            P(None, "dp", "mp"),
            P(None, "mp"),
            P("mp", "dp"),
            P(),
            P("dp", "mp"),
            P("mp"),
            P("mp", "dp"),
            split,
        ),
        out_specs=(
            split,
            split,
            P(),
            P(),
            P(None, "dp", "mp"),
            P(None, "mp"),
            P("mp", "dp"),
            P(),
            P("dp", "mp"),
            P("mp"),
            P("mp", "dp"),
        ),
        check_vma=False,
    )
```

```python
import functools

import jax
import jax.numpy as jnp
from jax import lax
from jax.experimental import pallas as pl
from jax.experimental.pallas import tpu as pltpu
from jax.sharding import PartitionSpec as P

HEAD = 64
BUF = 64
BF = jnp.bfloat16
F32 = jnp.float32
epsilon = 1e-06
masked_score = -1e30
MIB = 1 << 20
NT = (((1,), (1,)), ((), ()))
NN = (((1,), (0,)), ((), ()))
TN = (((0,), (0,)), ((), ()))
factor = HEAD ** (-0.5)
VMEM_SPEC = pl.BlockSpec(memory_space=pltpu.VMEM)
ANY_SPEC = pl.BlockSpec(memory_space=pl.ANY)


def mm(a, b, dims=NN):
    return lax.dot_general(a, b, dims, preferred_element_type=F32)


def normalise(values):
    average = jnp.mean(values, axis=-1, keepdims=True)
    centred = values - average
    spread = jnp.mean(centred * centred, axis=-1, keepdims=True)
    inv = lax.rsqrt(spread + epsilon)
    return centred * inv, inv


def norm_back(n, inv, scales, grad):
    e = grad * scales
    mean_e = jnp.mean(e, axis=-1, keepdims=True)
    mean_en = jnp.mean(e * n, axis=-1, keepdims=True)
    return (e - mean_e - n * mean_en) * inv


def gelu_parts(inputs):
    normal_cdf = 0.5 + 0.5 * lax.erf(inputs * 0.7071067811865476)
    density = jnp.exp(-0.5 * inputs * inputs) * 0.3989422804014327
    return inputs * normal_cdf, normal_cdf + inputs * density


def for_each(count, step):
    if count <= 4:
        for index in range(count):
            step(index)
    else:
        pl.loop(0, count)(step)


def valid_slots(meta_ref, image, slots, axis):
    shape = (slots, 1) if axis == 0 else (1, slots)
    row = lax.broadcasted_iota(jnp.int32, shape, axis)
    n = slots // 4
    k = (row >= n).astype(jnp.int32) + (row >= 2 * n) + (row >= 3 * n)
    slot = (k ^ meta_ref[3]) * n + (row - k * n)
    return slot < BUF + meta_ref[image]


def copy_att(parts, refs, w_scr, sem, kinds, n_i):
    n_j = parts[-1][0] + refs[-1].shape[0]
    wq = w_scr.shape[0] // n_j
    for (j0, i0), ref in zip(parts, refs):
        nj, ni, _, he = ref.shape

        def one(jj, ref=ref, j0=j0, i0=i0, ni=ni, wq=wq, he=he):
            rows = pl.ds(pl.multiple_of((j0 + jj) * wq, wq), wq) if not isinstance(jj, int) else pl.ds((j0 + jj) * wq, wq)
            for ii in range(ni):
                for t in range(kinds):
                    pltpu.make_async_copy(
                        ref.at[jj, ii, pl.ds(t * wq, wq)], w_scr.at[rows, pl.ds((t * n_i + i0 + ii) * he, he)], sem
                    ).start()

        for_each(nj, one)
    pltpu.make_async_copy(w_scr, w_scr, sem).wait()


def att_fwd_kernel(parts, n_i, x_ref, g_ref, c_ref, bias_ref, meta_ref, *rest):
    w_refs = rest[: len(parts)]
    n1_ref, qkv_ref, mix_ref, part_ref, w_scr, m_scr, sem = rest[len(parts) :]
    he = 2 * HEAD

    @pl.when(pl.program_id(0) == 0)
    def _():
        copy_att(parts, w_refs, w_scr, sem, 4, n_i)

    hat, _ = normalise(x_ref[0].astype(F32))
    n1 = (hat * g_ref[...] + c_ref[...]).astype(BF)
    n1_ref[...] = n1
    for t in range(3):
        cols = pl.ds(t * n_i * he, n_i * he)
        res = (mm(n1, w_scr[:, cols]) + bias_ref[:, cols]).astype(BF)
        for i in range(n_i):
            qkv_ref[t * n_i + i] = res[:, i * he : (i + 1) * he]
    image = pl.program_id(0)
    bias = jnp.where(valid_slots(meta_ref, image, x_ref.shape[1], 1), 0.0, masked_score)
    lane = lax.broadcasted_iota(jnp.int32, (1, he), 1)
    low_half = lane < HEAD
    for i in range(n_i):
        q2, k2, v2 = qkv_ref[i], qkv_ref[n_i + i], qkv_ref[2 * n_i + i]
        outs = []
        for h in range(2):
            qm = jnp.where(low_half if h == 0 else ~low_half, q2, jnp.zeros_like(q2))
            s = mm(qm, k2, NT) * factor + bias
            top = jnp.max(s, axis=-1, keepdims=True)
            p = jnp.exp(s - top)
            w = (p / jnp.sum(p, axis=-1, keepdims=True)).astype(BF)
            outs.append(mm(w, v2))
        mixed = jnp.where(low_half, outs[0], outs[1]).astype(BF)
        m_scr[:, i * he : (i + 1) * he] = mixed
    mix_ref[...] = m_scr[...]
    part_ref[...] = mm(m_scr[...], w_scr[:, 3 * n_i * he :], NT).astype(BF)


def att_forward(x, gain, shift, bias, meta, parts, arrays):
    images, slots, width = x.shape
    n_i = 4
    he = 2 * HEAD
    rows = images * slots
    row_block = lambda last: pl.BlockSpec((slots, last), lambda a: (a, 0))
    whole = lambda *shape: pl.BlockSpec(shape, lambda a: (0,) * len(shape))
    return pl.pallas_call(
        functools.partial(att_fwd_kernel, parts, n_i),
        grid=(images,),
        in_specs=[
            pl.BlockSpec((1, slots, width), lambda a: (a, 0, 0)),
            whole(1, width),
            whole(1, width),
            whole(1, 3 * n_i * he),
            pl.BlockSpec(memory_space=pltpu.SMEM),
        ]
        + [ANY_SPEC] * len(arrays),
        out_specs=[
            row_block(width),
            pl.BlockSpec((3 * n_i, slots, he), lambda a: (0, a, 0)),
            row_block(n_i * he),
            row_block(width),
        ],
        out_shape=[
            jax.ShapeDtypeStruct((rows, width), BF),
            jax.ShapeDtypeStruct((3 * n_i, rows, he), BF),
            jax.ShapeDtypeStruct((rows, n_i * he), BF),
            jax.ShapeDtypeStruct((rows, width), BF),
        ],
        scratch_shapes=[
            pltpu.VMEM((width, 4 * n_i * he), BF),
            pltpu.VMEM((slots, n_i * he), BF),
            pltpu.SemaphoreType.DMA,
        ],
        compiler_params=pltpu.CompilerParams(vmem_limit_bytes=32 * MIB),
        cost_estimate=pl.CostEstimate(flops=8_000_000_000, bytes_accessed=20_000_000, transcendentals=2_500_000),
        name="att_forward",
    )(x, gain, shift, bias, meta, *arrays)


def ffn_kernel(parts, n_i, first, last, *refs):
    if first:
        x_ref, pa_ref, pb_ref, b_ref, g_ref, c_ref = refs[:6]
        refs = refs[6:]
    else:
        n2, n2t, got, acc_b, acc_g = refs[:5]
        refs = refs[5:]
    go_ref, upb_ref = refs[:2]
    w_refs, refs = refs[2 : 2 + len(parts)], refs[2 + len(parts) :]
    if first:
        hidden_ref, n2, n2t, got = refs[:4]
        refs = refs[4:]
    sum_b, sum_g, grads_ref, upg_ref, wbuf, gbuf, act_s, pre_s, wsem, gsem = refs[:10]
    run_b, run_g = refs[10:] if last else (sum_b, sum_g)
    rows, width = go_ref.shape
    n_j, _, _, wq, _ = grads_ref.shape

    def fetch(i, slot):
        for (j0, i0), ref in zip(parts, w_refs):
            nj, ni = ref.shape[:2]
            if not i0 <= i < i0 + ni:
                continue

            def one(jj, ref=ref, j0=j0, i0=i0):
                start = (j0 + jj) * wq
                rws = pl.ds(start if isinstance(jj, int) else pl.multiple_of(start, wq), wq)
                for kind in range(2):
                    pltpu.make_async_copy(
                        ref.at[jj, i - i0, kind], wbuf.at[slot, kind, rws], wsem.at[slot]
                    ).start()

            for_each(nj, one)

    def fetched(slot):
        pltpu.make_async_copy(wbuf.at[slot], wbuf.at[slot], wsem.at[slot]).wait()

    def put(i, slot):
        def one(jj):
            start = jj * wq
            rws = pl.ds(start if isinstance(jj, int) else pl.multiple_of(start, wq), wq)
            for kind in range(2):
                pltpu.make_async_copy(
                    gbuf.at[slot, kind, rws], grads_ref.at[jj, i, kind], gsem.at[slot]
                ).start()

        for_each(n_j, one)

    def stored(slot):
        pltpu.make_async_copy(gbuf.at[slot], gbuf.at[slot], gsem.at[slot]).wait()

    fetch(0, 0)
    if first:
        block = 192

        @pl.loop(0, rows // block)
        def _(r):
            rw = pl.ds(pl.multiple_of(r * block, block), block)
            h = (
                x_ref[rw, :].astype(F32)
                + (pa_ref[rw, :].astype(F32) + pb_ref[rw, :].astype(F32))
                + b_ref[...]
            )
            hidden_ref[rw, :] = h
            hat, _ = normalise(h)
            n2[rw, :] = (hat * g_ref[...] + c_ref[...]).astype(BF)

        n2t[...] = n2[...].T
        got[...] = go_ref[...].T
    rb = rows // 3
    for i in range(n_i):
        slot = i % 2
        if i + 1 < n_i:
            fetch(i + 1, 1 - slot)
        fetched(slot)

        @pl.loop(0, 3)
        def _(r, i=i, slot=slot):
            rw = pl.ds(pl.multiple_of(r * rb, rb), rb)
            u, w = wbuf[slot, 0], wbuf[slot, 1]
            up = mm(n2[rw, :], u) + upb_ref[i : i + 1, :]
            act, slope = gelu_parts(up)
            act = act.astype(BF)
            act_s[rw, :] = act
            pre = (mm(go_ref[rw, :], w) * slope).astype(BF)
            pre_s[rw, :] = pre
            down = mm(act, w, NT)
            back = mm(pre, u, NT)
            if i > 0:
                down += run_b[rw, :]
                back += run_g[rw, :]
            elif not first:
                down += acc_b[rw, :]
                back += acc_g[rw, :]
            if i < n_i - 1:
                run_b[rw, :] = down
                run_g[rw, :] = back
            else:
                sum_b[rw, :] = down.astype(sum_b.dtype)
                sum_g[rw, :] = back.astype(sum_g.dtype)

        upg_ref[i : i + 1, :] = jnp.sum(pre_s[...].astype(F32), axis=0, keepdims=True)
        if i >= 2:
            stored(slot)
        gbuf[slot, 0] = mm(n2t[...], pre_s[...]).astype(BF)
        gbuf[slot, 1] = mm(got[...], act_s[...]).astype(BF)
        put(i, slot)
    for i in range(max(n_i - 2, 0), n_i):
        stored(i % 2)


def ffn_call(ins, n_j, n_i, fh, parts, arrays, first, last):
    go = ins[-2]
    rows, width = go.shape
    wq = width // n_j
    made = (
        [
            jax.ShapeDtypeStruct((rows, width), F32),
            jax.ShapeDtypeStruct((rows, width), BF),
            jax.ShapeDtypeStruct((width, rows), BF),
            jax.ShapeDtypeStruct((width, rows), BF),
        ]
        if first
        else []
    )
    sums = BF if last else F32
    return pl.pallas_call(
        functools.partial(ffn_kernel, parts, n_i, first, last),
        in_specs=[VMEM_SPEC] * len(ins) + [ANY_SPEC] * len(arrays),
        out_specs=[VMEM_SPEC] * (len(made) + 2) + [ANY_SPEC, VMEM_SPEC],
        out_shape=made
        + [
            jax.ShapeDtypeStruct((rows, width), sums),
            jax.ShapeDtypeStruct((rows, width), sums),
            jax.ShapeDtypeStruct((n_j, n_i, 2, wq, fh), BF),
            jax.ShapeDtypeStruct((n_i, fh), F32),
        ],
        scratch_shapes=[
            pltpu.VMEM((2, 2, width, fh), BF),
            pltpu.VMEM((2, 2, width, fh), BF),
            pltpu.VMEM((rows, fh), BF),
            pltpu.VMEM((rows, fh), BF),
            pltpu.SemaphoreType.DMA((2,)),
            pltpu.SemaphoreType.DMA((2,)),
        ]
        + [pltpu.VMEM((rows, width), F32)] * (2 if last else 0),
        compiler_params=pltpu.CompilerParams(vmem_limit_bytes=58 * MIB),
        cost_estimate=pl.CostEstimate(
            flops=9_000_000_000 * n_i, bytes_accessed=30_000_000, transcendentals=1_000_000 * n_i
        ),
        name="ffn_first" if first else "ffn_last",
    )(*ins, *arrays)


def att_bwd_kernel(
    parts, n_i, meta_ref, x_ref, hid_ref, ga_ref, gb_ref, g_ref, go_ref, n1_ref, qkv_ref, mix_ref, *rest
):
    w_refs = rest[: len(parts)]
    gh_ref, gn1_ref, grads_ref, bias_ref, sums_ref = rest[len(parts) : len(parts) + 5]
    ghb, gmix, gq, w_scr, gbuf, sem, gsem = rest[len(parts) + 5 :]
    rows, width = hid_ref.shape
    he = 2 * HEAD
    images = 3
    slots = rows // images
    n_j, _, _, wq, _ = grads_ref.shape
    copy_att(parts, w_refs, w_scr, sem, 4, n_i)
    block = 192
    proj_cols = pl.ds(3 * n_i * he, n_i * he)
    sums_ref[...] = jnp.zeros_like(sums_ref)

    @pl.loop(0, rows // block)
    def _(r):
        rw = pl.ds(pl.multiple_of(r * block, block), block)
        hat, inv = normalise(hid_ref[rw, :])
        grad = ga_ref[rw, :].astype(F32) + gb_ref[rw, :].astype(F32)
        gout = go_ref[rw, :].astype(F32)
        gh = gout + norm_back(hat, inv, g_ref[...], grad)
        gh_ref[rw, :] = gh
        low = gh.astype(BF)
        ghb[rw, :] = low
        sums_ref[0:1, :] += jnp.sum(grad * hat, axis=0, keepdims=True)
        sums_ref[1:2, :] += jnp.sum(grad, axis=0, keepdims=True)
        sums_ref[2:3, :] += jnp.sum(gh, axis=0, keepdims=True)
        sums_ref[3:4, :] += jnp.sum(gout, axis=0, keepdims=True)
        res = mm(low, w_scr[:, proj_cols]).astype(BF)
        for i in range(n_i):
            gmix[i, rw, :] = res[:, i * he : (i + 1) * he]

    def put(kind):
        def one(jj):
            start = jj * wq
            rws = pl.ds(start if isinstance(jj, int) else pl.multiple_of(start, wq), wq)
            for i in range(n_i):
                pltpu.make_async_copy(
                    gbuf.at[kind, rws, pl.ds(i * he, he)], grads_ref.at[jj, i, kind], gsem.at[kind]
                ).start()

        for_each(n_j, one)

    gbuf[3] = mm(ghb[...].T, mix_ref[...]).astype(BF)
    put(3)
    lane = lax.broadcasted_iota(jnp.int32, (1, he), 1)
    low_half = lane < HEAD

    @pl.loop(0, images)
    def _(a):
        rw = pl.ds(pl.multiple_of(a * slots, slots), slots)
        bias = jnp.where(valid_slots(meta_ref, a, slots, 0), 0.0, masked_score)
        for i in range(n_i):
            q2, k2, v2 = qkv_ref[i, rw, :], qkv_ref[n_i + i, rw, :], qkv_ref[2 * n_i + i, rw, :]
            g2 = gmix[i, rw, :]
            dq, dk, dv = [], [], []
            for h in range(2):
                here = low_half if h == 0 else ~low_half
                qm = jnp.where(here, q2, jnp.zeros_like(q2))
                gm = jnp.where(here, g2, jnp.zeros_like(g2))
                st = mm(k2, qm, NT) * factor + bias
                top = jnp.max(st, axis=0, keepdims=True)
                p = jnp.exp(st - top)
                p = p / jnp.sum(p, axis=0, keepdims=True)
                dpt = mm(v2, gm, NT)
                dot = jnp.sum(p * dpt, axis=0, keepdims=True)
                ds = (p * (dpt - dot)).astype(BF)
                dk.append(mm(ds, q2))
                dv.append(mm(p.astype(BF), g2))
                dq.append(mm(ds, k2, TN))
            gq[rw, i * he : (i + 1) * he] = (jnp.where(low_half, dq[0], dq[1]) * factor).astype(BF)
            gq[rw, (n_i + i) * he : (n_i + i + 1) * he] = (
                jnp.where(low_half, dk[0], dk[1]) * factor
            ).astype(BF)
            gq[rw, (2 * n_i + i) * he : (2 * n_i + i + 1) * he] = jnp.where(
                low_half, dv[0], dv[1]
            ).astype(BF)

    n1t = n1_ref[...].T
    for t in range(3):
        cols = pl.ds(t * n_i * he, n_i * he)
        gbuf[t] = mm(n1t, gq[:, cols]).astype(BF)
        put(t)
    bias_ref[...] = jnp.sum(gq[...].astype(F32), axis=0, keepdims=True)
    rb = rows // 3

    @pl.loop(0, 3)
    def _(r):
        rw = pl.ds(pl.multiple_of(r * rb, rb), rb)
        grad = mm(gq[rw, :], w_scr[:, : 3 * n_i * he], NT)
        gn1_ref[rw, :] = grad.astype(BF)
        hat, _ = normalise(x_ref[rw, :].astype(F32))
        sums_ref[4:5, :] += jnp.sum(grad * hat, axis=0, keepdims=True)
        sums_ref[5:6, :] += jnp.sum(grad, axis=0, keepdims=True)

    for kind in range(4):
        pltpu.make_async_copy(gbuf.at[kind], gbuf.at[kind], gsem.at[kind]).wait()


def att_backward(meta, x, hidden, ga, gb, gain, go, n1, qkv, mix, n_j, parts, arrays):
    rows, width = hidden.shape
    n_i, he = 4, 2 * HEAD
    wq = width // n_j
    return pl.pallas_call(
        functools.partial(att_bwd_kernel, parts, n_i),
        in_specs=[pl.BlockSpec(memory_space=pltpu.SMEM)] + [VMEM_SPEC] * 9 + [ANY_SPEC] * len(arrays),
        out_specs=[VMEM_SPEC] * 2 + [ANY_SPEC] + [VMEM_SPEC] * 2,
        out_shape=[
            jax.ShapeDtypeStruct((rows, width), F32),
            jax.ShapeDtypeStruct((rows, width), BF),
            jax.ShapeDtypeStruct((n_j, n_i, 4, wq, he), BF),
            jax.ShapeDtypeStruct((1, 3 * n_i * he), F32),
            jax.ShapeDtypeStruct((8, width), F32),
        ],
        scratch_shapes=[
            pltpu.VMEM((rows, width), BF),
            pltpu.VMEM((n_i, rows, he), BF),
            pltpu.VMEM((rows, 3 * n_i * he), BF),
            pltpu.VMEM((width, 4 * n_i * he), BF),
            pltpu.VMEM((4, width, n_i * he), BF),
            pltpu.SemaphoreType.DMA,
            pltpu.SemaphoreType.DMA((4,)),
        ],
        compiler_params=pltpu.CompilerParams(vmem_limit_bytes=56 * MIB),
        cost_estimate=pl.CostEstimate(flops=20_000_000_000, bytes_accessed=40_000_000, transcendentals=2_500_000),
        name="att_backward",
    )(meta, x, hidden, ga, gb, gain, go, n1, qkv, mix, *arrays)


def swap(x, axis, bits, what):
    n = lax.axis_size(axis)
    with jax.named_scope(what):
        return lax.ppermute(x, axis, [(i, i ^ bits) for i in range(n)])


def gather_q(own, what):
    n_q = lax.axis_size("dp") // 2
    if n_q != 4:
        blocks = own[None]
        bit = 1
        while bit < n_q:
            blocks = jnp.concatenate([blocks, swap(blocks, "dp", 2 * bit, what)])
            bit *= 2
        return [(0, 0)], [blocks]
    half = own.shape[0] // 2
    one = swap(own, "dp", 2, what + "_x1")
    two = swap(own, "dp", 4, what + "_y1")
    three_a = swap(one[:half], "dp", 4, what + "_y2")
    three_b = swap(two[half:], "dp", 2, what + "_x2")
    places = [(0, 0), (1, 0), (2, 0), (3, 0), (3, half)]
    return places, [v[None] for v in (own, one, two, three_a, three_b)]


def add(*parts):
    total = parts[0].astype(F32)
    for part in parts[1:]:
        total = total + part.astype(F32)
    return total.astype(parts[0].dtype)


def scatter_q(parts, what):
    n_q = lax.axis_size("dp") // 2
    if n_q != 4:
        bit = n_q // 2
        while bit >= 1:
            parts = add(parts[:bit], swap(parts[bit:], "dp", 2 * bit, what))
            bit //= 2
        return parts[0]
    half = parts.shape[1] // 2
    into_one = swap(parts[3, :half], "dp", 4, what + "_y1")
    into_two = swap(parts[3, half:], "dp", 2, what + "_x1")
    one = jnp.concatenate([add(parts[1, :half], into_one), parts[1, half:]])
    two = jnp.concatenate([parts[2, :half], add(parts[2, half:], into_two)])
    return add(parts[0], swap(one, "dp", 2, what + "_x2"), swap(two, "dp", 4, what + "_y2"))


def gather_z(own, what):
    two = swap(own, "mp", 2, what + "_z2")
    one = swap(own, "mp", 1, what + "_z1")
    three = swap(two, "mp", 1, what + "_z3")
    return jnp.stack([own, one, two, three])


def scatter_z(parts, what):
    into_two = swap(parts[3], "mp", 1, what + "_z3")
    return add(parts[0], swap(parts[1], "mp", 1, what + "_z1"), swap(add(parts[2], into_two), "mp", 2, what + "_z2"))


def ordered_pair(own, other, core, axis=0):
    return jnp.stack(
        [jnp.where(core == 0, own, other), jnp.where(core == 0, other, own)], axis
    )


def image_routes(n_dp, n_mp, odd):
    pairs = []
    for plane in range(n_dp // 2):
        for core in range(2):
            for z in range(n_mp):
                shift = 2 * core + odd
                worker = (plane * 2 + core) * n_mp + z
                holder = (plane * 2 + (z >> 1)) * n_mp + (z ^ shift)
                pairs.append((holder, worker))
    return pairs


def to_images(x, z, what):
    n_dp, n_mp = lax.axis_size("dp"), lax.axis_size("mp")
    slots, images, width = x.shape
    groups = jnp.transpose(x, (1, 0, 2)).reshape(2, images // 2, slots, width)
    got = []
    for odd in (0, 1):
        send = lax.dynamic_index_in_dim(groups, (z ^ odd) & 1, 0, False)
        with jax.named_scope(what + "_route" + str(odd)):
            got.append(lax.ppermute(send, ("dp", "mp"), image_routes(n_dp, n_mp, odd)))
    return jnp.stack(got, 1)


def from_images(y, z, what):
    n_dp, n_mp = lax.axis_size("dp"), lax.axis_size("mp")
    back = []
    for odd in (0, 1):
        routes = [(b, a) for a, b in image_routes(n_dp, n_mp, odd)]
        with jax.named_scope(what + "_route" + str(odd)):
            back.append(lax.ppermute(y[:, odd], ("dp", "mp"), routes))
    flip = (z & 1) == 1
    groups = jnp.concatenate([jnp.where(flip, back[1], back[0]), jnp.where(flip, back[0], back[1])])
    return jnp.transpose(groups, (1, 0, 2))


def local(
    tokens,
    counts,
    norm_gains,
    norm_shifts,
    qkv_weight,
    qkv_bias,
    proj_weight,
    out_biases,
    up_weight,
    up_bias,
    down_weight,
    cotangent,
):
    slots, images, width = tokens.shape
    n_dp, n_mp = lax.axis_size("dp"), lax.axis_size("mp")
    n_q = n_dp // 2
    wq = width // n_q
    dp, z = lax.axis_index("dp"), lax.axis_index("mp")
    q, core = dp >> 1, dp & 1
    own_images = images // 2
    all_slots = slots * n_mp
    rows = own_images * all_slots

    def rel(v):
        blocks = [lax.dynamic_slice_in_dim(v, (q ^ j) * wq, wq, v.ndim - 1) for j in range(n_q)]
        return jnp.concatenate(blocks, -1)

    def half_of(v, which, axis):
        size = v.shape[axis] // 2
        return lax.dynamic_slice_in_dim(v, which * size, size, axis)

    att = jnp.concatenate([qkv_weight, jnp.transpose(proj_weight)[None]])
    ffn_w = jnp.stack([up_weight, jnp.transpose(down_weight)])
    he, fh = att.shape[-1] // 2, ffn_w.shape[-1] // 2

    count_rows = jnp.pad(counts.astype(BF)[None], ((0, 15), (0, he - images)))
    sent = jnp.concatenate([half_of(att, 1 - core, 2).reshape(-1, he), count_rows])
    got = swap(sent, "dp", 1, "att_w_core")
    other_counts = got[-16, :images].astype(jnp.int32)
    got = got[:-16].reshape(4, wq // 2, he)
    att_own = ordered_pair(half_of(att, core, 2), got, core, 1).reshape(-1, he)
    got = swap(half_of(ffn_w, 1 - core, 2), "dp", 1, "ffn_w_core")
    ffn_own = ordered_pair(half_of(ffn_w, core, 2), got, core, 1).reshape(2, wq, fh)
    left = jnp.concatenate(
        [half_of(qkv_bias, core, 1), half_of(up_bias, core, 0).reshape(-1, he)]
    )
    n_bias = left.shape[0]
    terms = []
    for _ in range(3):
        term = lax.reduce_precision(left, 8, 7)
        terms.append(term.astype(BF))
        left = left - term
    bias_pad = -(-3 * n_bias // 16) * 16
    bias_terms = jnp.pad(jnp.concatenate(terms), ((0, bias_pad - 3 * n_bias), (0, 0)))

    counts_here = jnp.where((z >> 1) == core, counts, other_counts)
    counts_here = lax.dynamic_slice_in_dim(counts_here, (z & 1) * own_images, own_images, 0)
    meta = jnp.concatenate([counts_here, z[None]])
    slot_ids = jnp.arange(slots, dtype=jnp.int32)
    keep_mine = ((z * slots + slot_ids)[:, None] < BUF + counts[None, :])[:, :, None]

    def whole_rows(got, what):
        return ordered_pair(got, swap(got, "dp", 1, what), core, 1).reshape(rows, width)

    n_i = n_mp
    gains, shifts, out_b = rel(norm_gains), rel(norm_shifts), rel(out_biases)
    token_rows = to_images(rel(tokens), z, "tokens")
    att_z = gather_z(jnp.concatenate([att_own, bias_terms]), "att_w")
    bias_all = att_z[:, 4 * wq : 4 * wq + 3 * n_bias].astype(F32).reshape(n_i, 3, n_bias, he)
    bias_all = bias_all[:, 0] + (bias_all[:, 1] + bias_all[:, 2])
    bias_rows = jnp.concatenate(
        [bias_all[:, 0].reshape(1, -1), jnp.zeros((1, n_i * he), F32), bias_all[:, 1].reshape(1, -1)], 1
    )
    x = whole_rows(token_rows, "tokens_core")
    att_places, att_parts = gather_q(att_z, "att_w")
    n1, qkv, mix, part = att_forward(
        x.reshape(own_images, all_slots, width),
        gains[0:1],
        shifts[0:1],
        bias_rows,
        meta,
        att_places,
        att_parts,
    )

    ffn_z = gather_z(ffn_own, "ffn_w")
    cot_rows = to_images(
        rel(jnp.where(keep_mine, cotangent, jnp.zeros_like(cotangent))), z, "cotangent"
    )
    go = whole_rows(cot_rows, "cotangent_core")
    up_rows = bias_all[:, 2:].reshape(n_i, fh)
    places0, parts0 = gather_q(ffn_z[:2], "ffn_w0")
    hidden, n2, n2t, got, sum_b, sum_g, ffn_g0, upg0 = ffn_call(
        [x, part, swap(part, "dp", 1, "attended"), out_b[0:1], gains[1:2], shifts[1:2], go, up_rows[:2]],
        n_q, 2, fh, places0, parts0, True, False,
    )
    places1, parts1 = gather_q(ffn_z[2:], "ffn_w2")
    branch, gn2, ffn_g1, upg1 = ffn_call(
        [n2, n2t, got, sum_b, sum_g, go, up_rows[2:]], n_q, 2, fh, places1, parts1, False, True
    )
    upg = jnp.concatenate([upg0, upg1])
    gn2_other = swap(gn2, "dp", 1, "grad_norm_two")
    gh, gn1, att_g, bias_sum, sums = att_backward(
        meta,
        x,
        hidden,
        gn2,
        gn2_other,
        gains[1:2],
        go,
        n1,
        qkv,
        mix,
        n_q,
        att_places,
        att_parts,
    )
    ffn_grad = scatter_z(
        jnp.concatenate([scatter_q(ffn_g0, "ffn_g0"), scatter_q(ffn_g1, "ffn_g2")]), "ffn_g"
    )

    row_half = lambda v, which: half_of(v.reshape(own_images, n_mp, slots, width), which, 1)
    theirs = swap(row_half(branch, 1 - core), "dp", 1, "branch").astype(F32)
    out_half = row_half(hidden, core) + row_half(branch, core).astype(F32) + theirs + out_b[1]
    block_out = from_images(rel(out_half.astype(BF)), z, "block_out")
    block_out = jnp.where(keep_mine, block_out, jnp.zeros_like(block_out))

    att_grad = scatter_z(scatter_q(att_g, "att_g"), "att_g")
    gn1 = row_half(gn1, core).astype(F32) + swap(row_half(gn1, 1 - core), "dp", 1, "grad_norm_one").astype(F32)
    hat1, inv1 = normalise(row_half(x, core).astype(F32))
    input_half = row_half(gh, core) + norm_back(hat1, inv1, gains[0], gn1)
    input_grad = from_images(rel(input_half.astype(BF)), z, "input_grad")

    def own_shard(grad, what):
        kinds, _, last = grad.shape
        pair = grad.reshape(kinds, 2, wq // 2, last)
        keep = lax.dynamic_index_in_dim(pair, core, 1, False)
        got = swap(lax.dynamic_index_in_dim(pair, 1 - core, 1, False), "dp", 1, what)
        return ordered_pair(keep, got, core, 2).reshape(kinds, wq // 2, 2 * last).astype(F32)

    att_shard, ffn_shard = own_shard(att_grad, "att_g_core"), own_shard(ffn_grad, "ffn_g_core")
    qkv_owned, proj_owned = att_shard[:3], jnp.transpose(att_shard[3])
    up_owned, down_owned = ffn_shard[0], jnp.transpose(ffn_shard[1])

    wide_up = jnp.zeros((n_mp, 2, fh), F32)
    wide_bias = jnp.zeros((2, n_mp, 2, he), F32)
    biases = bias_sum.reshape(3, n_i, he)[0::2]
    for i in range(n_i):
        wide_up = lax.dynamic_update_slice(wide_up, upg[i][None, None], (z ^ i, core, 0))
        wide_bias = lax.dynamic_update_slice(wide_bias, biases[:, i][:, None, None], (0, z ^ i, core, 0))
    small = rel(sums)
    vector = jnp.concatenate([small.reshape(-1), wide_bias.reshape(-1), wide_up.reshape(-1)])
    vector = vector.reshape(-1, 128)
    for axis, size in (("mp", n_mp), ("dp", n_dp)):
        bit = size // 2
        while bit >= 1:
            vector = vector + swap(vector, axis, bit, "sums_" + axis + str(bit))
            bit //= 2
    vector = vector.reshape(-1)
    n_small, n_wide = small.size, wide_bias.size
    small = vector[:n_small].reshape(small.shape)
    wide_bias = vector[n_small : n_small + n_wide].reshape(wide_bias.shape)
    wide_up = vector[n_small + n_wide :].reshape(wide_up.shape)
    small = jnp.concatenate([small[:4] * 0.5, small[4:]])
    gains_grad = jnp.stack([small[4], small[0]])
    shifts_grad = jnp.stack([small[5], small[1]])
    bias_grad = lax.dynamic_index_in_dim(wide_bias, z, 1, False).reshape(2, -1)
    upbias_grad = lax.dynamic_index_in_dim(wide_up, z, 0, False).reshape(-1)
    return (
        block_out,
        input_grad,
        gains_grad,
        shifts_grad,
        qkv_owned,
        bias_grad,
        proj_owned,
        small[2:4],
        up_owned,
        upbias_grad,
        down_owned,
    )


def solution(mesh):
    split = P("mp", "dp", None)
    return jax.shard_map(
        local,
        mesh=mesh,
        in_specs=(
            split,
            P("dp"),
            P(),
            P(),
            P(None, "dp", "mp"),
            P(None, "mp"),
            P("mp", "dp"),
            P(),
            P("dp", "mp"),
            P("mp"),
            P("mp", "dp"),
            split,
        ),
        out_specs=(
            split,
            split,
            P(),
            P(),
            P(None, "dp", "mp"),
            P(None, "mp"),
            P("mp", "dp"),
            P(),
            P("dp", "mp"),
            P("mp"),
            P("mp", "dp"),
        ),
        check_vma=False,
    )
```

```python
import functools

import jax
import jax.numpy as jnp
from jax import lax
from jax.experimental import pallas as pl
from jax.experimental.pallas import tpu as pltpu
from jax.sharding import PartitionSpec as P

HEAD = 64
BUF = 64
BF = jnp.bfloat16
F32 = jnp.float32
epsilon = 1e-06
masked_score = -1e30
MIB = 1 << 20
NT = (((1,), (1,)), ((), ()))
NN = (((1,), (0,)), ((), ()))
TN = (((0,), (0,)), ((), ()))
factor = HEAD ** (-0.5)
VMEM_SPEC = pl.BlockSpec(memory_space=pltpu.VMEM)
ANY_SPEC = pl.BlockSpec(memory_space=pl.ANY)
SMEM_SPEC = pl.BlockSpec(memory_space=pltpu.SMEM)


def mm(a, b, dims=NN):
    return lax.dot_general(a, b, dims, preferred_element_type=F32)


def normalise(values):
    average = jnp.mean(values, axis=-1, keepdims=True)
    centred = values - average
    spread = jnp.mean(centred * centred, axis=-1, keepdims=True)
    inv = lax.rsqrt(spread + epsilon)
    return centred * inv, inv


def norm_back(n, inv, scales, grad):
    e = grad * scales
    mean_e = jnp.mean(e, axis=-1, keepdims=True)
    mean_en = jnp.mean(e * n, axis=-1, keepdims=True)
    return (e - mean_e - n * mean_en) * inv


def gelu_parts(inputs):
    normal_cdf = 0.5 + 0.5 * lax.erf(inputs * 0.7071067811865476)
    density = jnp.exp(-0.5 * inputs * inputs) * 0.3989422804014327
    return inputs * normal_cdf, normal_cdf + inputs * density


def for_each(count, step):
    if count <= 4:
        for index in range(count):
            step(index)
    else:
        pl.loop(0, count)(step)


def valid_slots(meta_ref, image, slots, axis):
    shape = (slots, 1) if axis == 0 else (1, slots)
    row = lax.broadcasted_iota(jnp.int32, shape, axis)
    n = slots // 4
    k = (row >= n).astype(jnp.int32) + (row >= 2 * n) + (row >= 3 * n)
    slot = (k ^ meta_ref[3]) * n + (row - k * n)
    return slot < BUF + meta_ref[image]


def block_rows(jj, size):
    start = jj * size
    return pl.ds(start if isinstance(jj, int) else pl.multiple_of(start, size), size)


def load_blocks(parts, refs, q, kinds, wq, wanted, place, sem):
    for (j0, i0, t0, count, absolute), ref in zip(parts, refs):
        nj, ni = ref.shape[:2]

        def one(jj, ref=ref, j0=j0, i0=i0, t0=t0, count=count, absolute=absolute, ni=ni):
            source = jj ^ q if absolute else jj
            for ii in range(ni):
                if i0 + ii not in wanted:
                    continue
                for t in range(t0, t0 + count):
                    if t in kinds:
                        pltpu.make_async_copy(
                            ref.at[source, ii, pl.ds((t - t0) * wq, wq)],
                            place(block_rows(j0 + jj, wq), i0 + ii, t),
                            sem,
                        ).start()

        for_each(nj, one)


def store_blocks(refs, q, n_j, block, i, sem):
    def start(views, target):
        for t, view in enumerate(views):
            pltpu.make_async_copy(view, target.at[t], sem).start()

    if len(refs) == 1:
        for_each(n_j, lambda jj: start(block(jj), refs[0].at[jj ^ q, i]))
        return
    own, to_x, to_y, keep_x, keep_y = refs
    start(block(0), own.at[i])
    if i == 0:
        start(block(1), keep_x.at[0])
        start(block(2), to_y.at[1])
        start(block(3), to_y.at[0])
    else:
        start(block(1), to_x.at[1])
        start(block(2), keep_y.at[0])
        start(block(3), to_x.at[0])


def grad_shapes(n_j, n_i, absolute, block):
    shape = lambda *lead: jax.ShapeDtypeStruct(lead + block, BF)
    if absolute:
        return [shape(n_j, n_i)]
    return [shape(2), shape(2), shape(2), shape(1), shape(1)]


def att_column(n_i, i, t):
    he = 2 * HEAD
    if t == 3:
        return 3 * n_i * he + i * he
    return (i // 2) * 6 * he + (t * 2 + i % 2) * he


def att_fwd_kernel(parts, n_i, x_ref, g_ref, c_ref, bias_ref, meta_ref, *rest):
    w_refs = rest[: len(parts)]
    n1_ref, qkva_ref, qkvb_ref, mixa_ref, mixb_ref, part_ref, w_scr, m_scr, sem = rest[len(parts) :]
    he = 2 * HEAD
    width = w_scr.shape[0]
    image = pl.program_id(0)

    @pl.when(image == 0)
    def _():
        place = lambda rows, i, t: w_scr.at[rows, pl.ds(att_column(n_i, i, t), he)]
        wq = width // (parts[-1][0] + w_refs[-1].shape[0])
        load_blocks(parts, w_refs, meta_ref[4], range(4), wq, range(n_i), place, sem)
        pltpu.make_async_copy(w_scr, w_scr, sem).wait()

    hat, _ = normalise(x_ref[0].astype(F32))
    n1 = (hat * g_ref[...] + c_ref[...]).astype(BF)
    n1_ref[...] = n1
    qkv_refs = (qkva_ref, qkvb_ref)
    for half in range(2):
        cols = pl.ds(half * 6 * he, 6 * he)
        res = (mm(n1, w_scr[:, cols]) + bias_ref[:, cols]).astype(BF)
        for n in range(6):
            qkv_refs[half][n] = res[:, n * he : (n + 1) * he]
    bias = jnp.where(valid_slots(meta_ref, image, x_ref.shape[1], 1), 0.0, masked_score)
    lane = lax.broadcasted_iota(jnp.int32, (1, he), 1)
    low_half = lane < HEAD
    for i in range(n_i):
        ref = qkv_refs[i // 2]
        q2, k2, v2 = (ref[t * 2 + i % 2] for t in range(3))
        outs = []
        for h in range(2):
            qm = jnp.where(low_half if h == 0 else ~low_half, q2, jnp.zeros_like(q2))
            s = mm(qm, k2, NT) * factor + bias
            top = jnp.max(s, axis=-1, keepdims=True)
            p = jnp.exp(s - top)
            w = (p / jnp.sum(p, axis=-1, keepdims=True)).astype(BF)
            outs.append(mm(w, v2))
        mixed = jnp.where(low_half, outs[0], outs[1]).astype(BF)
        m_scr[:, i * he : (i + 1) * he] = mixed
    mixa_ref[...] = m_scr[:, : 2 * he]
    mixb_ref[...] = m_scr[:, 2 * he :]
    part_ref[...] = mm(m_scr[...], w_scr[:, 3 * n_i * he :], NT).astype(BF)


def att_forward(x, gain, shift, bias, meta, parts, arrays):
    images, slots, width = x.shape
    n_i = 4
    he = 2 * HEAD
    rows = images * slots
    row_block = lambda last: pl.BlockSpec((slots, last), lambda a: (a, 0))
    whole = lambda *shape: pl.BlockSpec(shape, lambda a: (0,) * len(shape))
    qkv_block = pl.BlockSpec((6, slots, he), lambda a: (0, a, 0))
    return pl.pallas_call(
        functools.partial(att_fwd_kernel, parts, n_i),
        grid=(images,),
        in_specs=[
            pl.BlockSpec((1, slots, width), lambda a: (a, 0, 0)),
            whole(1, width),
            whole(1, width),
            whole(1, 3 * n_i * he),
            SMEM_SPEC,
        ]
        + [ANY_SPEC] * len(arrays),
        out_specs=[row_block(width), qkv_block, qkv_block, row_block(2 * he), row_block(2 * he), row_block(width)],
        out_shape=[
            jax.ShapeDtypeStruct((rows, width), BF),
            jax.ShapeDtypeStruct((6, rows, he), BF),
            jax.ShapeDtypeStruct((6, rows, he), BF),
            jax.ShapeDtypeStruct((rows, 2 * he), BF),
            jax.ShapeDtypeStruct((rows, 2 * he), BF),
            jax.ShapeDtypeStruct((rows, width), BF),
        ],
        scratch_shapes=[
            pltpu.VMEM((width, 4 * n_i * he), BF),
            pltpu.VMEM((slots, n_i * he), BF),
            pltpu.SemaphoreType.DMA,
        ],
        compiler_params=pltpu.CompilerParams(vmem_limit_bytes=48 * MIB),
        cost_estimate=pl.CostEstimate(flops=16_000_000_000, bytes_accessed=20_000_000, transcendentals=2_500_000),
        name="att_forward",
    )(x, gain, shift, bias, meta, *arrays)


def ffn_kernel(parts, n_i, n_j, n_out, first, last, *refs):
    if first:
        x_ref, pa_ref, pb_ref, b_ref, g_ref, c_ref = refs[:6]
        refs = refs[6:]
    else:
        n2, n2t, got, acc_b, acc_g = refs[:5]
        refs = refs[5:]
    go_ref, upb_ref, meta_ref = refs[:3]
    w_refs, refs = refs[3 : 3 + len(parts)], refs[3 + len(parts) :]
    q = meta_ref[4]
    if first:
        hidden_ref, n2, n2t, got = refs[:4]
        refs = refs[4:]
    sum_b, sum_g, upg_ref = refs[:3]
    grad_refs, refs = refs[3 : 3 + n_out], refs[3 + n_out :]
    wbuf, gbuf, act_s, pre_s, wsem, gsem = refs[:6]
    run_b, run_g = refs[6:] if last else (sum_b, sum_g)
    rows, width = go_ref.shape
    wq = width // n_j

    def fetch(i, slot):
        place = lambda rws, _, t: wbuf.at[slot, t, rws]
        load_blocks(parts, w_refs, q, range(2), wq, (i,), place, wsem.at[slot])

    def fetched(slot):
        pltpu.make_async_copy(wbuf.at[slot], wbuf.at[slot], wsem.at[slot]).wait()

    def put(i, slot):
        block = lambda jj: [gbuf.at[slot, t, block_rows(jj, wq)] for t in range(2)]
        store_blocks(grad_refs, q, n_j, block, i, gsem.at[slot])

    def stored(slot):
        pltpu.make_async_copy(gbuf.at[slot], gbuf.at[slot], gsem.at[slot]).wait()

    fetch(0, 0)
    if first:
        block = 192

        @pl.loop(0, rows // block)
        def _(r):
            rw = pl.ds(pl.multiple_of(r * block, block), block)
            h = (
                x_ref[rw, :].astype(F32)
                + (pa_ref[rw, :].astype(F32) + pb_ref[rw, :].astype(F32))
                + b_ref[...]
            )
            hidden_ref[rw, :] = h
            hat, _ = normalise(h)
            n2[rw, :] = (hat * g_ref[...] + c_ref[...]).astype(BF)

        n2t[...] = n2[...].T
        got[...] = go_ref[...].T
    rb = rows // 3
    for i in range(n_i):
        slot = i % 2
        if i + 1 < n_i:
            fetch(i + 1, 1 - slot)
        fetched(slot)

        @pl.loop(0, 3)
        def _(r, i=i, slot=slot):
            rw = pl.ds(pl.multiple_of(r * rb, rb), rb)
            u, w = wbuf[slot, 0], wbuf[slot, 1]
            up = mm(n2[rw, :], u) + upb_ref[i : i + 1, :]
            act, slope = gelu_parts(up)
            act = act.astype(BF)
            act_s[rw, :] = act
            pre = (mm(go_ref[rw, :], w) * slope).astype(BF)
            pre_s[rw, :] = pre
            down = mm(act, w, NT)
            back = mm(pre, u, NT)
            if i > 0:
                down += run_b[rw, :]
                back += run_g[rw, :]
            elif not first:
                down += acc_b[rw, :]
                back += acc_g[rw, :]
            if i < n_i - 1:
                run_b[rw, :] = down
                run_g[rw, :] = back
            else:
                sum_b[rw, :] = down.astype(sum_b.dtype)
                sum_g[rw, :] = back.astype(sum_g.dtype)

        upg_ref[i : i + 1, :] = jnp.sum(pre_s[...].astype(F32), axis=0, keepdims=True)
        if i >= 2:
            stored(slot)
        gbuf[slot, 0] = mm(n2t[...], pre_s[...]).astype(BF)
        gbuf[slot, 1] = mm(got[...], act_s[...]).astype(BF)
        put(i, slot)
    for i in range(max(n_i - 2, 0), n_i):
        stored(i % 2)


def ffn_call(ins, n_j, n_i, fh, parts, arrays, first, last, absolute):
    go = ins[-3]
    rows, width = go.shape
    wq = width // n_j
    made = (
        [
            jax.ShapeDtypeStruct((rows, width), F32),
            jax.ShapeDtypeStruct((rows, width), BF),
            jax.ShapeDtypeStruct((width, rows), BF),
            jax.ShapeDtypeStruct((width, rows), BF),
        ]
        if first
        else []
    )
    sums = BF if last else F32
    grads = grad_shapes(n_j, n_i, absolute, (2, wq, fh))
    return pl.pallas_call(
        functools.partial(ffn_kernel, parts, n_i, n_j, len(grads), first, last),
        in_specs=[VMEM_SPEC] * (len(ins) - 1) + [SMEM_SPEC] + [ANY_SPEC] * len(arrays),
        out_specs=[VMEM_SPEC] * (len(made) + 3) + [ANY_SPEC] * len(grads),
        out_shape=made
        + [
            jax.ShapeDtypeStruct((rows, width), sums),
            jax.ShapeDtypeStruct((rows, width), sums),
            jax.ShapeDtypeStruct((n_i, fh), F32),
        ]
        + grads,
        scratch_shapes=[
            pltpu.VMEM((2, 2, width, fh), BF),
            pltpu.VMEM((2, 2, width, fh), BF),
            pltpu.VMEM((rows, fh), BF),
            pltpu.VMEM((rows, fh), BF),
            pltpu.SemaphoreType.DMA((2,)),
            pltpu.SemaphoreType.DMA((2,)),
        ]
        + [pltpu.VMEM((rows, width), F32)] * (2 if last else 0),
        compiler_params=pltpu.CompilerParams(vmem_limit_bytes=58 * MIB),
        cost_estimate=pl.CostEstimate(
            flops=12_000_000_000 * n_i, bytes_accessed=30_000_000, transcendentals=1_000_000 * n_i
        ),
        name="ffn_first" if first else "ffn_last",
    )(*ins, *arrays)


def att_back_blocks(meta_ref, qkv_ref, gmix, gq, rows, which):
    he = 2 * HEAD
    images = 3
    slots = rows // images
    lane = lax.broadcasted_iota(jnp.int32, (1, he), 1)
    low_half = lane < HEAD

    @pl.loop(0, images)
    def _(a):
        rw = pl.ds(pl.multiple_of(a * slots, slots), slots)
        bias = jnp.where(valid_slots(meta_ref, a, slots, 0), 0.0, masked_score)
        for i in range(2):
            q2, k2, v2 = (qkv_ref[t * 2 + i, rw, :] for t in range(3))
            g2 = gmix[which + i, rw, :]
            dq, dk, dv = [], [], []
            for h in range(2):
                here = low_half if h == 0 else ~low_half
                qm = jnp.where(here, q2, jnp.zeros_like(q2))
                gm = jnp.where(here, g2, jnp.zeros_like(g2))
                st = mm(k2, qm, NT) * factor + bias
                top = jnp.max(st, axis=0, keepdims=True)
                p = jnp.exp(st - top)
                p = p / jnp.sum(p, axis=0, keepdims=True)
                dpt = mm(v2, gm, NT)
                dot = jnp.sum(p * dpt, axis=0, keepdims=True)
                ds = (p * (dpt - dot)).astype(BF)
                dk.append(mm(ds, q2))
                dv.append(mm(p.astype(BF), g2))
                dq.append(mm(ds, k2, TN))
            for t, (pair, scale) in enumerate(((dq, factor), (dk, factor), (dv, 1.0))):
                both = jnp.where(low_half, pair[0], pair[1])
                gq[rw, (t * 2 + i) * he : (t * 2 + i + 1) * he] = (both * scale).astype(BF)


def put_att_grads(grad_refs, q, n_j, wq, gbuf, gsem):
    he = 2 * HEAD
    for i in range(2):
        block = lambda jj, i=i: [
            gbuf.at[t, block_rows(jj, wq), pl.ds(i * he, he)] for t in range(4)
        ]
        store_blocks(grad_refs, q, n_j, block, i, gsem)


def hidden_back_kernel(
    parts, n_i, n_j, meta_ref, hid_ref, ga_ref, gb_ref, g_ref, go_ref, *rest
):
    w_refs = rest[: len(parts)]
    gh_ref, ght, gmixa, gmixb, sums_ref = rest[len(parts) : len(parts) + 5]
    ghb, w_scr, sem = rest[len(parts) + 5 :]
    rows, width = hid_ref.shape
    he = 2 * HEAD
    place = lambda rws, i, t: w_scr.at[rws, pl.ds(i * he, he)]
    load_blocks(parts, w_refs, meta_ref[4], (3,), width // n_j, range(n_i), place, sem)
    sums_ref[...] = jnp.zeros_like(sums_ref)
    pltpu.make_async_copy(w_scr, w_scr, sem).wait()
    block = 192

    @pl.loop(0, rows // block)
    def _(r):
        rw = pl.ds(pl.multiple_of(r * block, block), block)
        hat, inv = normalise(hid_ref[rw, :])
        grad = ga_ref[rw, :].astype(F32) + gb_ref[rw, :].astype(F32)
        gout = go_ref[rw, :].astype(F32)
        gh = gout + norm_back(hat, inv, g_ref[...], grad)
        gh_ref[rw, :] = gh
        low = gh.astype(BF)
        ghb[rw, :] = low
        sums_ref[0:1, :] += jnp.sum(grad * hat, axis=0, keepdims=True)
        sums_ref[1:2, :] += jnp.sum(grad, axis=0, keepdims=True)
        sums_ref[2:3, :] += jnp.sum(gh, axis=0, keepdims=True)
        sums_ref[3:4, :] += jnp.sum(gout, axis=0, keepdims=True)
        res = mm(low, w_scr[...]).astype(BF)
        for i in range(n_i):
            (gmixa, gmixb)[i // 2][i % 2, rw, :] = res[:, i * he : (i + 1) * he]

    ght[...] = ghb[...].T


def hidden_backward(meta, hidden, ga, gb, gain, go, n_j, parts, arrays):
    rows, width = hidden.shape
    n_i, he = 4, 2 * HEAD
    return pl.pallas_call(
        functools.partial(hidden_back_kernel, parts, n_i, n_j),
        in_specs=[SMEM_SPEC] + [VMEM_SPEC] * 5 + [ANY_SPEC] * len(arrays),
        out_specs=[VMEM_SPEC] * 5,
        out_shape=[
            jax.ShapeDtypeStruct((rows, width), F32),
            jax.ShapeDtypeStruct((width, rows), BF),
            jax.ShapeDtypeStruct((2, rows, he), BF),
            jax.ShapeDtypeStruct((2, rows, he), BF),
            jax.ShapeDtypeStruct((8, width), F32),
        ],
        scratch_shapes=[
            pltpu.VMEM((rows, width), BF),
            pltpu.VMEM((width, n_i * he), BF),
            pltpu.SemaphoreType.DMA,
        ],
        compiler_params=pltpu.CompilerParams(vmem_limit_bytes=48 * MIB),
        cost_estimate=pl.CostEstimate(flops=10_000_000_000, bytes_accessed=20_000_000, transcendentals=0),
        name="hidden_backward",
    )(meta, hidden, ga, gb, gain, go, *arrays)


def att_bwd_first_kernel(n_i, n_j, n_out, meta_ref, gmix, ght, n1_ref, qkv_ref, mix_ref, *rest):
    n1t, gq, bias_ref = rest[:3]
    grad_refs = rest[3 : 3 + n_out]
    gbuf, gsem = rest[3 + n_out :]
    width, rows = ght.shape
    he = 2 * HEAD
    gbuf[3] = mm(ght[...], mix_ref[...]).astype(BF)
    att_back_blocks(meta_ref, qkv_ref, gmix, gq, rows, 0)
    n1t[...] = n1_ref[...].T
    for t in range(3):
        gbuf[t] = mm(n1t[...], gq[:, 2 * t * he : 2 * (t + 1) * he]).astype(BF)
    put_att_grads(grad_refs, meta_ref[4], n_j, width // n_j, gbuf, gsem)
    bias_ref[...] = jnp.sum(gq[...].astype(F32), axis=0, keepdims=True)
    pltpu.make_async_copy(gbuf, gbuf, gsem).wait()


def att_backward_first(meta, gmix, ght, n1, qkv, mix, n_j, absolute):
    width, rows = ght.shape
    n_i, he = 4, 2 * HEAD
    wq = width // n_j
    grads = grad_shapes(n_j, 2, absolute, (4, wq, he))
    return pl.pallas_call(
        functools.partial(att_bwd_first_kernel, n_i, n_j, len(grads)),
        in_specs=[SMEM_SPEC] + [VMEM_SPEC] * 5,
        out_specs=[VMEM_SPEC] * 3 + [ANY_SPEC] * len(grads),
        out_shape=[
            jax.ShapeDtypeStruct((width, rows), BF),
            jax.ShapeDtypeStruct((rows, 6 * he), BF),
            jax.ShapeDtypeStruct((1, 6 * he), F32),
        ]
        + grads,
        scratch_shapes=[pltpu.VMEM((4, width, 2 * he), BF), pltpu.SemaphoreType.DMA],
        compiler_params=pltpu.CompilerParams(vmem_limit_bytes=48 * MIB),
        cost_estimate=pl.CostEstimate(flops=16_000_000_000, bytes_accessed=20_000_000, transcendentals=1_250_000),
        name="att_backward_first",
    )(meta, gmix, ght, n1, qkv, mix)


def att_bwd_last_kernel(
    parts, n_i, n_j, n_out, meta_ref, x_ref, gmix, ght, n1t, gqa_ref, qkv_ref, mix_ref, *rest
):
    w_refs = rest[: len(parts)]
    gn1_ref, bias_ref, sums_ref = rest[len(parts) : len(parts) + 3]
    rest = rest[len(parts) + 3 :]
    grad_refs = rest[:n_out]
    gq, w_scr, gbuf, sem, gsem = rest[n_out:]
    rows, width = x_ref.shape
    he = 2 * HEAD
    wq = width // n_j
    q = meta_ref[4]
    place = lambda rws, i, t: w_scr.at[rws, pl.ds(att_column(n_i, i, t), he)]
    load_blocks(parts, w_refs, q, (0, 1, 2), wq, range(n_i), place, sem)
    gbuf[3] = mm(ght[...], mix_ref[...]).astype(BF)
    att_back_blocks(meta_ref, qkv_ref, gmix, gq, rows, 0)
    for t in range(3):
        gbuf[t] = mm(n1t[...], gq[:, 2 * t * he : 2 * (t + 1) * he]).astype(BF)
    put_att_grads(grad_refs, q, n_j, wq, gbuf, gsem)
    bias_ref[...] = jnp.sum(gq[...].astype(F32), axis=0, keepdims=True)
    sums_ref[...] = jnp.zeros_like(sums_ref)
    pltpu.make_async_copy(w_scr, w_scr, sem).wait()
    rb = rows // 3

    @pl.loop(0, 3)
    def _(r):
        rw = pl.ds(pl.multiple_of(r * rb, rb), rb)
        grad = mm(gqa_ref[rw, :], w_scr[:, : 6 * he], NT) + mm(gq[rw, :], w_scr[:, 6 * he :], NT)
        gn1_ref[rw, :] = grad.astype(BF)
        hat, _ = normalise(x_ref[rw, :].astype(F32))
        sums_ref[0:1, :] += jnp.sum(grad * hat, axis=0, keepdims=True)
        sums_ref[1:2, :] += jnp.sum(grad, axis=0, keepdims=True)

    pltpu.make_async_copy(gbuf, gbuf, gsem).wait()


def att_backward_last(meta, x, gmix, ght, n1t, gqa, qkv, mix, n_j, parts, arrays, absolute):
    rows, width = x.shape
    n_i, he = 4, 2 * HEAD
    wq = width // n_j
    grads = grad_shapes(n_j, 2, absolute, (4, wq, he))
    return pl.pallas_call(
        functools.partial(att_bwd_last_kernel, parts, n_i, n_j, len(grads)),
        in_specs=[SMEM_SPEC] + [VMEM_SPEC] * 7 + [ANY_SPEC] * len(arrays),
        out_specs=[VMEM_SPEC] * 3 + [ANY_SPEC] * len(grads),
        out_shape=[
            jax.ShapeDtypeStruct((rows, width), BF),
            jax.ShapeDtypeStruct((1, 6 * he), F32),
            jax.ShapeDtypeStruct((8, width), F32),
        ]
        + grads,
        scratch_shapes=[
            pltpu.VMEM((rows, 6 * he), BF),
            pltpu.VMEM((width, 3 * n_i * he), BF),
            pltpu.VMEM((4, width, 2 * he), BF),
            pltpu.SemaphoreType.DMA,
            pltpu.SemaphoreType.DMA,
        ],
        compiler_params=pltpu.CompilerParams(vmem_limit_bytes=56 * MIB),
        cost_estimate=pl.CostEstimate(flops=20_000_000_000, bytes_accessed=30_000_000, transcendentals=1_250_000),
        name="att_backward_last",
    )(meta, x, gmix, ght, n1t, gqa, qkv, mix, *arrays)


def swap(x, axis, bits, what):
    n = lax.axis_size(axis)
    with jax.named_scope(what):
        return lax.ppermute(x, axis, [(i, i ^ bits) for i in range(n)])


def after(x, *deps):
    return lax.optimization_barrier((x,) + deps)[0] if deps else x


def add(*parts):
    total = parts[0].astype(F32)
    for part in parts[1:]:
        total = total + part.astype(F32)
    return total.astype(parts[0].dtype)


def planes():
    n_dp = lax.axis_size("dp")
    return [list(range(core, n_dp, 2)) for core in range(2)]


def gather_plane(block, what):
    with jax.named_scope(what):
        return lax.all_gather(block, "dp", axis_index_groups=planes())


def scatter_plane(blocks, what):
    flat = blocks.reshape(-1, blocks.shape[-1])
    with jax.named_scope(what):
        mine = lax.psum_scatter(
            flat, "dp", scatter_dimension=0, axis_index_groups=planes(), tiled=True
        )
    return mine.reshape(blocks.shape[1:])


def gather_near(own, what):
    return swap(own, "dp", 2, what + "_x1"), swap(own, "dp", 4, what + "_y1")


def gather_far(one, two, what):
    half = one.shape[0] // 2
    return swap(one[:half], "dp", 4, what + "_y2"), swap(two[half:], "dp", 2, what + "_x2")


def scatter_reach(grads, what):
    if len(grads) == 1:
        return (scatter_plane(grads[0], what),)
    _, to_x, to_y, _, _ = grads
    return swap(to_x, "dp", 2, what + "_x1"), swap(to_y, "dp", 4, what + "_y1")


def scatter_last(grads, reach, what):
    if len(grads) == 1:
        return ()
    from_x, from_y = reach
    _, _, _, keep_x, keep_y = grads
    on_x, on_y = add(keep_x[0], from_y[0]), add(keep_y[0], from_x[0])
    return swap(on_x, "dp", 2, what + "_x2"), swap(on_y, "dp", 4, what + "_y2")


def scatter_sum(grads, reach, last):
    if len(grads) == 1:
        return reach[0][0], reach[0][1]
    own = grads[0]
    return add(own[0], reach[1][1], last[0]), add(own[1], reach[0][1], last[1])


def gather_z(own, what):
    two = swap(own, "mp", 2, what + "_z2")
    one = swap(own, "mp", 1, what + "_z1")
    return one, two, swap(two, "mp", 1, what + "_z3")


def scatter_z(zero, one, two, three, what):
    two = add(two, swap(three, "mp", 1, what + "_z3"))
    return add(zero, swap(one, "mp", 1, what + "_z1"), swap(two, "mp", 2, what + "_z2"))


def ordered_pair(own, other, core, axis=0):
    return jnp.stack(
        [jnp.where(core == 0, own, other), jnp.where(core == 0, other, own)], axis
    )


def image_routes(n_dp, n_mp, odd):
    pairs = []
    for plane in range(n_dp // 2):
        for core in range(2):
            for z in range(n_mp):
                shift = 2 * core + odd
                worker = (plane * 2 + core) * n_mp + z
                holder = (plane * 2 + (z >> 1)) * n_mp + (z ^ shift)
                pairs.append((holder, worker))
    return pairs


def to_images(x, z, what):
    n_dp, n_mp = lax.axis_size("dp"), lax.axis_size("mp")
    slots, images, width = x.shape
    groups = jnp.transpose(x, (1, 0, 2)).reshape(2, images // 2, slots, width)
    got = []
    for odd in (0, 1):
        send = lax.dynamic_index_in_dim(groups, (z ^ odd) & 1, 0, False)
        with jax.named_scope(what + "_route" + str(odd)):
            got.append(lax.ppermute(send, ("dp", "mp"), image_routes(n_dp, n_mp, odd)))
    return got


def from_images(y, z, what):
    n_dp, n_mp = lax.axis_size("dp"), lax.axis_size("mp")
    back = []
    for odd in (0, 1):
        routes = [(b, a) for a, b in image_routes(n_dp, n_mp, odd)]
        with jax.named_scope(what + "_route" + str(odd)):
            back.append(lax.ppermute(y[:, odd], ("dp", "mp"), routes))
    return back


def joined_images(back, z):
    flip = (z & 1) == 1
    groups = jnp.concatenate([jnp.where(flip, back[1], back[0]), jnp.where(flip, back[0], back[1])])
    return jnp.transpose(groups, (1, 0, 2))


def local(
    tokens,
    counts,
    norm_gains,
    norm_shifts,
    qkv_weight,
    qkv_bias,
    proj_weight,
    out_biases,
    up_weight,
    up_bias,
    down_weight,
    cotangent,
):
    slots, images, width = tokens.shape
    n_dp, n_mp = lax.axis_size("dp"), lax.axis_size("mp")
    n_q = n_dp // 2
    wq = width // n_q
    dp, z = lax.axis_index("dp"), lax.axis_index("mp")
    q, core = dp >> 1, dp & 1
    own_images = images // 2
    all_slots = slots * n_mp
    rows = own_images * all_slots

    def rel(v):
        blocks = [lax.dynamic_slice_in_dim(v, (q ^ j) * wq, wq, v.ndim - 1) for j in range(n_q)]
        return jnp.concatenate(blocks, -1)

    def half_of(v, which, axis):
        size = v.shape[axis] // 2
        return lax.dynamic_slice_in_dim(v, which * size, size, axis)

    att = jnp.concatenate([qkv_weight, jnp.transpose(proj_weight)[None]])
    ffn_w = jnp.stack([up_weight, jnp.transpose(down_weight)])
    he, fh = att.shape[-1] // 2, ffn_w.shape[-1] // 2

    count_rows = jnp.pad(counts.astype(BF)[None], ((0, 15), (0, he - images)))
    sent = jnp.concatenate([half_of(att, 1 - core, 2).reshape(-1, he), count_rows])
    got = swap(sent, "dp", 1, "att_w_core")
    other_counts = got[-16, :images].astype(jnp.int32)
    got = got[:-16].reshape(4, wq // 2, he)
    att_own = ordered_pair(half_of(att, core, 2), got, core, 1).reshape(-1, he)
    got = swap(half_of(ffn_w, 1 - core, 2), "dp", 1, "ffn_w_core")
    ffn_own = ordered_pair(half_of(ffn_w, core, 2), got, core, 1).reshape(2, wq, fh)
    left = jnp.concatenate(
        [half_of(qkv_bias, core, 1), half_of(up_bias, core, 0).reshape(-1, he)]
    )
    n_bias = left.shape[0]
    terms = []
    for _ in range(3):
        term = lax.reduce_precision(left, 8, 7)
        terms.append(term.astype(BF))
        left = left - term
    bias_pad = -(-3 * n_bias // 16) * 16
    bias_terms = jnp.pad(jnp.concatenate(terms), ((0, bias_pad - 3 * n_bias), (0, 0)))

    counts_here = jnp.where((z >> 1) == core, counts, other_counts)
    counts_here = lax.dynamic_slice_in_dim(counts_here, (z & 1) * own_images, own_images, 0)
    meta = jnp.concatenate([counts_here, z[None], q[None]])
    slot_ids = jnp.arange(slots, dtype=jnp.int32)
    keep_mine = ((z * slots + slot_ids)[:, None] < BUF + counts[None, :])[:, :, None]

    def whole_rows(got, what):
        return ordered_pair(got, swap(got, "dp", 1, what), core, 1).reshape(rows, width)

    n_i = n_mp
    gains, shifts, out_b = rel(norm_gains), rel(norm_shifts), rel(out_biases)
    square = n_q == 4
    pair_places = [(j, i, 0, 2, False) for j, i in ((0, 0), (1, 0), (2, 0), (3, 0), (3, 1))]
    both = lax.optimization_barrier

    def flat(v):
        return v.reshape(v.shape[:-3] + (-1, v.shape[-1]))

    row_half = lambda v, which: half_of(v.reshape(own_images, n_mp, slots, width), which, 1)

    att_mine = jnp.concatenate([att_own, bias_terms])
    two = swap(att_mine, "mp", 2, "att_w_z2")
    one = swap(att_mine, "mp", 1, "att_w_z1")
    one, two, tokens_in, ffn_own = both((one, two, rel(tokens), ffn_own))
    three = swap(two, "mp", 1, "att_w_z3")
    token_rows = to_images(tokens_in, z, "tokens")
    att_z = jnp.stack([att_mine, one, two, three])
    bias_all = att_z[:, 4 * wq : 4 * wq + 3 * n_bias].astype(F32).reshape(n_i, 3, n_bias, he)
    bias_all = bias_all[:, 0] + (bias_all[:, 1] + bias_all[:, 2])
    bias_three = jnp.stack([bias_all[:, 0], jnp.zeros((n_i, he), F32), bias_all[:, 1]])
    bias_rows = jnp.transpose(bias_three.reshape(3, 2, 2, he), (1, 0, 2, 3)).reshape(1, -1)
    att_near = gather_near(att_z, "att_w") if square else ()
    cot = rel(jnp.where(keep_mine, cotangent, jnp.zeros_like(cotangent)))
    token_rows, att_near, ffn_own, cot, bias_rows = both((token_rows, att_near, ffn_own, cot, bias_rows))

    if square:
        att_far = gather_far(*att_near, "att_w")
        att_places = [(j, i, 0, 4, False) for j, i in ((0, 0), (1, 0), (2, 0), (3, 0), (3, 2))]
    else:
        att_far, att_places = (gather_plane(att_z, "att_w"),), [(0, 0, 0, 4, True)]
    x = whole_rows(jnp.stack(token_rows, 1), "tokens_core")
    one, two = swap(ffn_own, "mp", 1, "ffn_w_z1"), swap(ffn_own, "mp", 2, "ffn_w_z2")
    x, att_far, cot, ffn_own = both((x, att_far, cot, ffn_own))
    att_parts = [v[None] for v in (att_z, *att_near, *att_far)] if square else list(att_far)
    cot_rows = to_images(cot, z, "cotangent")
    n1, qkva, qkvb, mixa, mixb, part = att_forward(
        x.reshape(own_images, all_slots, width),
        gains[0:1],
        shifts[0:1],
        bias_rows,
        meta,
        att_places,
        att_parts,
    )
    part, one, two, n1, x, cot_rows[0] = both((part, one, two, n1, x, cot_rows[0]))

    part_other = swap(part, "dp", 1, "attended")
    three = swap(two, "mp", 1, "ffn_w_z3")
    ffn_here = flat(jnp.stack([ffn_own, one]))
    here_near = gather_near(ffn_here, "ffn_w0") if square else ()
    here_near, three, part_other, cot_rows = both((here_near, three, part_other, cot_rows))
    go = whole_rows(jnp.stack(cot_rows, 1), "cotangent_core")
    ffn_far = flat(jnp.stack([two, three]))
    if square:
        here_far = gather_far(*here_near, "ffn_w0")
        go, here_far, ffn_far = both((go, here_far, ffn_far))
        parts0 = [v[None] for v in (ffn_here, *here_near, *here_far)]
        far_near = gather_near(ffn_far, "ffn_w2")
        places = pair_places
    else:
        parts0, places, far_near = [gather_plane(ffn_here, "ffn_w0")], [(0, 0, 0, 2, True)], ()
    up_rows = bias_all[:, 2:].reshape(n_i, fh)
    hidden, n2, n2t, got, sum_b, sum_g, upg0, *ffn_g0 = ffn_call(
        [x, part, part_other, out_b[0:1], gains[1:2], shifts[1:2], go, up_rows[:2], meta],
        n_q,
        2,
        fh,
        places,
        parts0,
        True,
        False,
        not square,
    )
    n2, far_near, ffn_g0 = both((n2, far_near, ffn_g0))
    if square:
        far_far = gather_far(*far_near, "ffn_w2")
        parts1 = [v[None] for v in (ffn_far, *far_near, *far_far)]
    else:
        parts1 = [gather_plane(ffn_far, "ffn_w2")]
    n2, parts1, ffn_g0 = both((n2, parts1, ffn_g0))
    reach_f0 = scatter_reach(ffn_g0, "ffn_g0")
    branch, gn2, upg1, *ffn_g1 = ffn_call(
        [n2, n2t, got, sum_b, sum_g, go, up_rows[2:], meta],
        n_q,
        2,
        fh,
        places,
        parts1,
        False,
        True,
        not square,
    )
    branch, gn2, ffn_g1, reach_f0 = both((branch, gn2, ffn_g1, reach_f0))

    last_f0 = scatter_last(ffn_g0, reach_f0, "ffn_g0")
    reach_f1 = scatter_reach(ffn_g1, "ffn_g1")
    gn2_other = swap(gn2, "dp", 1, "grad_norm_two")
    gn2_other, branch = both((gn2_other, branch))
    theirs = swap(row_half(branch, 1 - core), "dp", 1, "branch")
    gh, ght, gmixa, gmixb, sums = hidden_backward(
        meta, hidden, gn2, gn2_other, gains[1:2], go, n_q, att_places, att_parts
    )
    gmixa, last_f0, theirs, branch = both((gmixa, last_f0, theirs, branch))
    ffn0, ffn1 = scatter_sum(ffn_g0, reach_f0, last_f0)
    out_half = row_half(hidden, core) + row_half(branch, core).astype(F32) + theirs.astype(F32) + out_b[1]
    gmixa, out_half, ffn0, ffn1 = both((gmixa, rel(out_half.astype(BF)), ffn0, ffn1))
    out_routes = from_images(out_half, z, "block_out")
    n1t, gqa, bias_a, *att_ga = att_backward_first(
        meta, gmixa, ght, n1, qkva, mixa, n_q, not square
    )
    n1t, gqa, reach_f1, att_ga, out_routes, ffn1 = both((n1t, gqa, reach_f1, att_ga, out_routes, ffn1))
    reach_aa = scatter_reach(att_ga, "att_ga")
    last_f1 = scatter_last(ffn_g1, reach_f1, "ffn_g1")
    ffn_one = swap(ffn1, "mp", 1, "ffn_g_z1")
    gn1, bias_b, more_sums, *att_gb = att_backward_last(
        meta, x, gmixb, ght, n1t, gqa, qkvb, mixb, n_q, att_places, att_parts, not square
    )
    gn1, out_routes, last_f1, ffn_one, reach_aa, att_gb, x = both(
        (gn1, out_routes, last_f1, ffn_one, reach_aa, att_gb, x)
    )

    gn1_other = swap(row_half(gn1, 1 - core), "dp", 1, "grad_norm_one")
    ffn2, ffn3 = scatter_sum(ffn_g1, reach_f1, last_f1)
    ffn_three = swap(ffn3, "mp", 1, "ffn_g_z3")
    last_aa = scatter_last(att_ga, reach_aa, "att_ga")
    gn1_other, att_gb = both((gn1_other, att_gb))
    gn1 = row_half(gn1, core).astype(F32) + gn1_other.astype(F32)
    hat1, inv1 = normalise(row_half(x, core).astype(F32))
    input_half = row_half(gh, core) + norm_back(hat1, inv1, gains[0], gn1)
    input_half = rel(input_half.astype(BF))
    in_routes = from_images(input_half, z, "input_grad")
    reach_ab = scatter_reach(att_gb, "att_gb")
    ffn_three, last_aa, reach_ab, input_half, upg0, upg1, bias_a, bias_b, sums, more_sums, out_routes = both(
        (ffn_three, last_aa, reach_ab, input_half, upg0, upg1, bias_a, bias_b, sums, more_sums, out_routes)
    )
    ffn_two = swap(add(ffn2, ffn_three), "mp", 2, "ffn_g_z2")
    last_ab = scatter_last(att_gb, reach_ab, "att_gb")
    att0, att1 = scatter_sum(att_ga, reach_aa, last_aa)
    att2, att3 = scatter_sum(att_gb, reach_ab, last_ab)
    att_grad = scatter_z(att0, att1, att2, att3, "att_g")
    ffn_grad = add(ffn0, ffn_one, ffn_two)
    block_out = joined_images(out_routes, z)
    block_out = jnp.where(keep_mine, block_out, jnp.zeros_like(block_out))
    input_grad = joined_images(in_routes, z)

    def own_shard(grad, what):
        kinds, _, last = grad.shape
        pair = grad.reshape(kinds, 2, wq // 2, last)
        keep = lax.dynamic_index_in_dim(pair, core, 1, False)
        got = swap(lax.dynamic_index_in_dim(pair, 1 - core, 1, False), "dp", 1, what)
        return ordered_pair(keep, got, core, 2).reshape(kinds, wq // 2, 2 * last).astype(F32)

    att_shard, ffn_shard = own_shard(att_grad, "att_g_core"), own_shard(ffn_grad, "ffn_g_core")
    qkv_owned, proj_owned = att_shard[:3], jnp.transpose(att_shard[3])
    up_owned, down_owned = ffn_shard[0], jnp.transpose(ffn_shard[1])

    def placed(values):
        mine = jnp.concatenate([lax.dynamic_slice_in_dim(values, z ^ i, 1, 0) for i in range(n_i)])
        return jnp.stack([jnp.where(core == c, mine, jnp.zeros_like(mine)) for c in range(2)], 1)

    bias_a, bias_b = (v.reshape(3, 2, he) for v in (bias_a, bias_b))
    wide = [placed(jnp.concatenate([bias_a[t], bias_b[t]])) for t in (0, 2)]
    wide.append(placed(jnp.concatenate([upg0, upg1])))
    small = [rel(sums), rel(more_sums)]
    values = [*wide, *small]
    vector = jnp.concatenate([v.reshape(-1, 128) for v in values])
    for axis, size in (("dp", n_dp), ("mp", n_mp)):
        bit = 1
        while bit < size:
            vector = vector + swap(vector, axis, bit, "sums_" + axis + str(bit))
            bit *= 2
    ends = [0]
    for v in values:
        ends.append(ends[-1] + v.size // 128)
    *wide, sums, more_sums = [
        vector[start:end].reshape(v.shape) for v, start, end in zip(values, ends, ends[1:])
    ]
    wide = [lax.dynamic_index_in_dim(v, z, 0, False).reshape(-1) for v in wide]
    bias_grad, upbias_grad = jnp.stack(wide[:2]), wide[2]
    gains_grad = jnp.stack([more_sums[0], sums[0] * 0.5])
    shifts_grad = jnp.stack([more_sums[1], sums[1] * 0.5])
    outbias_grad = sums[2:4] * 0.5
    return (
        block_out,
        input_grad,
        gains_grad,
        shifts_grad,
        qkv_owned,
        bias_grad,
        proj_owned,
        outbias_grad,
        up_owned,
        upbias_grad,
        down_owned,
    )


def solution(mesh):
    split = P("mp", "dp", None)
    return jax.shard_map(
        local,
        mesh=mesh,
        in_specs=(
            split,
            P("dp"),
            P(),
            P(),
            P(None, "dp", "mp"),
            P(None, "mp"),
            P("mp", "dp"),
            P(),
            P("dp", "mp"),
            P("mp"),
            P("mp", "dp"),
            split,
        ),
        out_specs=(
            split,
            split,
            P(),
            P(),
            P(None, "dp", "mp"),
            P(None, "mp"),
            P("mp", "dp"),
            P(),
            P("dp", "mp"),
            P("mp"),
            P("mp", "dp"),
        ),
        check_vma=False,
    )
```

```python
import functools

import jax
import jax.numpy as jnp
from jax import lax
from jax.experimental import pallas as pl
from jax.experimental.pallas import tpu as pltpu
from jax.sharding import PartitionSpec as P

HEAD = 64
BUF = 64
BF = jnp.bfloat16
F32 = jnp.float32
epsilon = 1e-06
masked_score = -1e30
MIB = 1 << 20
NT = (((1,), (1,)), ((), ()))
NN = (((1,), (0,)), ((), ()))
TN = (((0,), (0,)), ((), ()))
factor = HEAD ** (-0.5)
VMEM_SPEC = pl.BlockSpec(memory_space=pltpu.VMEM)
ANY_SPEC = pl.BlockSpec(memory_space=pl.ANY)
SMEM_SPEC = pl.BlockSpec(memory_space=pltpu.SMEM)


def mm(a, b, dims=NN):
    return lax.dot_general(a, b, dims, preferred_element_type=F32)


def normalise(values):
    average = jnp.mean(values, axis=-1, keepdims=True)
    centred = values - average
    spread = jnp.mean(centred * centred, axis=-1, keepdims=True)
    inv = lax.rsqrt(spread + epsilon)
    return centred * inv, inv


def norm_back(n, inv, scales, grad):
    e = grad * scales
    mean_e = jnp.mean(e, axis=-1, keepdims=True)
    mean_en = jnp.mean(e * n, axis=-1, keepdims=True)
    return (e - mean_e - n * mean_en) * inv


def gelu_parts(inputs):
    normal_cdf = 0.5 + 0.5 * lax.erf(inputs * 0.7071067811865476)
    density = jnp.exp(-0.5 * inputs * inputs) * 0.3989422804014327
    return inputs * normal_cdf, normal_cdf + inputs * density


def for_each(count, step):
    if count <= 4:
        for index in range(count):
            step(index)
    else:
        pl.loop(0, count)(step)


def valid_slots(meta_ref, image, slots, axis):
    shape = (slots, 1) if axis == 0 else (1, slots)
    row = lax.broadcasted_iota(jnp.int32, shape, axis)
    n = slots // 4
    k = (row >= n).astype(jnp.int32) + (row >= 2 * n) + (row >= 3 * n)
    slot = (k ^ meta_ref[3]) * n + (row - k * n)
    return slot < BUF + meta_ref[image]


def block_rows(jj, size):
    start = jj * size
    return pl.ds(start if isinstance(jj, int) else pl.multiple_of(start, size), size)


def load_blocks(parts, refs, q, kinds, wq, wanted, place, sem):
    for (j0, i0, t0, count, absolute), ref in zip(parts, refs):
        nj, ni = ref.shape[:2]

        def one(jj, ref=ref, j0=j0, i0=i0, t0=t0, count=count, absolute=absolute, ni=ni):
            source = jj ^ q if absolute else jj
            for ii in range(ni):
                if i0 + ii not in wanted:
                    continue
                for t in range(t0, t0 + count):
                    if t in kinds:
                        pltpu.make_async_copy(
                            ref.at[source, ii, pl.ds((t - t0) * wq, wq)],
                            place(block_rows(j0 + jj, wq), i0 + ii, t),
                            sem,
                        ).start()

        for_each(nj, one)


def store_blocks(refs, q, n_j, block, i, sem, pair=0):
    def start(views, target):
        for t, view in enumerate(views):
            pltpu.make_async_copy(view, target.at[t], sem).start()

    if len(refs) == 1:
        for_each(n_j, lambda jj: start(block(jj), refs[0].at[jj ^ q, 2 * pair + i]))
        return
    own, to_x, to_y, keep_x, keep_y = refs
    start(block(0), own.at[2 * pair + i])
    if i == 0:
        start(block(1), keep_x.at[pair])
        start(block(2), to_y.at[2 * pair + 1])
        start(block(3), to_y.at[2 * pair])
    else:
        start(block(1), to_x.at[2 * pair + 1])
        start(block(2), keep_y.at[pair])
        start(block(3), to_x.at[2 * pair])


def grad_shapes(n_j, n_i, absolute, block):
    shape = lambda *lead: jax.ShapeDtypeStruct(lead + block, BF)
    if absolute:
        return [shape(n_j, n_i)]
    return [shape(n_i), shape(n_i), shape(n_i), shape(n_i // 2), shape(n_i // 2)]


def att_column(n_i, i, t):
    he = 2 * HEAD
    if t == 3:
        return 3 * n_i * he + i * he
    return (i // 2) * 6 * he + (t * 2 + i % 2) * he


def att_fwd_kernel(parts, n_i, x_ref, g_ref, c_ref, bias_ref, meta_ref, *rest):
    w_refs = rest[: len(parts)]
    n1_ref, qkva_ref, qkvb_ref, mixa_ref, mixb_ref, part_ref, w_scr, m_scr, sem = rest[len(parts) :]
    he = 2 * HEAD
    width = w_scr.shape[0]
    image = pl.program_id(0)

    @pl.when(image == 0)
    def _():
        place = lambda rows, i, t: w_scr.at[rows, pl.ds(att_column(n_i, i, t), he)]
        wq = width // max(p[0] + r.shape[0] for p, r in zip(parts, w_refs))
        load_blocks(parts, w_refs, meta_ref[4], range(4), wq, range(n_i), place, sem)
        pltpu.make_async_copy(w_scr, w_scr, sem).wait()

    hat, _ = normalise(x_ref[0].astype(F32))
    n1 = (hat * g_ref[...] + c_ref[...]).astype(BF)
    n1_ref[...] = n1
    qkv_refs = (qkva_ref, qkvb_ref)
    for half in range(2):
        cols = pl.ds(half * 6 * he, 6 * he)
        res = (mm(n1, w_scr[:, cols]) + bias_ref[:, cols]).astype(BF)
        for n in range(6):
            qkv_refs[half][n] = res[:, n * he : (n + 1) * he]
    bias = jnp.where(valid_slots(meta_ref, image, x_ref.shape[1], 1), 0.0, masked_score)
    lane = lax.broadcasted_iota(jnp.int32, (1, he), 1)
    low_half = lane < HEAD
    for i in range(n_i):
        ref = qkv_refs[i // 2]
        q2, k2, v2 = (ref[t * 2 + i % 2] for t in range(3))
        outs = []
        for h in range(2):
            qm = jnp.where(low_half if h == 0 else ~low_half, q2, jnp.zeros_like(q2))
            s = mm(qm, k2, NT) * factor + bias
            top = jnp.max(s, axis=-1, keepdims=True)
            p = jnp.exp(s - top)
            w = (p / jnp.sum(p, axis=-1, keepdims=True)).astype(BF)
            outs.append(mm(w, v2))
        mixed = jnp.where(low_half, outs[0], outs[1]).astype(BF)
        m_scr[:, i * he : (i + 1) * he] = mixed
    mixa_ref[...] = m_scr[:, : 2 * he]
    mixb_ref[...] = m_scr[:, 2 * he :]
    part_ref[...] = mm(m_scr[...], w_scr[:, 3 * n_i * he :], NT).astype(BF)


def att_forward(x, gain, shift, bias, meta, parts, arrays):
    images, slots, width = x.shape
    n_i = 4
    he = 2 * HEAD
    rows = images * slots
    row_block = lambda last: pl.BlockSpec((slots, last), lambda a: (a, 0))
    whole = lambda *shape: pl.BlockSpec(shape, lambda a: (0,) * len(shape))
    qkv_block = pl.BlockSpec((6, slots, he), lambda a: (0, a, 0))
    return pl.pallas_call(
        functools.partial(att_fwd_kernel, parts, n_i),
        grid=(images,),
        in_specs=[
            pl.BlockSpec((1, slots, width), lambda a: (a, 0, 0)),
            whole(1, width),
            whole(1, width),
            whole(1, 3 * n_i * he),
            SMEM_SPEC,
        ]
        + [ANY_SPEC] * len(arrays),
        out_specs=[row_block(width), qkv_block, qkv_block, row_block(2 * he), row_block(2 * he), row_block(width)],
        out_shape=[
            jax.ShapeDtypeStruct((rows, width), BF),
            jax.ShapeDtypeStruct((6, rows, he), BF),
            jax.ShapeDtypeStruct((6, rows, he), BF),
            jax.ShapeDtypeStruct((rows, 2 * he), BF),
            jax.ShapeDtypeStruct((rows, 2 * he), BF),
            jax.ShapeDtypeStruct((rows, width), BF),
        ],
        scratch_shapes=[
            pltpu.VMEM((width, 4 * n_i * he), BF),
            pltpu.VMEM((slots, n_i * he), BF),
            pltpu.SemaphoreType.DMA,
        ],
        compiler_params=pltpu.CompilerParams(vmem_limit_bytes=48 * MIB),
        cost_estimate=pl.CostEstimate(flops=16_000_000_000, bytes_accessed=20_000_000, transcendentals=2_500_000),
        name="att_forward",
    )(x, gain, shift, bias, meta, *arrays)


def ffn_kernel(parts, n_i, n_j, n_out, first, *refs):
    if first:
        x_ref, pa_ref, pb_ref, b_ref, g_ref, c_ref = refs[:6]
        refs = refs[6:]
    else:
        kept, refs = refs[:5], refs[5:]
    go_ref, upb_ref, meta_ref = refs[:3]
    w_refs, refs = refs[3 : 3 + len(parts)], refs[3 + len(parts) :]
    q = meta_ref[4]
    if first:
        hidden_out, refs = refs[0], refs[1:]
        kept, refs = refs[:5], refs[5:]
        sum_outs = kept[3:]
    else:
        sum_outs, refs = refs[:2], refs[2:]
    upg_ref, refs = refs[0], refs[1:]
    grad_refs, refs = refs[:n_out], refs[n_out:]
    n2, n2t, got, run_b, run_g, wbuf, gbuf, act_s, pre_s, wsem, gsem, ksem, ssem = refs[:13]
    held = (n2, n2t, got, run_b, run_g)
    if first:
        hidden, hsem = refs[13:]
        low_sums = (run_b, run_g)
    else:
        low_sums = refs[13:]
    rows, width = go_ref.shape
    wq = width // n_j
    rb = rows // 3

    def fetch(i, slot):
        place = lambda rws, _, t: wbuf.at[slot, t, rws]
        load_blocks(parts, w_refs, q, range(2), wq, (i,), place, wsem.at[slot])

    def fetched(slot):
        pltpu.make_async_copy(wbuf.at[slot], wbuf.at[slot], wsem.at[slot]).wait()

    def put(i, slot):
        block = lambda jj: [gbuf.at[slot, t, block_rows(jj, wq)] for t in range(2)]
        store_blocks(grad_refs, q, n_j, block, i, gsem.at[slot])

    def stored(slot):
        pltpu.make_async_copy(gbuf.at[slot], gbuf.at[slot], gsem.at[slot]).wait()

    def keep(n):
        if first:
            return pltpu.make_async_copy(held[n], kept[n], ksem.at[n])
        return pltpu.make_async_copy(kept[n], held[n], ksem.at[n])

    fetch(0, 0)
    if first:
        block = 192

        @pl.loop(0, rows // block)
        def _(r):
            rw = pl.ds(pl.multiple_of(r * block, block), block)
            h = (
                x_ref[rw, :].astype(F32)
                + (pa_ref[rw, :].astype(F32) + pb_ref[rw, :].astype(F32))
                + b_ref[...]
            )
            hidden[rw, :] = h
            hat, _ = normalise(h)
            n2[rw, :] = (hat * g_ref[...] + c_ref[...]).astype(BF)

        pltpu.make_async_copy(hidden, hidden_out, hsem).start()
        keep(0).start()
        n2t[...] = n2[...].T
        keep(1).start()
        got[...] = go_ref[...].T
        keep(2).start()
    else:
        for n in (0, 3, 4, 1, 2):
            keep(n).start()
        keep(0).wait()
    for i in range(n_i):
        slot = i % 2
        if i + 1 < n_i:
            fetch(i + 1, 1 - slot)
        fetched(slot)
        if i == 0 and not first:
            keep(3).wait()
            keep(4).wait()

        @pl.loop(0, 3)
        def _(r, i=i, slot=slot):
            rw = pl.ds(pl.multiple_of(r * rb, rb), rb)
            u, w = wbuf[slot, 0], wbuf[slot, 1]
            up = mm(n2[rw, :], u) + upb_ref[i : i + 1, :]
            act, slope = gelu_parts(up)
            act = act.astype(BF)
            act_s[rw, :] = act
            pre = (mm(go_ref[rw, :], w) * slope).astype(BF)
            pre_s[rw, :] = pre
            down = mm(act, w, NT)
            back = mm(pre, u, NT)
            if i > 0 or not first:
                down += run_b[rw, :]
                back += run_g[rw, :]
            if i < n_i - 1:
                run_b[rw, :] = down
                run_g[rw, :] = back
            else:
                for n, total in enumerate((down, back)):
                    low_sums[n][rw, :] = total.astype(low_sums[n].dtype)
                    pltpu.make_async_copy(low_sums[n].at[rw], sum_outs[n].at[rw], ssem.at[n]).start()

        if i == 0 and not first:
            keep(1).wait()
            keep(2).wait()
        upg_ref[i : i + 1, :] = jnp.sum(pre_s[...].astype(F32), axis=0, keepdims=True)
        if i >= 2:
            stored(slot)
        gbuf[slot, 0] = mm(n2t[...], pre_s[...]).astype(BF)
        gbuf[slot, 1] = mm(got[...], act_s[...]).astype(BF)
        put(i, slot)
    for n in range(2):
        pltpu.make_async_copy(low_sums[n], sum_outs[n], ssem.at[n]).wait()
    if first:
        pltpu.make_async_copy(hidden, hidden_out, hsem).wait()
        for n in range(3):
            keep(n).wait()
    for i in range(max(n_i - 2, 0), n_i):
        stored(i % 2)


def ffn_call(ins, n_j, n_i, fh, parts, arrays, first, absolute):
    go = ins[-3]
    rows, width = go.shape
    wq = width // n_j
    wide, low, turned = (rows, width, F32), (rows, width, BF), (width, rows, BF)
    outs = [wide, low, turned, turned, wide, wide] if first else [low, low]
    grads = grad_shapes(n_j, n_i, absolute, (2, wq, fh))
    if first:
        in_specs = [VMEM_SPEC] * (len(ins) - 1)
    else:
        in_specs = [ANY_SPEC] * 5 + [VMEM_SPEC] * 2
    extra = (
        [pltpu.VMEM((rows, width), F32), pltpu.SemaphoreType.DMA]
        if first
        else [pltpu.VMEM((rows, width), BF)] * 2
    )
    return pl.pallas_call(
        functools.partial(ffn_kernel, parts, n_i, n_j, len(grads), first),
        in_specs=in_specs + [SMEM_SPEC] + [ANY_SPEC] * len(arrays),
        out_specs=[ANY_SPEC] * len(outs) + [VMEM_SPEC] + [ANY_SPEC] * len(grads),
        out_shape=[jax.ShapeDtypeStruct((m, n), kind) for m, n, kind in outs]
        + [jax.ShapeDtypeStruct((n_i, fh), F32)]
        + grads,
        scratch_shapes=[
            pltpu.VMEM((rows, width), BF),
            pltpu.VMEM((width, rows), BF),
            pltpu.VMEM((width, rows), BF),
            pltpu.VMEM((rows, width), F32),
            pltpu.VMEM((rows, width), F32),
            pltpu.VMEM((2, 2, width, fh), BF),
            pltpu.VMEM((2, 2, width, fh), BF),
            pltpu.VMEM((rows, fh), BF),
            pltpu.VMEM((rows, fh), BF),
            pltpu.SemaphoreType.DMA((2,)),
            pltpu.SemaphoreType.DMA((2,)),
            pltpu.SemaphoreType.DMA((5,)),
            pltpu.SemaphoreType.DMA((2,)),
        ]
        + extra,
        compiler_params=pltpu.CompilerParams(vmem_limit_bytes=56 * MIB),
        cost_estimate=pl.CostEstimate(
            flops=12_000_000_000 * n_i, bytes_accessed=30_000_000, transcendentals=1_000_000 * n_i
        ),
        name="ffn_first" if first else "ffn_last",
    )(*ins, *arrays)


def att_back_blocks(meta_ref, qkv_ref, gmix, gq, rows, which):
    he = 2 * HEAD
    images = 3
    slots = rows // images
    lane = lax.broadcasted_iota(jnp.int32, (1, he), 1)
    low_half = lane < HEAD

    @pl.loop(0, images)
    def _(a):
        rw = pl.ds(pl.multiple_of(a * slots, slots), slots)
        bias = jnp.where(valid_slots(meta_ref, a, slots, 0), 0.0, masked_score)
        for i in range(2):
            q2, k2, v2 = (qkv_ref[t * 2 + i, rw, :] for t in range(3))
            g2 = gmix[which + i, rw, :]
            dq, dk, dv = [], [], []
            for h in range(2):
                here = low_half if h == 0 else ~low_half
                qm = jnp.where(here, q2, jnp.zeros_like(q2))
                gm = jnp.where(here, g2, jnp.zeros_like(g2))
                st = mm(k2, qm, NT) * factor + bias
                top = jnp.max(st, axis=0, keepdims=True)
                p = jnp.exp(st - top)
                p = p / jnp.sum(p, axis=0, keepdims=True)
                dpt = mm(v2, gm, NT)
                dot = jnp.sum(p * dpt, axis=0, keepdims=True)
                ds = (p * (dpt - dot)).astype(BF)
                dk.append(mm(ds, q2))
                dv.append(mm(p.astype(BF), g2))
                dq.append(mm(ds, k2, TN))
            for t, (pair, scale) in enumerate(((dq, factor), (dk, factor), (dv, 1.0))):
                both = jnp.where(low_half, pair[0], pair[1])
                gq[rw, (t * 2 + i) * he : (t * 2 + i + 1) * he] = (both * scale).astype(BF)


def put_att_grads(grad_refs, q, n_j, wq, gbuf, gsem, pair):
    he = 2 * HEAD
    for i in range(2):
        block = lambda jj, i=i: [
            gbuf.at[t, block_rows(jj, wq), pl.ds(i * he, he)] for t in range(4)
        ]
        store_blocks(grad_refs, q, n_j, block, i, gsem, pair)


def hidden_back_kernel(
    parts, n_i, n_j, meta_ref, hid_ref, ga_ref, gb_ref, g_ref, go_ref, *rest
):
    w_refs = rest[: len(parts)]
    gh_ref, ght, gmixa, gmixb, sums_ref = rest[len(parts) : len(parts) + 5]
    ghb, w_scr, sem = rest[len(parts) + 5 :]
    rows, width = hid_ref.shape
    he = 2 * HEAD
    place = lambda rws, i, t: w_scr.at[rws, pl.ds(i * he, he)]
    load_blocks(parts, w_refs, meta_ref[4], (3,), width // n_j, range(n_i), place, sem)
    sums_ref[...] = jnp.zeros_like(sums_ref)
    pltpu.make_async_copy(w_scr, w_scr, sem).wait()
    block = 192

    @pl.loop(0, rows // block)
    def _(r):
        rw = pl.ds(pl.multiple_of(r * block, block), block)
        hat, inv = normalise(hid_ref[rw, :])
        grad = ga_ref[rw, :].astype(F32) + gb_ref[rw, :].astype(F32)
        gout = go_ref[rw, :].astype(F32)
        gh = gout + norm_back(hat, inv, g_ref[...], grad)
        gh_ref[rw, :] = gh
        low = gh.astype(BF)
        ghb[rw, :] = low
        sums_ref[0:1, :] += jnp.sum(grad * hat, axis=0, keepdims=True)
        sums_ref[1:2, :] += jnp.sum(grad, axis=0, keepdims=True)
        sums_ref[2:3, :] += jnp.sum(gh, axis=0, keepdims=True)
        sums_ref[3:4, :] += jnp.sum(gout, axis=0, keepdims=True)
        res = mm(low, w_scr[...]).astype(BF)
        for i in range(n_i):
            (gmixa, gmixb)[i // 2][i % 2, rw, :] = res[:, i * he : (i + 1) * he]

    ght[...] = ghb[...].T


def hidden_backward(meta, hidden, ga, gb, gain, go, n_j, parts, arrays):
    rows, width = hidden.shape
    n_i, he = 4, 2 * HEAD
    return pl.pallas_call(
        functools.partial(hidden_back_kernel, parts, n_i, n_j),
        in_specs=[SMEM_SPEC] + [VMEM_SPEC] * 5 + [ANY_SPEC] * len(arrays),
        out_specs=[VMEM_SPEC] * 5,
        out_shape=[
            jax.ShapeDtypeStruct((rows, width), F32),
            jax.ShapeDtypeStruct((width, rows), BF),
            jax.ShapeDtypeStruct((2, rows, he), BF),
            jax.ShapeDtypeStruct((2, rows, he), BF),
            jax.ShapeDtypeStruct((8, width), F32),
        ],
        scratch_shapes=[
            pltpu.VMEM((rows, width), BF),
            pltpu.VMEM((width, n_i * he), BF),
            pltpu.SemaphoreType.DMA,
        ],
        compiler_params=pltpu.CompilerParams(vmem_limit_bytes=48 * MIB),
        cost_estimate=pl.CostEstimate(flops=10_000_000_000, bytes_accessed=20_000_000, transcendentals=0),
        name="hidden_backward",
    )(meta, hidden, ga, gb, gain, go, *arrays)


def att_bwd_first_kernel(n_i, n_j, n_out, meta_ref, gmix, ght, n1_ref, qkv_ref, mix_ref, *rest):
    n1t, gq, bias_ref = rest[:3]
    grad_refs = rest[3 : 3 + n_out]
    gbuf, gsem = rest[3 + n_out :]
    width, rows = ght.shape
    he = 2 * HEAD
    gbuf[3] = mm(ght[...], mix_ref[...]).astype(BF)
    att_back_blocks(meta_ref, qkv_ref, gmix, gq, rows, 0)
    n1t[...] = n1_ref[...].T
    for t in range(3):
        gbuf[t] = mm(n1t[...], gq[:, 2 * t * he : 2 * (t + 1) * he]).astype(BF)
    put_att_grads(grad_refs, meta_ref[4], n_j, width // n_j, gbuf, gsem, 0)
    bias_ref[...] = jnp.sum(gq[...].astype(F32), axis=0, keepdims=True)
    pltpu.make_async_copy(gbuf, gbuf, gsem).wait()


def att_backward_first(meta, gmix, ght, n1, qkv, mix, n_j, absolute):
    width, rows = ght.shape
    n_i, he = 4, 2 * HEAD
    wq = width // n_j
    grads = grad_shapes(n_j, n_i, absolute, (4, wq, he))
    return pl.pallas_call(
        functools.partial(att_bwd_first_kernel, n_i, n_j, len(grads)),
        in_specs=[SMEM_SPEC] + [VMEM_SPEC] * 5,
        out_specs=[VMEM_SPEC] * 3 + [ANY_SPEC] * len(grads),
        out_shape=[
            jax.ShapeDtypeStruct((width, rows), BF),
            jax.ShapeDtypeStruct((rows, 6 * he), BF),
            jax.ShapeDtypeStruct((1, 6 * he), F32),
        ]
        + grads,
        scratch_shapes=[pltpu.VMEM((4, width, 2 * he), BF), pltpu.SemaphoreType.DMA],
        compiler_params=pltpu.CompilerParams(vmem_limit_bytes=60 * MIB),
        cost_estimate=pl.CostEstimate(flops=16_000_000_000, bytes_accessed=20_000_000, transcendentals=1_250_000),
        name="att_backward_first",
    )(meta, gmix, ght, n1, qkv, mix)


def att_bwd_last_kernel(
    parts, n_i, n_j, n_out, meta_ref, x_ref, gmix, ght, n1t, gqa_ref, qkv_ref, mix_ref, *rest
):
    w_refs = rest[: len(parts)]
    rest = rest[len(parts) + n_out :]
    gn1_ref, bias_ref, sums_ref = rest[:3]
    rest = rest[3:]
    grad_refs = rest[:n_out]
    gq, w_scr, gbuf, sem, gsem = rest[n_out:]
    rows, width = x_ref.shape
    he = 2 * HEAD
    wq = width // n_j
    q = meta_ref[4]
    place = lambda rws, i, t: w_scr.at[rws, pl.ds(att_column(n_i, i, t), he)]
    load_blocks(parts, w_refs, q, (0, 1, 2), wq, range(n_i), place, sem)
    gbuf[3] = mm(ght[...], mix_ref[...]).astype(BF)
    att_back_blocks(meta_ref, qkv_ref, gmix, gq, rows, 0)
    for t in range(3):
        gbuf[t] = mm(n1t[...], gq[:, 2 * t * he : 2 * (t + 1) * he]).astype(BF)
    put_att_grads(grad_refs, q, n_j, wq, gbuf, gsem, 1)
    bias_ref[...] = jnp.sum(gq[...].astype(F32), axis=0, keepdims=True)
    sums_ref[...] = jnp.zeros_like(sums_ref)
    pltpu.make_async_copy(w_scr, w_scr, sem).wait()
    rb = rows // 3

    @pl.loop(0, 3)
    def _(r):
        rw = pl.ds(pl.multiple_of(r * rb, rb), rb)
        grad = mm(gqa_ref[rw, :], w_scr[:, : 6 * he], NT) + mm(gq[rw, :], w_scr[:, 6 * he :], NT)
        gn1_ref[rw, :] = grad.astype(BF)
        hat, _ = normalise(x_ref[rw, :].astype(F32))
        sums_ref[0:1, :] += jnp.sum(grad * hat, axis=0, keepdims=True)
        sums_ref[1:2, :] += jnp.sum(grad, axis=0, keepdims=True)

    pltpu.make_async_copy(gbuf, gbuf, gsem).wait()


def att_backward_last(meta, x, gmix, ght, n1t, gqa, qkv, mix, n_j, parts, arrays, first_grads):
    rows, width = x.shape
    n_i, he = 4, 2 * HEAD
    grads = [jax.ShapeDtypeStruct(v.shape, v.dtype) for v in first_grads]
    return pl.pallas_call(
        functools.partial(att_bwd_last_kernel, parts, n_i, n_j, len(grads)),
        in_specs=[SMEM_SPEC] + [VMEM_SPEC] * 7 + [ANY_SPEC] * (len(arrays) + len(grads)),
        out_specs=[VMEM_SPEC] * 3 + [ANY_SPEC] * len(grads),
        out_shape=[
            jax.ShapeDtypeStruct((rows, width), BF),
            jax.ShapeDtypeStruct((1, 6 * he), F32),
            jax.ShapeDtypeStruct((8, width), F32),
        ]
        + grads,
        scratch_shapes=[
            pltpu.VMEM((rows, 6 * he), BF),
            pltpu.VMEM((width, 3 * n_i * he), BF),
            pltpu.VMEM((4, width, 2 * he), BF),
            pltpu.SemaphoreType.DMA,
            pltpu.SemaphoreType.DMA,
        ],
        compiler_params=pltpu.CompilerParams(vmem_limit_bytes=56 * MIB),
        cost_estimate=pl.CostEstimate(flops=20_000_000_000, bytes_accessed=30_000_000, transcendentals=1_250_000),
        input_output_aliases={8 + len(arrays) + n: 3 + n for n in range(len(grads))},
        name="att_backward_last",
    )(meta, x, gmix, ght, n1t, gqa, qkv, mix, *arrays, *first_grads)


def swap(x, axis, bits, what):
    n = lax.axis_size(axis)
    with jax.named_scope(what):
        return lax.ppermute(x, axis, [(i, i ^ bits) for i in range(n)])


def after(x, *deps):
    return lax.optimization_barrier((x,) + deps)[0] if deps else x


def add(*parts):
    total = parts[0].astype(F32)
    for part in parts[1:]:
        total = total + part.astype(F32)
    return total.astype(parts[0].dtype)


def planes():
    n_dp = lax.axis_size("dp")
    return [list(range(core, n_dp, 2)) for core in range(2)]


def gather_plane(block, what):
    with jax.named_scope(what):
        return lax.all_gather(block, "dp", axis_index_groups=planes())


def scatter_plane(blocks, what):
    flat = blocks.reshape(-1, blocks.shape[-1])
    with jax.named_scope(what):
        mine = lax.psum_scatter(
            flat, "dp", scatter_dimension=0, axis_index_groups=planes(), tiled=True
        )
    return mine.reshape(blocks.shape[1:])


def gather_near(own, what):
    return swap(own, "dp", 2, what + "_x1"), swap(own, "dp", 4, what + "_y1")


def gather_far(one, two, what):
    half = one.shape[0] // 2
    return swap(one[:half], "dp", 4, what + "_y2"), swap(two[half:], "dp", 2, what + "_x2")


def scatter_reach(grads, what):
    if len(grads) == 1:
        return (scatter_plane(grads[0], what),)
    _, to_x, to_y, _, _ = grads
    return swap(to_x, "dp", 2, what + "_x1"), swap(to_y, "dp", 4, what + "_y1")


def scatter_last(grads, reach, what):
    if len(grads) == 1:
        return ()
    from_x, from_y = reach
    _, _, _, keep_x, keep_y = grads
    on_x, on_y = add(keep_x, from_y[0::2]), add(keep_y, from_x[0::2])
    return swap(on_x, "dp", 2, what + "_x2"), swap(on_y, "dp", 4, what + "_y2")


def scatter_sum(grads, reach, last):
    if len(grads) == 1:
        return [reach[0][i] for i in range(reach[0].shape[0])]
    own = grads[0]
    return [
        add(own[i], reach[1 - i % 2][i + 1 - i % 2], last[i % 2][i // 2]) for i in range(own.shape[0])
    ]


def gather_z(own, what):
    two = swap(own, "mp", 2, what + "_z2")
    one = swap(own, "mp", 1, what + "_z1")
    return one, two, swap(two, "mp", 1, what + "_z3")


def scatter_z(zero, one, two, three, what):
    two = add(two, swap(three, "mp", 1, what + "_z3"))
    return add(zero, swap(one, "mp", 1, what + "_z1"), swap(two, "mp", 2, what + "_z2"))


def ordered_pair(own, other, core, axis=0):
    return jnp.stack(
        [jnp.where(core == 0, own, other), jnp.where(core == 0, other, own)], axis
    )


def image_routes(n_dp, n_mp, odd):
    pairs = []
    for plane in range(n_dp // 2):
        for core in range(2):
            for z in range(n_mp):
                shift = 2 * core + odd
                worker = (plane * 2 + core) * n_mp + z
                holder = (plane * 2 + (z >> 1)) * n_mp + (z ^ shift)
                pairs.append((holder, worker))
    return pairs


def image_groups(x):
    slots, images, width = x.shape
    return jnp.transpose(x, (1, 0, 2)).reshape(2, images // 2, slots, width)


def for_route(groups, z, odd):
    return lax.dynamic_index_in_dim(groups, (z ^ odd) & 1, 0, False)


def to_image(send, odd, what):
    n_dp, n_mp = lax.axis_size("dp"), lax.axis_size("mp")
    with jax.named_scope(what + "_route" + str(odd)):
        return lax.ppermute(send, ("dp", "mp"), image_routes(n_dp, n_mp, odd))


def from_image(y, z, odd, what):
    n_dp, n_mp = lax.axis_size("dp"), lax.axis_size("mp")
    routes = [(b, a) for a, b in image_routes(n_dp, n_mp, odd)]
    with jax.named_scope(what + "_route" + str(odd)):
        return lax.ppermute(y[:, odd], ("dp", "mp"), routes)


def joined_images(back, z):
    flip = (z & 1) == 1
    groups = jnp.concatenate([jnp.where(flip, back[1], back[0]), jnp.where(flip, back[0], back[1])])
    return jnp.transpose(groups, (1, 0, 2))


def local(
    tokens,
    counts,
    norm_gains,
    norm_shifts,
    qkv_weight,
    qkv_bias,
    proj_weight,
    out_biases,
    up_weight,
    up_bias,
    down_weight,
    cotangent,
):
    slots, images, width = tokens.shape
    n_dp, n_mp = lax.axis_size("dp"), lax.axis_size("mp")
    n_q = n_dp // 2
    wq = width // n_q
    dp, z = lax.axis_index("dp"), lax.axis_index("mp")
    q, core = dp >> 1, dp & 1
    own_images = images // 2
    all_slots = slots * n_mp
    rows = own_images * all_slots

    def rel(v):
        blocks = [lax.dynamic_slice_in_dim(v, (q ^ j) * wq, wq, v.ndim - 1) for j in range(n_q)]
        return jnp.concatenate(blocks, -1)

    def half_of(v, which, axis):
        size = v.shape[axis] // 2
        return lax.dynamic_slice_in_dim(v, which * size, size, axis)

    att = jnp.concatenate([qkv_weight, jnp.transpose(proj_weight)[None]])
    ffn_w = jnp.stack([up_weight, jnp.transpose(down_weight)])
    he, fh = att.shape[-1] // 2, ffn_w.shape[-1] // 2

    count_rows = jnp.pad(counts.astype(BF)[None], ((0, 15), (0, he - images)))
    sent = jnp.concatenate([half_of(att, 1 - core, 2).reshape(-1, he), count_rows])
    got = swap(sent, "dp", 1, "att_w_core")
    other_counts = got[-16, :images].astype(jnp.int32)
    got = got[:-16].reshape(4, wq // 2, he)
    att_own = ordered_pair(half_of(att, core, 2), got, core, 1).reshape(-1, he)
    got = swap(half_of(ffn_w, 1 - core, 2), "dp", 1, "ffn_w_core")
    ffn_own = ordered_pair(half_of(ffn_w, core, 2), got, core, 1).reshape(2, wq, fh)
    left = jnp.concatenate(
        [half_of(qkv_bias, core, 1), half_of(up_bias, core, 0).reshape(-1, he)]
    )
    n_bias = left.shape[0]
    terms = []
    for _ in range(3):
        term = lax.reduce_precision(left, 8, 7)
        terms.append(term.astype(BF))
        left = left - term
    bias_pad = -(-3 * n_bias // 16) * 16
    bias_terms = jnp.pad(jnp.concatenate(terms), ((0, bias_pad - 3 * n_bias), (0, 0)))

    counts_here = jnp.where((z >> 1) == core, counts, other_counts)
    counts_here = lax.dynamic_slice_in_dim(counts_here, (z & 1) * own_images, own_images, 0)
    meta = jnp.concatenate([counts_here, z[None], q[None]])
    slot_ids = jnp.arange(slots, dtype=jnp.int32)
    keep_mine = ((z * slots + slot_ids)[:, None] < BUF + counts[None, :])[:, :, None]

    def whole_rows(got, what):
        return ordered_pair(got, swap(got, "dp", 1, what), core, 1).reshape(rows, width)

    n_i = n_mp
    gains, shifts, out_b = rel(norm_gains), rel(norm_shifts), rel(out_biases)
    square = n_q == 4
    pair_places = [(j, i, 0, 2, False) for j, i in ((0, 0), (1, 0), (2, 0), (3, 0), (3, 1))]
    both = lax.optimization_barrier

    def flat(v):
        return v.reshape(v.shape[:-3] + (-1, v.shape[-1]))

    row_half = lambda v, which: half_of(v.reshape(own_images, n_mp, slots, width), which, 1)

    att_mine = jnp.concatenate([att_own, bias_terms])
    two = swap(att_mine, "mp", 2, "att_w_z2")
    one = swap(att_mine, "mp", 1, "att_w_z1")
    token_groups = image_groups(rel(tokens))
    sends = [for_route(token_groups, z, odd) for odd in (0, 1)]
    one, two, sends, ffn_own = both((one, two, sends, ffn_own))
    three = swap(two, "mp", 1, "att_w_z3")
    token_rows = [to_image(sends[odd], odd, "tokens") for odd in (0, 1)]
    att_z = jnp.stack([att_mine, one, two, three])
    bias_all = att_z[:, 4 * wq : 4 * wq + 3 * n_bias].astype(F32).reshape(n_i, 3, n_bias, he)
    bias_all = bias_all[:, 0] + (bias_all[:, 1] + bias_all[:, 2])
    bias_three = jnp.stack([bias_all[:, 0], jnp.zeros((n_i, he), F32), bias_all[:, 1]])
    bias_rows = jnp.transpose(bias_three.reshape(3, 2, 2, he), (1, 0, 2, 3)).reshape(1, -1)
    att_near = gather_near(att_z, "att_w") if square else ()
    cot = rel(jnp.where(keep_mine, cotangent, jnp.zeros_like(cotangent)))
    one = swap(ffn_own, "mp", 1, "ffn_w_z1")
    two = swap(after(ffn_own, *token_rows), "mp", 2, "ffn_w_z2")
    token_rows, att_near, bias_rows = both((token_rows, att_near, bias_rows))

    if square:
        att_far = gather_far(*att_near, "att_w")
        att_places = [(j, i, 0, 4, False) for j, i in ((0, 0), (1, 0), (2, 0), (3, 0), (3, 2))]
    else:
        att_far, att_places = (gather_plane(att_z, "att_w"),), [(0, 0, 0, 4, True)]
    x = whole_rows(jnp.stack(token_rows, 1), "tokens_core")
    cot_groups = image_groups(cot)
    sends = [for_route(cot_groups, z, odd) for odd in (0, 1)]
    x, att_far, one, two, ffn_own, sends = both((x, att_far, one, two, ffn_own, sends))
    att_parts = [v[None] for v in (att_z, *att_near, *att_far)] if square else list(att_far)
    three = swap(two, "mp", 1, "ffn_w_z3")
    ffn_here = flat(jnp.stack([ffn_own, one]))
    x, ffn_here = both((x, ffn_here))
    here_near = gather_near(ffn_here, "ffn_w0") if square else ()
    cot_rows = [to_image(sends[odd], odd, "cotangent") for odd in (0, 1)]
    n1, qkva, qkvb, mixa, mixb, part = att_forward(
        x.reshape(own_images, all_slots, width),
        gains[0:1],
        shifts[0:1],
        bias_rows,
        meta,
        att_places,
        att_parts,
    )
    part, two, three, n1, x, here_near = both((part, two, three, n1, x, here_near))

    part_other = swap(part, "dp", 1, "attended")
    ffn_far = flat(jnp.stack([two, three]))
    far_near = gather_near(ffn_far, "ffn_w2") if square else ()
    far_near, cot_rows, part_other, here_near = both((far_near, cot_rows, part_other, here_near))
    if square:
        far_far = gather_far(*far_near, "ffn_w2")
        parts0 = [v[None] for v in (ffn_far, *far_near, *far_far)]
        places = pair_places
    else:
        parts0, places = [gather_plane(ffn_far, "ffn_w2")], [(0, 0, 0, 2, True)]
    go = whole_rows(jnp.stack(cot_rows, 1), "cotangent_core")
    go, parts0, here_near = both((go, parts0, here_near))
    here_far = gather_far(*here_near, "ffn_w0") if square else ()
    up_rows = bias_all[:, 2:].reshape(n_i, fh)
    hidden, n2, n2t, got, sum_b, sum_g, upg1, *ffn_g0 = ffn_call(
        [x, part, part_other, out_b[0:1], gains[1:2], shifts[1:2], go, up_rows[2:], meta],
        n_q,
        2,
        fh,
        places,
        parts0,
        True,
        not square,
    )
    n2, ffn_g0, here_far = both((n2, ffn_g0, here_far))
    if square:
        parts1 = [v[None] for v in (ffn_here, *here_near, *here_far)]
    else:
        parts1 = [gather_plane(ffn_here, "ffn_w0")]
    reach_f0 = scatter_reach(ffn_g0, "ffn_g0")
    branch, gn2, upg0, *ffn_g1 = ffn_call(
        [n2, n2t, got, sum_b, sum_g, go, up_rows[:2], meta],
        n_q,
        2,
        fh,
        places,
        parts1,
        False,
        not square,
    )
    branch, gn2, ffn_g1, reach_f0 = both((branch, gn2, ffn_g1, reach_f0))

    last_f0 = scatter_last(ffn_g0, reach_f0, "ffn_g0")
    reach_f1 = scatter_reach(ffn_g1, "ffn_g1")
    gn2_other = swap(gn2, "dp", 1, "grad_norm_two")
    theirs = swap(row_half(branch, 1 - core), "dp", 1, "branch")
    gn2_other, theirs = both((gn2_other, theirs))
    out_half = row_half(hidden, core) + row_half(branch, core).astype(F32) + theirs.astype(F32) + out_b[1]
    gn2_other, out_half = both((gn2_other, rel(out_half.astype(BF))))
    out_first = from_image(out_half, z, 0, "block_out")
    gh, ght, gmixa, gmixb, sums = hidden_backward(
        meta, hidden, gn2, gn2_other, gains[1:2], go, n_q, att_places, att_parts
    )
    gmixa, last_f0, out_first, out_half = both((gmixa, last_f0, out_first, out_half))
    ffn2, ffn3 = scatter_sum(ffn_g0, reach_f0, last_f0)
    ffn_three = swap(ffn3, "mp", 1, "ffn_g_z3")
    out_last = from_image(out_half, z, 1, "block_out")
    gmixa, ffn2 = both((gmixa, ffn2))
    n1t, gqa, bias_a, *att_g = att_backward_first(
        meta, gmixa, ght, n1, qkva, mixa, n_q, not square
    )
    n1t, gqa, reach_f1, ffn_three, out_last = both((n1t, gqa, reach_f1, ffn_three, out_last))
    last_f1 = scatter_last(ffn_g1, reach_f1, "ffn_g1")
    ffn_two = swap(add(ffn2, ffn_three), "mp", 2, "ffn_g_z2")
    gn1, bias_b, more_sums, *att_g = att_backward_last(
        meta, x, gmixb, ght, n1t, gqa, qkvb, mixb, n_q, att_places, att_parts, att_g
    )
    gn1, last_f1, att_g, x, ffn_two = both((gn1, last_f1, att_g, x, ffn_two))

    ffn0, ffn1 = scatter_sum(ffn_g1, reach_f1, last_f1)
    ffn_one = swap(ffn1, "mp", 1, "ffn_g_z1")
    gn1_other = swap(after(row_half(gn1, 1 - core), ffn1), "dp", 1, "grad_norm_one")
    reach_a = scatter_reach(att_g, "att_g")
    gn1 = row_half(gn1, core).astype(F32) + gn1_other.astype(F32)
    hat1, inv1 = normalise(after(row_half(x, core), gn1_other).astype(F32))
    input_half = row_half(gh, core) + norm_back(hat1, inv1, gains[0], gn1)
    input_half = rel(input_half.astype(BF))
    in_first = from_image(input_half, z, 0, "input_grad")
    reach_a, ffn_one, in_first, input_half, upg0, upg1, bias_a, bias_b, sums, more_sums = both(
        (reach_a, ffn_one, in_first, input_half, upg0, upg1, bias_a, bias_b, sums, more_sums)
    )
    in_last = from_image(input_half, z, 1, "input_grad")
    last_a = scatter_last(att_g, reach_a, "att_g")

    def placed(values):
        mine = jnp.concatenate([lax.dynamic_slice_in_dim(values, z ^ i, 1, 0) for i in range(n_i)])
        return jnp.stack([jnp.where(core == c, mine, jnp.zeros_like(mine)) for c in range(2)], 1)

    bias_a, bias_b = (v.reshape(3, 2, he) for v in (bias_a, bias_b))
    wide = [placed(jnp.concatenate([bias_a[t], bias_b[t]])) for t in (0, 2)]
    wide.append(placed(jnp.concatenate([upg0, upg1])))
    values = [*wide, rel(sums), rel(more_sums)]
    vector = jnp.concatenate([v.reshape(-1, 128) for v in values])
    vector = vector + swap(vector, "dp", 1, "sums_core")
    last_a, vector = both((last_a, vector))
    att0, att1, att2, att3 = scatter_sum(att_g, reach_a, last_a)
    att_three = swap(att3, "mp", 1, "att_g_z3")
    att_one = swap(att1, "mp", 1, "att_g_z1")
    vector = vector + swap(vector, "dp", 2, "sums_dp2")
    att_three, vector = both((att_three, vector))
    att_two = swap(add(att2, att_three), "mp", 2, "att_g_z2")
    bit = 4
    while bit < n_dp:
        vector = vector + swap(vector, "dp", bit, "sums_dp" + str(bit))
        bit *= 2
    for bit in (1, 2):
        vector = vector + swap(vector, "mp", bit, "sums_z" + str(bit))
    att_grad = add(att0, att_one, att_two)
    ffn_grad = add(ffn0, ffn_one, ffn_two)
    in_routes = [in_first, in_last]
    block_out = joined_images([out_first, out_last], z)
    block_out = jnp.where(keep_mine, block_out, jnp.zeros_like(block_out))
    input_grad = joined_images(in_routes, z)

    def own_shard(grad, what):
        kinds, _, last = grad.shape
        pair = grad.reshape(kinds, 2, wq // 2, last)
        keep = lax.dynamic_index_in_dim(pair, core, 1, False)
        got = swap(lax.dynamic_index_in_dim(pair, 1 - core, 1, False), "dp", 1, what)
        return ordered_pair(keep, got, core, 2).reshape(kinds, wq // 2, 2 * last).astype(F32)

    att_shard, ffn_shard = own_shard(att_grad, "att_g_core"), own_shard(ffn_grad, "ffn_g_core")
    qkv_owned, proj_owned = att_shard[:3], jnp.transpose(att_shard[3])
    up_owned, down_owned = ffn_shard[0], jnp.transpose(ffn_shard[1])

    ends = [0]
    for v in values:
        ends.append(ends[-1] + v.size // 128)
    *wide, sums, more_sums = [
        vector[start:end].reshape(v.shape) for v, start, end in zip(values, ends, ends[1:])
    ]
    wide = [lax.dynamic_index_in_dim(v, z, 0, False).reshape(-1) for v in wide]
    bias_grad, upbias_grad = jnp.stack(wide[:2]), wide[2]
    gains_grad = jnp.stack([more_sums[0], sums[0] * 0.5])
    shifts_grad = jnp.stack([more_sums[1], sums[1] * 0.5])
    outbias_grad = sums[2:4] * 0.5
    return (
        block_out,
        input_grad,
        gains_grad,
        shifts_grad,
        qkv_owned,
        bias_grad,
        proj_owned,
        outbias_grad,
        up_owned,
        upbias_grad,
        down_owned,
    )


def solution(mesh):
    split = P("mp", "dp", None)
    return jax.shard_map(
        local,
        mesh=mesh,
        in_specs=(
            split,
            P("dp"),
            P(),
            P(),
            P(None, "dp", "mp"),
            P(None, "mp"),
            P("mp", "dp"),
            P(),
            P("dp", "mp"),
            P("mp"),
            P("mp", "dp"),
            split,
        ),
        out_specs=(
            split,
            split,
            P(),
            P(),
            P(None, "dp", "mp"),
            P(None, "mp"),
            P("mp", "dp"),
            P(),
            P("dp", "mp"),
            P("mp"),
            P("mp", "dp"),
        ),
        check_vma=False,
    )
```

```python
import functools

import jax
import jax.numpy as jnp
from jax import lax
from jax.experimental import pallas as pl
from jax.experimental.pallas import tpu as pltpu
from jax.sharding import PartitionSpec as P

HEAD = 64
BUF = 64
BF = jnp.bfloat16
F32 = jnp.float32
epsilon = 1e-06
masked_score = -1e30
MIB = 1 << 20
NT = (((1,), (1,)), ((), ()))
NN = (((1,), (0,)), ((), ()))
TN = (((0,), (0,)), ((), ()))
factor = HEAD ** (-0.5)
VMEM_SPEC = pl.BlockSpec(memory_space=pltpu.VMEM)
ANY_SPEC = pl.BlockSpec(memory_space=pl.ANY)
SMEM_SPEC = pl.BlockSpec(memory_space=pltpu.SMEM)


def mm(a, b, dims=NN):
    return lax.dot_general(a, b, dims, preferred_element_type=F32)


def normalise(values):
    average = jnp.mean(values, axis=-1, keepdims=True)
    centred = values - average
    spread = jnp.mean(centred * centred, axis=-1, keepdims=True)
    inv = lax.rsqrt(spread + epsilon)
    return centred * inv, inv


def norm_back(n, inv, scales, grad):
    e = grad * scales
    mean_e = jnp.mean(e, axis=-1, keepdims=True)
    mean_en = jnp.mean(e * n, axis=-1, keepdims=True)
    return (e - mean_e - n * mean_en) * inv


def gelu_parts(inputs):
    normal_cdf = 0.5 + 0.5 * lax.erf(inputs * 0.7071067811865476)
    density = jnp.exp(-0.5 * inputs * inputs) * 0.3989422804014327
    return inputs * normal_cdf, normal_cdf + inputs * density


def for_each(count, step):
    if count <= 4:
        for index in range(count):
            step(index)
    else:
        pl.loop(0, count)(step)


def valid_slots(meta_ref, image, slots, axis):
    shape = (slots, 1) if axis == 0 else (1, slots)
    row = lax.broadcasted_iota(jnp.int32, shape, axis)
    n = slots // 4
    k = (row >= n).astype(jnp.int32) + (row >= 2 * n) + (row >= 3 * n)
    slot = (k ^ meta_ref[3]) * n + (row - k * n)
    return slot < BUF + meta_ref[image]


def block_rows(jj, size):
    start = jj * size
    return pl.ds(start if isinstance(jj, int) else pl.multiple_of(start, size), size)


def load_blocks(parts, refs, q, kinds, wq, wanted, place, sem):
    for (j0, i0, t0, count, absolute), ref in zip(parts, refs):
        nj, ni = ref.shape[:2]

        def one(jj, ref=ref, j0=j0, i0=i0, t0=t0, count=count, absolute=absolute, ni=ni):
            source = jj ^ q if absolute else jj
            for ii in range(ni):
                if i0 + ii not in wanted:
                    continue
                for t in range(t0, t0 + count):
                    if t in kinds:
                        pltpu.make_async_copy(
                            ref.at[source, ii, pl.ds((t - t0) * wq, wq)],
                            place(block_rows(j0 + jj, wq), i0 + ii, t),
                            sem,
                        ).start()

        for_each(nj, one)


def store_blocks(refs, q, n_j, block, i, sem, pair=0):
    def start(views, target):
        for t, view in enumerate(views):
            pltpu.make_async_copy(view, target.at[t], sem).start()

    if len(refs) == 1:
        for_each(n_j, lambda jj: start(block(jj), refs[0].at[jj ^ q, 2 * pair + i]))
        return
    own, to_x, to_y, keep_x, keep_y = refs
    start(block(0), own.at[2 * pair + i])
    if i == 0:
        start(block(1), keep_x.at[pair])
        start(block(2), to_y.at[2 * pair + 1])
        start(block(3), to_y.at[2 * pair])
    else:
        start(block(1), to_x.at[2 * pair + 1])
        start(block(2), keep_y.at[pair])
        start(block(3), to_x.at[2 * pair])


def grad_shapes(n_j, n_i, absolute, block):
    shape = lambda *lead: jax.ShapeDtypeStruct(lead + block, BF)
    if absolute:
        return [shape(n_j, n_i)]
    return [shape(n_i), shape(n_i), shape(n_i), shape(n_i // 2), shape(n_i // 2)]


def att_column(n_i, i, t):
    he = 2 * HEAD
    if t == 3:
        return 3 * n_i * he + i * he
    return (i // 2) * 6 * he + (t * 2 + i % 2) * he


def att_fwd_kernel(parts, n_i, x_ref, g_ref, c_ref, bias_ref, meta_ref, *rest):
    w_refs = rest[: len(parts)]
    n1_ref, qkva_ref, qkvb_ref, mixa_ref, mixb_ref, part_ref, w_scr, m_scr, sem = rest[len(parts) :]
    he = 2 * HEAD
    width = w_scr.shape[0]
    image = pl.program_id(0)

    @pl.when(image == 0)
    def _():
        place = lambda rows, i, t: w_scr.at[rows, pl.ds(att_column(n_i, i, t), he)]
        wq = width // max(p[0] + r.shape[0] for p, r in zip(parts, w_refs))
        load_blocks(parts, w_refs, meta_ref[4], range(4), wq, range(n_i), place, sem)
        pltpu.make_async_copy(w_scr, w_scr, sem).wait()

    hat, _ = normalise(x_ref[0].astype(F32))
    n1 = (hat * g_ref[...] + c_ref[...]).astype(BF)
    n1_ref[...] = n1
    qkv_refs = (qkva_ref, qkvb_ref)
    for half in range(2):
        cols = pl.ds(half * 6 * he, 6 * he)
        res = (mm(n1, w_scr[:, cols]) + bias_ref[:, cols]).astype(BF)
        for n in range(6):
            qkv_refs[half][n] = res[:, n * he : (n + 1) * he]
    bias = jnp.where(valid_slots(meta_ref, image, x_ref.shape[1], 1), 0.0, masked_score)
    lane = lax.broadcasted_iota(jnp.int32, (1, he), 1)
    low_half = lane < HEAD
    for i in range(n_i):
        ref = qkv_refs[i // 2]
        q2, k2, v2 = (ref[t * 2 + i % 2] for t in range(3))
        outs = []
        for h in range(2):
            qm = jnp.where(low_half if h == 0 else ~low_half, q2, jnp.zeros_like(q2))
            s = mm(qm, k2, NT) * factor + bias
            top = jnp.max(s, axis=-1, keepdims=True)
            p = jnp.exp(s - top)
            w = (p / jnp.sum(p, axis=-1, keepdims=True)).astype(BF)
            outs.append(mm(w, v2))
        mixed = jnp.where(low_half, outs[0], outs[1]).astype(BF)
        m_scr[:, i * he : (i + 1) * he] = mixed
    mixa_ref[...] = m_scr[:, : 2 * he]
    mixb_ref[...] = m_scr[:, 2 * he :]
    part_ref[...] = mm(m_scr[...], w_scr[:, 3 * n_i * he :], NT).astype(BF)


def att_forward(x, gain, shift, bias, meta, parts, arrays):
    images, slots, width = x.shape
    n_i = 4
    he = 2 * HEAD
    rows = images * slots
    row_block = lambda last: pl.BlockSpec((slots, last), lambda a: (a, 0))
    whole = lambda *shape: pl.BlockSpec(shape, lambda a: (0,) * len(shape))
    qkv_block = pl.BlockSpec((6, slots, he), lambda a: (0, a, 0))
    return pl.pallas_call(
        functools.partial(att_fwd_kernel, parts, n_i),
        grid=(images,),
        in_specs=[
            pl.BlockSpec((1, slots, width), lambda a: (a, 0, 0)),
            whole(1, width),
            whole(1, width),
            whole(1, 3 * n_i * he),
            SMEM_SPEC,
        ]
        + [ANY_SPEC] * len(arrays),
        out_specs=[row_block(width), qkv_block, qkv_block, row_block(2 * he), row_block(2 * he), row_block(width)],
        out_shape=[
            jax.ShapeDtypeStruct((rows, width), BF),
            jax.ShapeDtypeStruct((6, rows, he), BF),
            jax.ShapeDtypeStruct((6, rows, he), BF),
            jax.ShapeDtypeStruct((rows, 2 * he), BF),
            jax.ShapeDtypeStruct((rows, 2 * he), BF),
            jax.ShapeDtypeStruct((rows, width), BF),
        ],
        scratch_shapes=[
            pltpu.VMEM((width, 4 * n_i * he), BF),
            pltpu.VMEM((slots, n_i * he), BF),
            pltpu.SemaphoreType.DMA,
        ],
        compiler_params=pltpu.CompilerParams(vmem_limit_bytes=48 * MIB),
        cost_estimate=pl.CostEstimate(flops=16_000_000_000, bytes_accessed=20_000_000, transcendentals=2_500_000),
        name="att_forward",
    )(x, gain, shift, bias, meta, *arrays)


def ffn_kernel(parts, n_i, n_j, n_out, first, *refs):
    if first:
        x_ref, pa_ref, pb_ref, b_ref, g_ref, c_ref = refs[:6]
        refs = refs[6:]
    else:
        kept, refs = refs[:5], refs[5:]
    go_ref, upb_ref, meta_ref = refs[:3]
    w_refs, refs = refs[3 : 3 + len(parts)], refs[3 + len(parts) :]
    q = meta_ref[4]
    if first:
        hidden_out, refs = refs[0], refs[1:]
        kept, refs = refs[:5], refs[5:]
        sum_outs = kept[3:]
    else:
        sum_outs, refs = refs[:2], refs[2:]
    upg_ref, refs = refs[0], refs[1:]
    grad_refs, refs = refs[:n_out], refs[n_out:]
    n2, n2t, got, run_b, run_g, wbuf, gbuf, act_s, pre_s, wsem, gsem, ksem, ssem = refs[:13]
    held = (n2, n2t, got, run_b, run_g)
    if first:
        hidden, hsem = refs[13:]
        low_sums = (run_b, run_g)
    else:
        low_sums = refs[13:]
    rows, width = go_ref.shape
    wq = width // n_j
    rb = rows // 3

    def fetch(i, slot):
        place = lambda rws, _, t: wbuf.at[slot, t, rws]
        load_blocks(parts, w_refs, q, range(2), wq, (i,), place, wsem.at[slot])

    def fetched(slot):
        pltpu.make_async_copy(wbuf.at[slot], wbuf.at[slot], wsem.at[slot]).wait()

    def put(i, slot):
        block = lambda jj: [gbuf.at[slot, t, block_rows(jj, wq)] for t in range(2)]
        store_blocks(grad_refs, q, n_j, block, i, gsem.at[slot])

    def stored(slot):
        pltpu.make_async_copy(gbuf.at[slot], gbuf.at[slot], gsem.at[slot]).wait()

    def keep(n):
        if first:
            return pltpu.make_async_copy(held[n], kept[n], ksem.at[n])
        return pltpu.make_async_copy(kept[n], held[n], ksem.at[n])

    fetch(0, 0)
    if first:
        block = 192

        @pl.loop(0, rows // block)
        def _(r):
            rw = pl.ds(pl.multiple_of(r * block, block), block)
            h = (
                x_ref[rw, :].astype(F32)
                + (pa_ref[rw, :].astype(F32) + pb_ref[rw, :].astype(F32))
                + b_ref[...]
            )
            hidden[rw, :] = h
            hat, _ = normalise(h)
            n2[rw, :] = (hat * g_ref[...] + c_ref[...]).astype(BF)

        pltpu.make_async_copy(hidden, hidden_out, hsem).start()
        keep(0).start()
        n2t[...] = n2[...].T
        keep(1).start()
        got[...] = go_ref[...].T
        keep(2).start()
    else:
        for n in (0, 3, 4, 1, 2):
            keep(n).start()
        keep(0).wait()
    for i in range(n_i):
        slot = i % 2
        if i + 1 < n_i:
            fetch(i + 1, 1 - slot)
        fetched(slot)
        if i == 0 and not first:
            keep(3).wait()
            keep(4).wait()

        @pl.loop(0, 3)
        def _(r, i=i, slot=slot):
            rw = pl.ds(pl.multiple_of(r * rb, rb), rb)
            u, w = wbuf[slot, 0], wbuf[slot, 1]
            up = mm(n2[rw, :], u) + upb_ref[i : i + 1, :]
            act, slope = gelu_parts(up)
            act = act.astype(BF)
            act_s[rw, :] = act
            pre = (mm(go_ref[rw, :], w) * slope).astype(BF)
            pre_s[rw, :] = pre
            down = mm(act, w, NT)
            back = mm(pre, u, NT)
            if i > 0 or not first:
                down += run_b[rw, :]
                back += run_g[rw, :]
            if i < n_i - 1:
                run_b[rw, :] = down
                run_g[rw, :] = back
            else:
                for n, total in enumerate((down, back)):
                    low_sums[n][rw, :] = total.astype(low_sums[n].dtype)
                    pltpu.make_async_copy(low_sums[n].at[rw], sum_outs[n].at[rw], ssem.at[n]).start()

        if i == 0 and not first:
            keep(1).wait()
            keep(2).wait()
        upg_ref[i : i + 1, :] = jnp.sum(pre_s[...].astype(F32), axis=0, keepdims=True)
        if i >= 2:
            stored(slot)
        gbuf[slot, 0] = mm(n2t[...], pre_s[...]).astype(BF)
        gbuf[slot, 1] = mm(got[...], act_s[...]).astype(BF)
        put(i, slot)
    for n in range(2):
        pltpu.make_async_copy(low_sums[n], sum_outs[n], ssem.at[n]).wait()
    if first:
        pltpu.make_async_copy(hidden, hidden_out, hsem).wait()
        for n in range(3):
            keep(n).wait()
    for i in range(max(n_i - 2, 0), n_i):
        stored(i % 2)


def ffn_call(ins, n_j, n_i, fh, parts, arrays, first, absolute):
    go = ins[-3]
    rows, width = go.shape
    wq = width // n_j
    wide, low, turned = (rows, width, F32), (rows, width, BF), (width, rows, BF)
    outs = [wide, low, turned, turned, wide, wide] if first else [low, low]
    grads = grad_shapes(n_j, n_i, absolute, (2, wq, fh))
    if first:
        in_specs = [VMEM_SPEC] * (len(ins) - 1)
    else:
        in_specs = [ANY_SPEC] * 5 + [VMEM_SPEC] * 2
    extra = (
        [pltpu.VMEM((rows, width), F32), pltpu.SemaphoreType.DMA]
        if first
        else [pltpu.VMEM((rows, width), BF)] * 2
    )
    return pl.pallas_call(
        functools.partial(ffn_kernel, parts, n_i, n_j, len(grads), first),
        in_specs=in_specs + [SMEM_SPEC] + [ANY_SPEC] * len(arrays),
        out_specs=[ANY_SPEC] * len(outs) + [VMEM_SPEC] + [ANY_SPEC] * len(grads),
        out_shape=[jax.ShapeDtypeStruct((m, n), kind) for m, n, kind in outs]
        + [jax.ShapeDtypeStruct((n_i, fh), F32)]
        + grads,
        scratch_shapes=[
            pltpu.VMEM((rows, width), BF),
            pltpu.VMEM((width, rows), BF),
            pltpu.VMEM((width, rows), BF),
            pltpu.VMEM((rows, width), F32),
            pltpu.VMEM((rows, width), F32),
            pltpu.VMEM((2, 2, width, fh), BF),
            pltpu.VMEM((2, 2, width, fh), BF),
            pltpu.VMEM((rows, fh), BF),
            pltpu.VMEM((rows, fh), BF),
            pltpu.SemaphoreType.DMA((2,)),
            pltpu.SemaphoreType.DMA((2,)),
            pltpu.SemaphoreType.DMA((5,)),
            pltpu.SemaphoreType.DMA((2,)),
        ]
        + extra,
        compiler_params=pltpu.CompilerParams(vmem_limit_bytes=56 * MIB),
        cost_estimate=pl.CostEstimate(
            flops=12_000_000_000 * n_i, bytes_accessed=30_000_000, transcendentals=1_000_000 * n_i
        ),
        name="ffn_first" if first else "ffn_last",
    )(*ins, *arrays)


def att_back_blocks(meta_ref, qkv_ref, gmix, gq, rows, which):
    he = 2 * HEAD
    images = 3
    slots = rows // images
    lane = lax.broadcasted_iota(jnp.int32, (1, he), 1)
    low_half = lane < HEAD

    @pl.loop(0, images)
    def _(a):
        rw = pl.ds(pl.multiple_of(a * slots, slots), slots)
        bias = jnp.where(valid_slots(meta_ref, a, slots, 0), 0.0, masked_score)
        for i in range(2):
            q2, k2, v2 = (qkv_ref[t * 2 + i, rw, :] for t in range(3))
            g2 = gmix[which + i, rw, :]
            dq, dk, dv = [], [], []
            for h in range(2):
                here = low_half if h == 0 else ~low_half
                qm = jnp.where(here, q2, jnp.zeros_like(q2))
                gm = jnp.where(here, g2, jnp.zeros_like(g2))
                st = mm(k2, qm, NT) * factor + bias
                top = jnp.max(st, axis=0, keepdims=True)
                p = jnp.exp(st - top)
                p = p / jnp.sum(p, axis=0, keepdims=True)
                dpt = mm(v2, gm, NT)
                dot = jnp.sum(p * dpt, axis=0, keepdims=True)
                ds = (p * (dpt - dot)).astype(BF)
                dk.append(mm(ds, q2))
                dv.append(mm(p.astype(BF), g2))
                dq.append(mm(ds, k2, TN))
            for t, (pair, scale) in enumerate(((dq, factor), (dk, factor), (dv, 1.0))):
                both = jnp.where(low_half, pair[0], pair[1])
                gq[rw, (t * 2 + i) * he : (t * 2 + i + 1) * he] = (both * scale).astype(BF)


def put_att_grads(grad_refs, q, n_j, wq, gbuf, gsem, pair):
    he = 2 * HEAD
    for i in range(2):
        block = lambda jj, i=i: [
            gbuf.at[t, block_rows(jj, wq), pl.ds(i * he, he)] for t in range(4)
        ]
        store_blocks(grad_refs, q, n_j, block, i, gsem, pair)


def hidden_back_kernel(
    parts, n_i, n_j, meta_ref, hid_ref, ga_ref, gb_ref, g_ref, go_ref, *rest
):
    w_refs = rest[: len(parts)]
    gh_ref, ght, gmixa, gmixb, sums_ref = rest[len(parts) : len(parts) + 5]
    ghb, w_scr, sem = rest[len(parts) + 5 :]
    rows, width = hid_ref.shape
    he = 2 * HEAD
    place = lambda rws, i, t: w_scr.at[rws, pl.ds(i * he, he)]
    load_blocks(parts, w_refs, meta_ref[4], (3,), width // n_j, range(n_i), place, sem)
    sums_ref[...] = jnp.zeros_like(sums_ref)
    pltpu.make_async_copy(w_scr, w_scr, sem).wait()
    block = 192

    @pl.loop(0, rows // block)
    def _(r):
        rw = pl.ds(pl.multiple_of(r * block, block), block)
        hat, inv = normalise(hid_ref[rw, :])
        grad = ga_ref[rw, :].astype(F32) + gb_ref[rw, :].astype(F32)
        gout = go_ref[rw, :].astype(F32)
        gh = gout + norm_back(hat, inv, g_ref[...], grad)
        gh_ref[rw, :] = gh
        low = gh.astype(BF)
        ghb[rw, :] = low
        sums_ref[0:1, :] += jnp.sum(grad * hat, axis=0, keepdims=True)
        sums_ref[1:2, :] += jnp.sum(grad, axis=0, keepdims=True)
        sums_ref[2:3, :] += jnp.sum(gh, axis=0, keepdims=True)
        sums_ref[3:4, :] += jnp.sum(gout, axis=0, keepdims=True)
        res = mm(low, w_scr[...]).astype(BF)
        for i in range(n_i):
            (gmixa, gmixb)[i // 2][i % 2, rw, :] = res[:, i * he : (i + 1) * he]

    ght[...] = ghb[...].T


def hidden_backward(meta, hidden, ga, gb, gain, go, n_j, parts, arrays):
    rows, width = hidden.shape
    n_i, he = 4, 2 * HEAD
    return pl.pallas_call(
        functools.partial(hidden_back_kernel, parts, n_i, n_j),
        in_specs=[SMEM_SPEC] + [VMEM_SPEC] * 5 + [ANY_SPEC] * len(arrays),
        out_specs=[VMEM_SPEC] * 5,
        out_shape=[
            jax.ShapeDtypeStruct((rows, width), F32),
            jax.ShapeDtypeStruct((width, rows), BF),
            jax.ShapeDtypeStruct((2, rows, he), BF),
            jax.ShapeDtypeStruct((2, rows, he), BF),
            jax.ShapeDtypeStruct((8, width), F32),
        ],
        scratch_shapes=[
            pltpu.VMEM((rows, width), BF),
            pltpu.VMEM((width, n_i * he), BF),
            pltpu.SemaphoreType.DMA,
        ],
        compiler_params=pltpu.CompilerParams(vmem_limit_bytes=48 * MIB),
        cost_estimate=pl.CostEstimate(flops=10_000_000_000, bytes_accessed=20_000_000, transcendentals=0),
        name="hidden_backward",
    )(meta, hidden, ga, gb, gain, go, *arrays)


def att_bwd_first_kernel(n_i, n_j, n_out, meta_ref, gmix, ght, n1_ref, qkv_ref, mix_ref, *rest):
    n1t, gq, bias_ref = rest[:3]
    grad_refs = rest[3 : 3 + n_out]
    gbuf, gsem = rest[3 + n_out :]
    width, rows = ght.shape
    he = 2 * HEAD
    gbuf[3] = mm(ght[...], mix_ref[...]).astype(BF)
    att_back_blocks(meta_ref, qkv_ref, gmix, gq, rows, 0)
    n1t[...] = n1_ref[...].T
    for t in range(3):
        gbuf[t] = mm(n1t[...], gq[:, 2 * t * he : 2 * (t + 1) * he]).astype(BF)
    put_att_grads(grad_refs, meta_ref[4], n_j, width // n_j, gbuf, gsem, 0)
    bias_ref[...] = jnp.sum(gq[...].astype(F32), axis=0, keepdims=True)
    pltpu.make_async_copy(gbuf, gbuf, gsem).wait()


def att_backward_first(meta, gmix, ght, n1, qkv, mix, n_j, absolute):
    width, rows = ght.shape
    n_i, he = 4, 2 * HEAD
    wq = width // n_j
    grads = grad_shapes(n_j, n_i, absolute, (4, wq, he))
    return pl.pallas_call(
        functools.partial(att_bwd_first_kernel, n_i, n_j, len(grads)),
        in_specs=[SMEM_SPEC] + [VMEM_SPEC] * 5,
        out_specs=[VMEM_SPEC] * 3 + [ANY_SPEC] * len(grads),
        out_shape=[
            jax.ShapeDtypeStruct((width, rows), BF),
            jax.ShapeDtypeStruct((rows, 6 * he), BF),
            jax.ShapeDtypeStruct((1, 6 * he), F32),
        ]
        + grads,
        scratch_shapes=[pltpu.VMEM((4, width, 2 * he), BF), pltpu.SemaphoreType.DMA],
        compiler_params=pltpu.CompilerParams(vmem_limit_bytes=60 * MIB),
        cost_estimate=pl.CostEstimate(flops=16_000_000_000, bytes_accessed=20_000_000, transcendentals=1_250_000),
        name="att_backward_first",
    )(meta, gmix, ght, n1, qkv, mix)


def att_bwd_last_kernel(
    parts, n_i, n_j, n_out, meta_ref, x_ref, gmix, ght, n1t, gqa_ref, qkv_ref, mix_ref, *rest
):
    w_refs = rest[: len(parts)]
    rest = rest[len(parts) + n_out :]
    gn1_ref, bias_ref, sums_ref = rest[:3]
    rest = rest[3:]
    grad_refs = rest[:n_out]
    gq, w_scr, gbuf, sem, gsem = rest[n_out:]
    rows, width = x_ref.shape
    he = 2 * HEAD
    wq = width // n_j
    q = meta_ref[4]
    place = lambda rws, i, t: w_scr.at[rws, pl.ds(att_column(n_i, i, t), he)]
    load_blocks(parts, w_refs, q, (0, 1, 2), wq, range(n_i), place, sem)
    gbuf[3] = mm(ght[...], mix_ref[...]).astype(BF)
    att_back_blocks(meta_ref, qkv_ref, gmix, gq, rows, 0)
    for t in range(3):
        gbuf[t] = mm(n1t[...], gq[:, 2 * t * he : 2 * (t + 1) * he]).astype(BF)
    put_att_grads(grad_refs, q, n_j, wq, gbuf, gsem, 1)
    bias_ref[...] = jnp.sum(gq[...].astype(F32), axis=0, keepdims=True)
    sums_ref[...] = jnp.zeros_like(sums_ref)
    pltpu.make_async_copy(w_scr, w_scr, sem).wait()
    rb = rows // 3

    @pl.loop(0, 3)
    def _(r):
        rw = pl.ds(pl.multiple_of(r * rb, rb), rb)
        grad = mm(gqa_ref[rw, :], w_scr[:, : 6 * he], NT) + mm(gq[rw, :], w_scr[:, 6 * he :], NT)
        gn1_ref[rw, :] = grad.astype(BF)
        hat, _ = normalise(x_ref[rw, :].astype(F32))
        sums_ref[0:1, :] += jnp.sum(grad * hat, axis=0, keepdims=True)
        sums_ref[1:2, :] += jnp.sum(grad, axis=0, keepdims=True)

    pltpu.make_async_copy(gbuf, gbuf, gsem).wait()


def att_backward_last(meta, x, gmix, ght, n1t, gqa, qkv, mix, n_j, parts, arrays, first_grads):
    rows, width = x.shape
    n_i, he = 4, 2 * HEAD
    grads = [jax.ShapeDtypeStruct(v.shape, v.dtype) for v in first_grads]
    return pl.pallas_call(
        functools.partial(att_bwd_last_kernel, parts, n_i, n_j, len(grads)),
        in_specs=[SMEM_SPEC] + [VMEM_SPEC] * 7 + [ANY_SPEC] * (len(arrays) + len(grads)),
        out_specs=[VMEM_SPEC] * 3 + [ANY_SPEC] * len(grads),
        out_shape=[
            jax.ShapeDtypeStruct((rows, width), BF),
            jax.ShapeDtypeStruct((1, 6 * he), F32),
            jax.ShapeDtypeStruct((8, width), F32),
        ]
        + grads,
        scratch_shapes=[
            pltpu.VMEM((rows, 6 * he), BF),
            pltpu.VMEM((width, 3 * n_i * he), BF),
            pltpu.VMEM((4, width, 2 * he), BF),
            pltpu.SemaphoreType.DMA,
            pltpu.SemaphoreType.DMA,
        ],
        compiler_params=pltpu.CompilerParams(vmem_limit_bytes=56 * MIB),
        cost_estimate=pl.CostEstimate(flops=20_000_000_000, bytes_accessed=30_000_000, transcendentals=1_250_000),
        input_output_aliases={8 + len(arrays) + n: 3 + n for n in range(len(grads))},
        name="att_backward_last",
    )(meta, x, gmix, ght, n1t, gqa, qkv, mix, *arrays, *first_grads)


def swap(x, axis, bits, what):
    n = lax.axis_size(axis)
    with jax.named_scope(what):
        return lax.ppermute(x, axis, [(i, i ^ bits) for i in range(n)])


def after(x, *deps):
    return lax.optimization_barrier((x,) + deps)[0] if deps else x


def add(*parts):
    total = parts[0].astype(F32)
    for part in parts[1:]:
        total = total + part.astype(F32)
    return total.astype(parts[0].dtype)


def planes():
    n_dp = lax.axis_size("dp")
    return [list(range(core, n_dp, 2)) for core in range(2)]


def gather_plane(block, what):
    with jax.named_scope(what):
        return lax.all_gather(block, "dp", axis_index_groups=planes())


def scatter_plane(blocks, what):
    flat = blocks.reshape(-1, blocks.shape[-1])
    with jax.named_scope(what):
        mine = lax.psum_scatter(
            flat, "dp", scatter_dimension=0, axis_index_groups=planes(), tiled=True
        )
    return mine.reshape(blocks.shape[1:])


def gather_near(own, what):
    return swap(own, "dp", 2, what + "_x1"), swap(own, "dp", 4, what + "_y1")


def gather_far(one, two, what):
    half = one.shape[0] // 2
    return swap(one[:half], "dp", 4, what + "_y2"), swap(two[half:], "dp", 2, what + "_x2")


def scatter_reach(grads, what):
    if len(grads) == 1:
        return (scatter_plane(grads[0], what),)
    _, to_x, to_y, _, _ = grads
    return swap(to_x, "dp", 2, what + "_x1"), swap(to_y, "dp", 4, what + "_y1")


def scatter_last(grads, reach, what):
    if len(grads) == 1:
        return ()
    from_x, from_y = reach
    _, _, _, keep_x, keep_y = grads
    on_x, on_y = add(keep_x, from_y[0::2]), add(keep_y, from_x[0::2])
    return swap(on_x, "dp", 2, what + "_x2"), swap(on_y, "dp", 4, what + "_y2")


def scatter_sum(grads, reach, last):
    if len(grads) == 1:
        return [reach[0][i] for i in range(reach[0].shape[0])]
    own = grads[0]
    return [
        add(own[i], reach[1 - i % 2][i + 1 - i % 2], last[i % 2][i // 2]) for i in range(own.shape[0])
    ]


def gather_z(own, what):
    two = swap(own, "mp", 2, what + "_z2")
    one = swap(own, "mp", 1, what + "_z1")
    return one, two, swap(two, "mp", 1, what + "_z3")


def scatter_z(zero, one, two, three, what):
    two = add(two, swap(three, "mp", 1, what + "_z3"))
    return add(zero, swap(one, "mp", 1, what + "_z1"), swap(two, "mp", 2, what + "_z2"))


def ordered_pair(own, other, core, axis=0):
    return jnp.stack(
        [jnp.where(core == 0, own, other), jnp.where(core == 0, other, own)], axis
    )


def image_routes(n_dp, n_mp, odd):
    pairs = []
    for plane in range(n_dp // 2):
        for core in range(2):
            for z in range(n_mp):
                shift = 2 * core + odd
                worker = (plane * 2 + core) * n_mp + z
                holder = (plane * 2 + (z >> 1)) * n_mp + (z ^ shift)
                pairs.append((holder, worker))
    return pairs


def image_groups(x):
    slots, images, width = x.shape
    return jnp.transpose(x, (1, 0, 2)).reshape(2, images // 2, slots, width)


def for_route(groups, z, odd):
    return lax.dynamic_index_in_dim(groups, (z ^ odd) & 1, 0, False)


def to_image(send, odd, what):
    n_dp, n_mp = lax.axis_size("dp"), lax.axis_size("mp")
    with jax.named_scope(what + "_route" + str(odd)):
        return lax.ppermute(send, ("dp", "mp"), image_routes(n_dp, n_mp, odd))


def from_image(y, z, odd, what):
    n_dp, n_mp = lax.axis_size("dp"), lax.axis_size("mp")
    routes = [(b, a) for a, b in image_routes(n_dp, n_mp, odd)]
    with jax.named_scope(what + "_route" + str(odd)):
        return lax.ppermute(y[:, odd], ("dp", "mp"), routes)


def joined_images(back, z):
    flip = (z & 1) == 1
    groups = jnp.concatenate([jnp.where(flip, back[1], back[0]), jnp.where(flip, back[0], back[1])])
    return jnp.transpose(groups, (1, 0, 2))


def local(
    tokens,
    counts,
    norm_gains,
    norm_shifts,
    qkv_weight,
    qkv_bias,
    proj_weight,
    out_biases,
    up_weight,
    up_bias,
    down_weight,
    cotangent,
):
    slots, images, width = tokens.shape
    n_dp, n_mp = lax.axis_size("dp"), lax.axis_size("mp")
    n_q = n_dp // 2
    wq = width // n_q
    dp, z = lax.axis_index("dp"), lax.axis_index("mp")
    q, core = dp >> 1, dp & 1
    own_images = images // 2
    all_slots = slots * n_mp
    rows = own_images * all_slots

    def rel(v):
        blocks = [lax.dynamic_slice_in_dim(v, (q ^ j) * wq, wq, v.ndim - 1) for j in range(n_q)]
        return jnp.concatenate(blocks, -1)

    def half_of(v, which, axis):
        size = v.shape[axis] // 2
        return lax.dynamic_slice_in_dim(v, which * size, size, axis)

    att = jnp.concatenate([qkv_weight, jnp.transpose(proj_weight)[None]])
    ffn_w = jnp.stack([up_weight, jnp.transpose(down_weight)])
    he, fh = att.shape[-1] // 2, ffn_w.shape[-1] // 2

    count_rows = jnp.pad(counts.astype(BF)[None], ((0, 15), (0, he - images)))
    sent = jnp.concatenate([half_of(att, 1 - core, 2).reshape(-1, he), count_rows])
    got = swap(sent, "dp", 1, "att_w_core")
    other_counts = got[-16, :images].astype(jnp.int32)
    got = got[:-16].reshape(4, wq // 2, he)
    att_own = ordered_pair(half_of(att, core, 2), got, core, 1).reshape(-1, he)
    got = swap(half_of(ffn_w, 1 - core, 2), "dp", 1, "ffn_w_core")
    ffn_own = ordered_pair(half_of(ffn_w, core, 2), got, core, 1).reshape(2, wq, fh)
    left = jnp.concatenate(
        [half_of(qkv_bias, core, 1), half_of(up_bias, core, 0).reshape(-1, he)]
    )
    n_bias = left.shape[0]
    terms = []
    for _ in range(3):
        term = lax.reduce_precision(left, 8, 7)
        terms.append(term.astype(BF))
        left = left - term
    bias_pad = -(-3 * n_bias // 16) * 16
    bias_terms = jnp.pad(jnp.concatenate(terms), ((0, bias_pad - 3 * n_bias), (0, 0)))

    counts_here = jnp.where((z >> 1) == core, counts, other_counts)
    counts_here = lax.dynamic_slice_in_dim(counts_here, (z & 1) * own_images, own_images, 0)
    meta = jnp.concatenate([counts_here, z[None], q[None]])
    slot_ids = jnp.arange(slots, dtype=jnp.int32)
    keep_mine = ((z * slots + slot_ids)[:, None] < BUF + counts[None, :])[:, :, None]

    def whole_rows(got, what):
        return ordered_pair(got, swap(got, "dp", 1, what), core, 1).reshape(rows, width)

    n_i = n_mp
    gains, shifts, out_b = rel(norm_gains), rel(norm_shifts), rel(out_biases)
    square = n_q == 4
    pair_places = [(j, i, 0, 2, False) for j, i in ((0, 0), (1, 0), (2, 0), (3, 0), (3, 1))]
    both = lax.optimization_barrier

    def flat(v):
        return v.reshape(v.shape[:-3] + (-1, v.shape[-1]))

    row_half = lambda v, which: half_of(v.reshape(own_images, n_mp, slots, width), which, 1)

    att_mine = jnp.concatenate([att_own, bias_terms])
    two = swap(att_mine, "mp", 2, "att_w_z2")
    one = swap(att_mine, "mp", 1, "att_w_z1")
    token_groups = image_groups(rel(tokens))
    sends = [for_route(token_groups, z, odd) for odd in (0, 1)]
    one, two, sends, ffn_own = both((one, two, sends, ffn_own))
    three = swap(two, "mp", 1, "att_w_z3")
    far_one, far_two = swap(ffn_own, "mp", 1, "ffn_w_z1"), swap(ffn_own, "mp", 2, "ffn_w_z2")
    att_z = jnp.stack([att_mine, one, two, three])
    bias_all = att_z[:, 4 * wq : 4 * wq + 3 * n_bias].astype(F32).reshape(n_i, 3, n_bias, he)
    bias_all = bias_all[:, 0] + (bias_all[:, 1] + bias_all[:, 2])
    bias_three = jnp.stack([bias_all[:, 0], jnp.zeros((n_i, he), F32), bias_all[:, 1]])
    bias_rows = jnp.transpose(bias_three.reshape(3, 2, 2, he), (1, 0, 2, 3)).reshape(1, -1)
    att_near = gather_near(att_z, "att_w") if square else ()
    far_one, far_two, sends, bias_rows = both((far_one, far_two, sends, bias_rows))
    far_three = swap(far_two, "mp", 1, "ffn_w_z3")
    token_rows = [to_image(sends[odd], odd, "tokens") for odd in (0, 1)]

    if square:
        att_far = gather_far(*att_near, "att_w")
        att_places = [(j, i, 0, 4, False) for j, i in ((0, 0), (1, 0), (2, 0), (3, 0), (3, 2))]
    else:
        att_far, att_places = (gather_plane(att_z, "att_w"),), [(0, 0, 0, 4, True)]
    cot = rel(jnp.where(keep_mine, cotangent, jnp.zeros_like(cotangent)))
    cot_groups = image_groups(cot)
    sends = [for_route(cot_groups, z, odd) for odd in (0, 1)]
    token_rows, att_far, far_three, sends = both((token_rows, att_far, far_three, sends))
    att_parts = [v[None] for v in (att_z, *att_near, *att_far)] if square else list(att_far)
    x = whole_rows(jnp.stack(token_rows, 1), "tokens_core")
    ffn_far = flat(jnp.stack([far_two, far_three]))
    x, ffn_far, sends = both((x, ffn_far, sends))
    far_near = gather_near(ffn_far, "ffn_w2") if square else ()
    cot_rows = [to_image(sends[odd], odd, "cotangent") for odd in (0, 1)]
    n1, qkva, qkvb, mixa, mixb, part = att_forward(
        x.reshape(own_images, all_slots, width),
        gains[0:1],
        shifts[0:1],
        bias_rows,
        meta,
        att_places,
        att_parts,
    )
    part, n1, x, far_near, cot_rows = both((part, n1, x, far_near, cot_rows))
    part_other = swap(part, "dp", 1, "attended")
    if square:
        far_far = gather_far(*far_near, "ffn_w2")
        parts0 = [v[None] for v in (ffn_far, *far_near, *far_far)]
        places = pair_places
    else:
        parts0, places = [gather_plane(ffn_far, "ffn_w2")], [(0, 0, 0, 2, True)]
    go = whole_rows(jnp.stack(cot_rows, 1), "cotangent_core")
    ffn_here = flat(jnp.stack([ffn_own, far_one]))
    go, parts0, part_other, ffn_here = both((go, parts0, part_other, ffn_here))
    here_near = gather_near(ffn_here, "ffn_w0") if square else ()
    up_rows = bias_all[:, 2:].reshape(n_i, fh)
    hidden, n2, n2t, got, sum_b, sum_g, upg1, *ffn_g0 = ffn_call(
        [x, part, part_other, out_b[0:1], gains[1:2], shifts[1:2], go, up_rows[2:], meta],
        n_q,
        2,
        fh,
        places,
        parts0,
        True,
        not square,
    )
    n2, ffn_g0, here_near = both((n2, ffn_g0, here_near))
    if square:
        parts1 = [v[None] for v in (ffn_here, *here_near, *gather_far(*here_near, "ffn_w0"))]
    else:
        parts1 = [gather_plane(ffn_here, "ffn_w0")]
    n2, parts1, ffn_g0 = both((n2, parts1, ffn_g0))
    reach_f0 = scatter_reach(ffn_g0, "ffn_g0")
    branch, gn2, upg0, *ffn_g1 = ffn_call(
        [n2, n2t, got, sum_b, sum_g, go, up_rows[:2], meta],
        n_q,
        2,
        fh,
        places,
        parts1,
        False,
        not square,
    )
    branch, gn2, ffn_g1, reach_f0 = both((branch, gn2, ffn_g1, reach_f0))

    last_f0 = scatter_last(ffn_g0, reach_f0, "ffn_g0")
    reach_f1 = scatter_reach(ffn_g1, "ffn_g1")
    gn2_other = swap(gn2, "dp", 1, "grad_norm_two")
    theirs = swap(row_half(branch, 1 - core), "dp", 1, "branch")
    gn2_other, theirs = both((gn2_other, theirs))
    out_half = row_half(hidden, core) + row_half(branch, core).astype(F32) + theirs.astype(F32) + out_b[1]
    gn2_other, out_half = both((gn2_other, rel(out_half.astype(BF))))
    out_first = from_image(out_half, z, 0, "block_out")
    gh, ght, gmixa, gmixb, sums = hidden_backward(
        meta, hidden, gn2, gn2_other, gains[1:2], go, n_q, att_places, att_parts
    )
    gmixa, last_f0, out_first, out_half = both((gmixa, last_f0, out_first, out_half))
    ffn2, ffn3 = scatter_sum(ffn_g0, reach_f0, last_f0)
    ffn_three = swap(ffn3, "mp", 1, "ffn_g_z3")
    out_last = from_image(out_half, z, 1, "block_out")
    gmixa, ffn2 = both((gmixa, ffn2))
    n1t, gqa, bias_a, *att_g = att_backward_first(
        meta, gmixa, ght, n1, qkva, mixa, n_q, not square
    )
    n1t, gqa, reach_f1, ffn_three, out_last = both((n1t, gqa, reach_f1, ffn_three, out_last))
    last_f1 = scatter_last(ffn_g1, reach_f1, "ffn_g1")
    ffn_two = swap(add(ffn2, ffn_three), "mp", 2, "ffn_g_z2")
    gn1, bias_b, more_sums, *att_g = att_backward_last(
        meta, x, gmixb, ght, n1t, gqa, qkvb, mixb, n_q, att_places, att_parts, att_g
    )
    gn1, last_f1, att_g, x, ffn_two = both((gn1, last_f1, att_g, x, ffn_two))

    ffn0, ffn1 = scatter_sum(ffn_g1, reach_f1, last_f1)
    ffn_one = swap(ffn1, "mp", 1, "ffn_g_z1")
    gn1_other = swap(after(row_half(gn1, 1 - core), ffn1), "dp", 1, "grad_norm_one")
    reach_a = scatter_reach(att_g, "att_g")
    gn1 = row_half(gn1, core).astype(F32) + gn1_other.astype(F32)
    hat1, inv1 = normalise(after(row_half(x, core), gn1_other).astype(F32))
    input_half = row_half(gh, core) + norm_back(hat1, inv1, gains[0], gn1)
    input_half = rel(input_half.astype(BF))
    in_first = from_image(input_half, z, 0, "input_grad")
    reach_a, ffn_one, in_first, input_half, upg0, upg1, bias_a, bias_b, sums, more_sums = both(
        (reach_a, ffn_one, in_first, input_half, upg0, upg1, bias_a, bias_b, sums, more_sums)
    )
    in_last = from_image(input_half, z, 1, "input_grad")
    last_a = scatter_last(att_g, reach_a, "att_g")

    def placed(values):
        mine = jnp.concatenate([lax.dynamic_slice_in_dim(values, z ^ i, 1, 0) for i in range(n_i)])
        return jnp.stack([jnp.where(core == c, mine, jnp.zeros_like(mine)) for c in range(2)], 1)

    bias_a, bias_b = (v.reshape(3, 2, he) for v in (bias_a, bias_b))
    wide = [placed(jnp.concatenate([bias_a[t], bias_b[t]])) for t in (0, 2)]
    wide.append(placed(jnp.concatenate([upg0, upg1])))
    values = [*wide, rel(sums), rel(more_sums)]
    vector = jnp.concatenate([v.reshape(-1, 128) for v in values])
    vector = vector + swap(vector, "dp", 1, "sums_core")
    last_a, vector = both((last_a, vector))
    att0, att1, att2, att3 = scatter_sum(att_g, reach_a, last_a)
    att_three = swap(att3, "mp", 1, "att_g_z3")
    att_one = swap(att1, "mp", 1, "att_g_z1")
    vector = vector + swap(vector, "dp", 2, "sums_dp2")
    att_three, vector = both((att_three, vector))
    att_two = swap(add(att2, att_three), "mp", 2, "att_g_z2")
    bit = 4
    while bit < n_dp:
        vector = vector + swap(vector, "dp", bit, "sums_dp" + str(bit))
        bit *= 2
    for bit in (1, 2):
        vector = vector + swap(vector, "mp", bit, "sums_z" + str(bit))
    att_grad = add(att0, att_one, att_two)
    ffn_grad = add(ffn0, ffn_one, ffn_two)
    in_routes = [in_first, in_last]
    block_out = joined_images([out_first, out_last], z)
    block_out = jnp.where(keep_mine, block_out, jnp.zeros_like(block_out))
    input_grad = joined_images(in_routes, z)

    def own_shard(grad, what):
        kinds, _, last = grad.shape
        pair = grad.reshape(kinds, 2, wq // 2, last)
        keep = lax.dynamic_index_in_dim(pair, core, 1, False)
        got = swap(lax.dynamic_index_in_dim(pair, 1 - core, 1, False), "dp", 1, what)
        return ordered_pair(keep, got, core, 2).reshape(kinds, wq // 2, 2 * last).astype(F32)

    att_shard, ffn_shard = own_shard(att_grad, "att_g_core"), own_shard(ffn_grad, "ffn_g_core")
    qkv_owned, proj_owned = att_shard[:3], jnp.transpose(att_shard[3])
    up_owned, down_owned = ffn_shard[0], jnp.transpose(ffn_shard[1])

    ends = [0]
    for v in values:
        ends.append(ends[-1] + v.size // 128)
    *wide, sums, more_sums = [
        vector[start:end].reshape(v.shape) for v, start, end in zip(values, ends, ends[1:])
    ]
    wide = [lax.dynamic_index_in_dim(v, z, 0, False).reshape(-1) for v in wide]
    bias_grad, upbias_grad = jnp.stack(wide[:2]), wide[2]
    gains_grad = jnp.stack([more_sums[0], sums[0] * 0.5])
    shifts_grad = jnp.stack([more_sums[1], sums[1] * 0.5])
    outbias_grad = sums[2:4] * 0.5
    return (
        block_out,
        input_grad,
        gains_grad,
        shifts_grad,
        qkv_owned,
        bias_grad,
        proj_owned,
        outbias_grad,
        up_owned,
        upbias_grad,
        down_owned,
    )


def solution(mesh):
    split = P("mp", "dp", None)
    return jax.shard_map(
        local,
        mesh=mesh,
        in_specs=(
            split,
            P("dp"),
            P(),
            P(),
            P(None, "dp", "mp"),
            P(None, "mp"),
            P("mp", "dp"),
            P(),
            P("dp", "mp"),
            P("mp"),
            P("mp", "dp"),
            split,
        ),
        out_specs=(
            split,
            split,
            P(),
            P(),
            P(None, "dp", "mp"),
            P(None, "mp"),
            P("mp", "dp"),
            P(),
            P("dp", "mp"),
            P("mp"),
            P("mp", "dp"),
        ),
        check_vma=False,
    )
```

```python
import functools

import jax
import jax.numpy as jnp
from jax import lax
from jax.experimental import pallas as pl
from jax.experimental.pallas import tpu as pltpu
from jax.sharding import PartitionSpec as P

HEAD = 64
BUF = 64
BF = jnp.bfloat16
F32 = jnp.float32
epsilon = 1e-06
masked_score = -1e30
MIB = 1 << 20
NT = (((1,), (1,)), ((), ()))
NN = (((1,), (0,)), ((), ()))
TN = (((0,), (0,)), ((), ()))
factor = HEAD ** (-0.5)
VMEM_SPEC = pl.BlockSpec(memory_space=pltpu.VMEM)
ANY_SPEC = pl.BlockSpec(memory_space=pl.ANY)
SMEM_SPEC = pl.BlockSpec(memory_space=pltpu.SMEM)


def mm(a, b, dims=NN):
    return lax.dot_general(a, b, dims, preferred_element_type=F32)


def normalise(values):
    average = jnp.mean(values, axis=-1, keepdims=True)
    centred = values - average
    spread = jnp.mean(centred * centred, axis=-1, keepdims=True)
    inv = lax.rsqrt(spread + epsilon)
    return centred * inv, inv


def norm_back(n, inv, scales, grad):
    e = grad * scales
    mean_e = jnp.mean(e, axis=-1, keepdims=True)
    mean_en = jnp.mean(e * n, axis=-1, keepdims=True)
    return (e - mean_e - n * mean_en) * inv


def gelu_parts(inputs):
    normal_cdf = 0.5 + 0.5 * lax.erf(inputs * 0.7071067811865476)
    density = jnp.exp(-0.5 * inputs * inputs) * 0.3989422804014327
    return inputs * normal_cdf, normal_cdf + inputs * density


def for_each(count, step):
    if count <= 4:
        for index in range(count):
            step(index)
    else:
        pl.loop(0, count)(step)


def valid_slots(meta_ref, image, slots, axis):
    shape = (slots, 1) if axis == 0 else (1, slots)
    row = lax.broadcasted_iota(jnp.int32, shape, axis)
    n = slots // 4
    k = (row >= n).astype(jnp.int32) + (row >= 2 * n) + (row >= 3 * n)
    slot = (k ^ meta_ref[3]) * n + (row - k * n)
    return slot < BUF + meta_ref[image]


def block_rows(jj, size):
    start = jj * size
    return pl.ds(start if isinstance(jj, int) else pl.multiple_of(start, size), size)


def load_blocks(parts, refs, q, kinds, wq, wanted, place, sem):
    for (j0, i0, t0, count, absolute), ref in zip(parts, refs):
        nj, ni = ref.shape[:2]

        def one(jj, ref=ref, j0=j0, i0=i0, t0=t0, count=count, absolute=absolute, ni=ni):
            source = jj ^ q if absolute else jj
            for ii in range(ni):
                if i0 + ii not in wanted:
                    continue
                for t in range(t0, t0 + count):
                    if t in kinds:
                        pltpu.make_async_copy(
                            ref.at[source, ii, pl.ds((t - t0) * wq, wq)],
                            place(block_rows(j0 + jj, wq), i0 + ii, t),
                            sem,
                        ).start()

        for_each(nj, one)


def store_blocks(refs, q, n_j, block, i, sem):
    def start(views, target):
        for t, view in enumerate(views):
            pltpu.make_async_copy(view, target.at[t], sem).start()

    if len(refs) == 1:
        for_each(n_j, lambda jj: start(block(jj), refs[0].at[jj ^ q, i]))
        return
    own, to_x, to_y, keep_x, keep_y = refs
    start(block(0), own.at[i])
    if i == 0:
        start(block(1), keep_x.at[0])
        start(block(2), to_y.at[1])
        start(block(3), to_y.at[0])
    else:
        start(block(1), to_x.at[1])
        start(block(2), keep_y.at[0])
        start(block(3), to_x.at[0])


def grad_shapes(n_j, n_i, absolute, block):
    shape = lambda *lead: jax.ShapeDtypeStruct(lead + block, BF)
    if absolute:
        return [shape(n_j, n_i)]
    return [shape(2), shape(2), shape(2), shape(1), shape(1)]


def att_column(n_i, i, t):
    he = 2 * HEAD
    if t == 3:
        return 3 * n_i * he + i * he
    return (i // 2) * 6 * he + (t * 2 + i % 2) * he


def att_fwd_kernel(parts, n_i, x_ref, g_ref, c_ref, bias_ref, meta_ref, *rest):
    w_refs = rest[: len(parts)]
    n1_ref, qkva_ref, qkvb_ref, mixa_ref, mixb_ref, part_ref, w_scr, m_scr, sem = rest[len(parts) :]
    he = 2 * HEAD
    width = w_scr.shape[0]
    image = pl.program_id(0)

    @pl.when(image == 0)
    def _():
        place = lambda rows, i, t: w_scr.at[rows, pl.ds(att_column(n_i, i, t), he)]
        wq = width // max(p[0] + r.shape[0] for p, r in zip(parts, w_refs))
        load_blocks(parts, w_refs, meta_ref[4], range(4), wq, range(n_i), place, sem)
        pltpu.make_async_copy(w_scr, w_scr, sem).wait()

    hat, _ = normalise(x_ref[0].astype(F32))
    n1 = (hat * g_ref[...] + c_ref[...]).astype(BF)
    n1_ref[...] = n1
    qkv_refs = (qkva_ref, qkvb_ref)
    for half in range(2):
        cols = pl.ds(half * 6 * he, 6 * he)
        res = (mm(n1, w_scr[:, cols]) + bias_ref[:, cols]).astype(BF)
        for n in range(6):
            qkv_refs[half][n] = res[:, n * he : (n + 1) * he]
    bias = jnp.where(valid_slots(meta_ref, image, x_ref.shape[1], 1), 0.0, masked_score)
    lane = lax.broadcasted_iota(jnp.int32, (1, he), 1)
    low_half = lane < HEAD
    for i in range(n_i):
        ref = qkv_refs[i // 2]
        q2, k2, v2 = (ref[t * 2 + i % 2] for t in range(3))
        outs = []
        for h in range(2):
            qm = jnp.where(low_half if h == 0 else ~low_half, q2, jnp.zeros_like(q2))
            s = mm(qm, k2, NT) * factor + bias
            top = jnp.max(s, axis=-1, keepdims=True)
            p = jnp.exp(s - top)
            w = (p / jnp.sum(p, axis=-1, keepdims=True)).astype(BF)
            outs.append(mm(w, v2))
        mixed = jnp.where(low_half, outs[0], outs[1]).astype(BF)
        m_scr[:, i * he : (i + 1) * he] = mixed
    mixa_ref[...] = m_scr[:, : 2 * he]
    mixb_ref[...] = m_scr[:, 2 * he :]
    part_ref[...] = mm(m_scr[...], w_scr[:, 3 * n_i * he :], NT).astype(BF)


def att_forward(x, gain, shift, bias, meta, parts, arrays):
    images, slots, width = x.shape
    n_i = 4
    he = 2 * HEAD
    rows = images * slots
    row_block = lambda last: pl.BlockSpec((slots, last), lambda a: (a, 0))
    whole = lambda *shape: pl.BlockSpec(shape, lambda a: (0,) * len(shape))
    qkv_block = pl.BlockSpec((6, slots, he), lambda a: (0, a, 0))
    return pl.pallas_call(
        functools.partial(att_fwd_kernel, parts, n_i),
        grid=(images,),
        in_specs=[
            pl.BlockSpec((1, slots, width), lambda a: (a, 0, 0)),
            whole(1, width),
            whole(1, width),
            whole(1, 3 * n_i * he),
            SMEM_SPEC,
        ]
        + [ANY_SPEC] * len(arrays),
        out_specs=[row_block(width), qkv_block, qkv_block, row_block(2 * he), row_block(2 * he), row_block(width)],
        out_shape=[
            jax.ShapeDtypeStruct((rows, width), BF),
            jax.ShapeDtypeStruct((6, rows, he), BF),
            jax.ShapeDtypeStruct((6, rows, he), BF),
            jax.ShapeDtypeStruct((rows, 2 * he), BF),
            jax.ShapeDtypeStruct((rows, 2 * he), BF),
            jax.ShapeDtypeStruct((rows, width), BF),
        ],
        scratch_shapes=[
            pltpu.VMEM((width, 4 * n_i * he), BF),
            pltpu.VMEM((slots, n_i * he), BF),
            pltpu.SemaphoreType.DMA,
        ],
        compiler_params=pltpu.CompilerParams(vmem_limit_bytes=48 * MIB),
        cost_estimate=pl.CostEstimate(flops=16_000_000_000, bytes_accessed=20_000_000, transcendentals=2_500_000),
        name="att_forward",
    )(x, gain, shift, bias, meta, *arrays)


def ffn_kernel(parts, n_i, n_j, n_out, first, *refs):
    if first:
        x_ref, pa_ref, pb_ref, b_ref, g_ref, c_ref = refs[:6]
        refs = refs[6:]
    else:
        kept, refs = refs[:5], refs[5:]
    go_ref, upb_ref, meta_ref = refs[:3]
    w_refs, refs = refs[3 : 3 + len(parts)], refs[3 + len(parts) :]
    q = meta_ref[4]
    if first:
        hidden_out, refs = refs[0], refs[1:]
        kept, refs = refs[:5], refs[5:]
        sum_outs = kept[3:]
    else:
        sum_outs, refs = refs[:2], refs[2:]
    upg_ref, refs = refs[0], refs[1:]
    grad_refs, refs = refs[:n_out], refs[n_out:]
    n2, n2t, got, run_b, run_g, wbuf, gbuf, act_s, pre_s, wsem, gsem, ksem, ssem = refs[:13]
    held = (n2, n2t, got, run_b, run_g)
    if first:
        hidden, hsem = refs[13:]
        low_sums = (run_b, run_g)
    else:
        low_sums = refs[13:]
    rows, width = go_ref.shape
    wq = width // n_j
    rb = rows // 3

    def fetch(i, slot):
        place = lambda rws, _, t: wbuf.at[slot, t, rws]
        load_blocks(parts, w_refs, q, range(2), wq, (i,), place, wsem.at[slot])

    def fetched(slot):
        pltpu.make_async_copy(wbuf.at[slot], wbuf.at[slot], wsem.at[slot]).wait()

    def put(i, slot):
        block = lambda jj: [gbuf.at[slot, t, block_rows(jj, wq)] for t in range(2)]
        store_blocks(grad_refs, q, n_j, block, i, gsem.at[slot])

    def stored(slot):
        pltpu.make_async_copy(gbuf.at[slot], gbuf.at[slot], gsem.at[slot]).wait()

    def keep(n):
        if first:
            return pltpu.make_async_copy(held[n], kept[n], ksem.at[n])
        return pltpu.make_async_copy(kept[n], held[n], ksem.at[n])

    fetch(0, 0)
    if first:
        block = 192

        @pl.loop(0, rows // block)
        def _(r):
            rw = pl.ds(pl.multiple_of(r * block, block), block)
            h = (
                x_ref[rw, :].astype(F32)
                + (pa_ref[rw, :].astype(F32) + pb_ref[rw, :].astype(F32))
                + b_ref[...]
            )
            hidden[rw, :] = h
            hat, _ = normalise(h)
            n2[rw, :] = (hat * g_ref[...] + c_ref[...]).astype(BF)

        pltpu.make_async_copy(hidden, hidden_out, hsem).start()
        keep(0).start()
        n2t[...] = n2[...].T
        keep(1).start()
        got[...] = go_ref[...].T
        keep(2).start()
    else:
        for n in (0, 3, 4, 1, 2):
            keep(n).start()
        keep(0).wait()
    for i in range(n_i):
        slot = i % 2
        if i + 1 < n_i:
            fetch(i + 1, 1 - slot)
        fetched(slot)
        if i == 0 and not first:
            keep(3).wait()
            keep(4).wait()

        @pl.loop(0, 3)
        def _(r, i=i, slot=slot):
            rw = pl.ds(pl.multiple_of(r * rb, rb), rb)
            u, w = wbuf[slot, 0], wbuf[slot, 1]
            up = mm(n2[rw, :], u) + upb_ref[i : i + 1, :]
            act, slope = gelu_parts(up)
            act = act.astype(BF)
            act_s[rw, :] = act
            pre = (mm(go_ref[rw, :], w) * slope).astype(BF)
            pre_s[rw, :] = pre
            down = mm(act, w, NT)
            back = mm(pre, u, NT)
            if i > 0 or not first:
                down += run_b[rw, :]
                back += run_g[rw, :]
            if i < n_i - 1:
                run_b[rw, :] = down
                run_g[rw, :] = back
            else:
                for n, total in enumerate((down, back)):
                    low_sums[n][rw, :] = total.astype(low_sums[n].dtype)
                    pltpu.make_async_copy(low_sums[n].at[rw], sum_outs[n].at[rw], ssem.at[n]).start()

        if i == 0 and not first:
            keep(1).wait()
            keep(2).wait()
        upg_ref[i : i + 1, :] = jnp.sum(pre_s[...].astype(F32), axis=0, keepdims=True)
        if i >= 2:
            stored(slot)
        gbuf[slot, 0] = mm(n2t[...], pre_s[...]).astype(BF)
        gbuf[slot, 1] = mm(got[...], act_s[...]).astype(BF)
        put(i, slot)
    for n in range(2):
        pltpu.make_async_copy(low_sums[n], sum_outs[n], ssem.at[n]).wait()
    if first:
        pltpu.make_async_copy(hidden, hidden_out, hsem).wait()
        for n in range(3):
            keep(n).wait()
    for i in range(max(n_i - 2, 0), n_i):
        stored(i % 2)


def ffn_call(ins, n_j, n_i, fh, parts, arrays, first, absolute):
    go = ins[-3]
    rows, width = go.shape
    wq = width // n_j
    wide, low, turned = (rows, width, F32), (rows, width, BF), (width, rows, BF)
    outs = [wide, low, turned, turned, wide, wide] if first else [low, low]
    grads = grad_shapes(n_j, n_i, absolute, (2, wq, fh))
    if first:
        in_specs = [VMEM_SPEC] * (len(ins) - 1)
    else:
        in_specs = [ANY_SPEC] * 5 + [VMEM_SPEC] * 2
    extra = (
        [pltpu.VMEM((rows, width), F32), pltpu.SemaphoreType.DMA]
        if first
        else [pltpu.VMEM((rows, width), BF)] * 2
    )
    return pl.pallas_call(
        functools.partial(ffn_kernel, parts, n_i, n_j, len(grads), first),
        in_specs=in_specs + [SMEM_SPEC] + [ANY_SPEC] * len(arrays),
        out_specs=[ANY_SPEC] * len(outs) + [VMEM_SPEC] + [ANY_SPEC] * len(grads),
        out_shape=[jax.ShapeDtypeStruct((m, n), kind) for m, n, kind in outs]
        + [jax.ShapeDtypeStruct((n_i, fh), F32)]
        + grads,
        scratch_shapes=[
            pltpu.VMEM((rows, width), BF),
            pltpu.VMEM((width, rows), BF),
            pltpu.VMEM((width, rows), BF),
            pltpu.VMEM((rows, width), F32),
            pltpu.VMEM((rows, width), F32),
            pltpu.VMEM((2, 2, width, fh), BF),
            pltpu.VMEM((2, 2, width, fh), BF),
            pltpu.VMEM((rows, fh), BF),
            pltpu.VMEM((rows, fh), BF),
            pltpu.SemaphoreType.DMA((2,)),
            pltpu.SemaphoreType.DMA((2,)),
            pltpu.SemaphoreType.DMA((5,)),
            pltpu.SemaphoreType.DMA((2,)),
        ]
        + extra,
        compiler_params=pltpu.CompilerParams(vmem_limit_bytes=56 * MIB),
        cost_estimate=pl.CostEstimate(
            flops=12_000_000_000 * n_i, bytes_accessed=30_000_000, transcendentals=1_000_000 * n_i
        ),
        name="ffn_first" if first else "ffn_last",
    )(*ins, *arrays)


def att_back_blocks(meta_ref, qkv_ref, gmix, gq, rows, which):
    he = 2 * HEAD
    images = 3
    slots = rows // images
    lane = lax.broadcasted_iota(jnp.int32, (1, he), 1)
    low_half = lane < HEAD

    @pl.loop(0, images)
    def _(a):
        rw = pl.ds(pl.multiple_of(a * slots, slots), slots)
        bias = jnp.where(valid_slots(meta_ref, a, slots, 0), 0.0, masked_score)
        for i in range(2):
            q2, k2, v2 = (qkv_ref[t * 2 + i, rw, :] for t in range(3))
            g2 = gmix[which + i, rw, :]
            dq, dk, dv = [], [], []
            for h in range(2):
                here = low_half if h == 0 else ~low_half
                qm = jnp.where(here, q2, jnp.zeros_like(q2))
                gm = jnp.where(here, g2, jnp.zeros_like(g2))
                st = mm(k2, qm, NT) * factor + bias
                top = jnp.max(st, axis=0, keepdims=True)
                p = jnp.exp(st - top)
                p = p / jnp.sum(p, axis=0, keepdims=True)
                dpt = mm(v2, gm, NT)
                dot = jnp.sum(p * dpt, axis=0, keepdims=True)
                ds = (p * (dpt - dot)).astype(BF)
                dk.append(mm(ds, q2))
                dv.append(mm(p.astype(BF), g2))
                dq.append(mm(ds, k2, TN))
            for t, (pair, scale) in enumerate(((dq, factor), (dk, factor), (dv, 1.0))):
                both = jnp.where(low_half, pair[0], pair[1])
                gq[rw, (t * 2 + i) * he : (t * 2 + i + 1) * he] = (both * scale).astype(BF)


def put_att_grads(grad_refs, q, n_j, wq, gbuf, gsem):
    he = 2 * HEAD
    for i in range(2):
        block = lambda jj, i=i: [
            gbuf.at[t, block_rows(jj, wq), pl.ds(i * he, he)] for t in range(4)
        ]
        store_blocks(grad_refs, q, n_j, block, i, gsem)


def hidden_back_kernel(
    parts, n_i, n_j, meta_ref, hid_ref, ga_ref, gb_ref, g_ref, go_ref, *rest
):
    w_refs = rest[: len(parts)]
    gh_ref, ght, gmixa, gmixb, sums_ref = rest[len(parts) : len(parts) + 5]
    ghb, w_scr, sem = rest[len(parts) + 5 :]
    rows, width = hid_ref.shape
    he = 2 * HEAD
    place = lambda rws, i, t: w_scr.at[rws, pl.ds(i * he, he)]
    load_blocks(parts, w_refs, meta_ref[4], (3,), width // n_j, range(n_i), place, sem)
    sums_ref[...] = jnp.zeros_like(sums_ref)
    pltpu.make_async_copy(w_scr, w_scr, sem).wait()
    block = 192

    @pl.loop(0, rows // block)
    def _(r):
        rw = pl.ds(pl.multiple_of(r * block, block), block)
        hat, inv = normalise(hid_ref[rw, :])
        grad = ga_ref[rw, :].astype(F32) + gb_ref[rw, :].astype(F32)
        gout = go_ref[rw, :].astype(F32)
        gh = gout + norm_back(hat, inv, g_ref[...], grad)
        gh_ref[rw, :] = gh
        low = gh.astype(BF)
        ghb[rw, :] = low
        sums_ref[0:1, :] += jnp.sum(grad * hat, axis=0, keepdims=True)
        sums_ref[1:2, :] += jnp.sum(grad, axis=0, keepdims=True)
        sums_ref[2:3, :] += jnp.sum(gh, axis=0, keepdims=True)
        sums_ref[3:4, :] += jnp.sum(gout, axis=0, keepdims=True)
        res = mm(low, w_scr[...]).astype(BF)
        for i in range(n_i):
            (gmixa, gmixb)[i // 2][i % 2, rw, :] = res[:, i * he : (i + 1) * he]

    ght[...] = ghb[...].T


def hidden_backward(meta, hidden, ga, gb, gain, go, n_j, parts, arrays):
    rows, width = hidden.shape
    n_i, he = 4, 2 * HEAD
    return pl.pallas_call(
        functools.partial(hidden_back_kernel, parts, n_i, n_j),
        in_specs=[SMEM_SPEC] + [VMEM_SPEC] * 5 + [ANY_SPEC] * len(arrays),
        out_specs=[VMEM_SPEC] * 5,
        out_shape=[
            jax.ShapeDtypeStruct((rows, width), F32),
            jax.ShapeDtypeStruct((width, rows), BF),
            jax.ShapeDtypeStruct((2, rows, he), BF),
            jax.ShapeDtypeStruct((2, rows, he), BF),
            jax.ShapeDtypeStruct((8, width), F32),
        ],
        scratch_shapes=[
            pltpu.VMEM((rows, width), BF),
            pltpu.VMEM((width, n_i * he), BF),
            pltpu.SemaphoreType.DMA,
        ],
        compiler_params=pltpu.CompilerParams(vmem_limit_bytes=48 * MIB),
        cost_estimate=pl.CostEstimate(flops=10_000_000_000, bytes_accessed=20_000_000, transcendentals=0),
        name="hidden_backward",
    )(meta, hidden, ga, gb, gain, go, *arrays)


def att_bwd_first_kernel(n_i, n_j, n_out, meta_ref, gmix, ght, n1_ref, qkv_ref, mix_ref, *rest):
    n1t, gq, bias_ref = rest[:3]
    grad_refs = rest[3 : 3 + n_out]
    gbuf, gsem = rest[3 + n_out :]
    width, rows = ght.shape
    he = 2 * HEAD
    gbuf[3] = mm(ght[...], mix_ref[...]).astype(BF)
    att_back_blocks(meta_ref, qkv_ref, gmix, gq, rows, 0)
    n1t[...] = n1_ref[...].T
    for t in range(3):
        gbuf[t] = mm(n1t[...], gq[:, 2 * t * he : 2 * (t + 1) * he]).astype(BF)
    put_att_grads(grad_refs, meta_ref[4], n_j, width // n_j, gbuf, gsem)
    bias_ref[...] = jnp.sum(gq[...].astype(F32), axis=0, keepdims=True)
    pltpu.make_async_copy(gbuf, gbuf, gsem).wait()


def att_backward_first(meta, gmix, ght, n1, qkv, mix, n_j, absolute):
    width, rows = ght.shape
    n_i, he = 4, 2 * HEAD
    wq = width // n_j
    grads = grad_shapes(n_j, 2, absolute, (4, wq, he))
    return pl.pallas_call(
        functools.partial(att_bwd_first_kernel, n_i, n_j, len(grads)),
        in_specs=[SMEM_SPEC] + [VMEM_SPEC] * 5,
        out_specs=[VMEM_SPEC] * 3 + [ANY_SPEC] * len(grads),
        out_shape=[
            jax.ShapeDtypeStruct((width, rows), BF),
            jax.ShapeDtypeStruct((rows, 6 * he), BF),
            jax.ShapeDtypeStruct((1, 6 * he), F32),
        ]
        + grads,
        scratch_shapes=[pltpu.VMEM((4, width, 2 * he), BF), pltpu.SemaphoreType.DMA],
        compiler_params=pltpu.CompilerParams(vmem_limit_bytes=60 * MIB),
        cost_estimate=pl.CostEstimate(flops=16_000_000_000, bytes_accessed=20_000_000, transcendentals=1_250_000),
        name="att_backward_first",
    )(meta, gmix, ght, n1, qkv, mix)


def att_bwd_last_kernel(
    parts, n_i, n_j, n_out, meta_ref, x_ref, gmix, ght, n1t, gqa_ref, qkv_ref, mix_ref, *rest
):
    w_refs = rest[: len(parts)]
    gn1_ref, bias_ref, sums_ref = rest[len(parts) : len(parts) + 3]
    rest = rest[len(parts) + 3 :]
    grad_refs = rest[:n_out]
    gq, w_scr, gbuf, sem, gsem = rest[n_out:]
    rows, width = x_ref.shape
    he = 2 * HEAD
    wq = width // n_j
    q = meta_ref[4]
    place = lambda rws, i, t: w_scr.at[rws, pl.ds(att_column(n_i, i, t), he)]
    load_blocks(parts, w_refs, q, (0, 1, 2), wq, range(n_i), place, sem)
    gbuf[3] = mm(ght[...], mix_ref[...]).astype(BF)
    att_back_blocks(meta_ref, qkv_ref, gmix, gq, rows, 0)
    for t in range(3):
        gbuf[t] = mm(n1t[...], gq[:, 2 * t * he : 2 * (t + 1) * he]).astype(BF)
    put_att_grads(grad_refs, q, n_j, wq, gbuf, gsem)
    bias_ref[...] = jnp.sum(gq[...].astype(F32), axis=0, keepdims=True)
    sums_ref[...] = jnp.zeros_like(sums_ref)
    pltpu.make_async_copy(w_scr, w_scr, sem).wait()
    rb = rows // 3

    @pl.loop(0, 3)
    def _(r):
        rw = pl.ds(pl.multiple_of(r * rb, rb), rb)
        grad = mm(gqa_ref[rw, :], w_scr[:, : 6 * he], NT) + mm(gq[rw, :], w_scr[:, 6 * he :], NT)
        gn1_ref[rw, :] = grad.astype(BF)
        hat, _ = normalise(x_ref[rw, :].astype(F32))
        sums_ref[0:1, :] += jnp.sum(grad * hat, axis=0, keepdims=True)
        sums_ref[1:2, :] += jnp.sum(grad, axis=0, keepdims=True)

    pltpu.make_async_copy(gbuf, gbuf, gsem).wait()


def att_backward_last(meta, x, gmix, ght, n1t, gqa, qkv, mix, n_j, parts, arrays, absolute):
    rows, width = x.shape
    n_i, he = 4, 2 * HEAD
    wq = width // n_j
    grads = grad_shapes(n_j, 2, absolute, (4, wq, he))
    return pl.pallas_call(
        functools.partial(att_bwd_last_kernel, parts, n_i, n_j, len(grads)),
        in_specs=[SMEM_SPEC] + [VMEM_SPEC] * 7 + [ANY_SPEC] * len(arrays),
        out_specs=[VMEM_SPEC] * 3 + [ANY_SPEC] * len(grads),
        out_shape=[
            jax.ShapeDtypeStruct((rows, width), BF),
            jax.ShapeDtypeStruct((1, 6 * he), F32),
            jax.ShapeDtypeStruct((8, width), F32),
        ]
        + grads,
        scratch_shapes=[
            pltpu.VMEM((rows, 6 * he), BF),
            pltpu.VMEM((width, 3 * n_i * he), BF),
            pltpu.VMEM((4, width, 2 * he), BF),
            pltpu.SemaphoreType.DMA,
            pltpu.SemaphoreType.DMA,
        ],
        compiler_params=pltpu.CompilerParams(vmem_limit_bytes=56 * MIB),
        cost_estimate=pl.CostEstimate(flops=20_000_000_000, bytes_accessed=30_000_000, transcendentals=1_250_000),
        name="att_backward_last",
    )(meta, x, gmix, ght, n1t, gqa, qkv, mix, *arrays)


def swap(x, axis, bits, what):
    n = lax.axis_size(axis)
    with jax.named_scope(what):
        return lax.ppermute(x, axis, [(i, i ^ bits) for i in range(n)])


def after(x, *deps):
    return lax.optimization_barrier((x,) + deps)[0] if deps else x


def add(*parts):
    total = parts[0].astype(F32)
    for part in parts[1:]:
        total = total + part.astype(F32)
    return total.astype(parts[0].dtype)


def planes():
    n_dp = lax.axis_size("dp")
    return [list(range(core, n_dp, 2)) for core in range(2)]


def gather_plane(block, what):
    with jax.named_scope(what):
        return lax.all_gather(block, "dp", axis_index_groups=planes())


def scatter_plane(blocks, what):
    flat = blocks.reshape(-1, blocks.shape[-1])
    with jax.named_scope(what):
        mine = lax.psum_scatter(
            flat, "dp", scatter_dimension=0, axis_index_groups=planes(), tiled=True
        )
    return mine.reshape(blocks.shape[1:])


def gather_near(own, what):
    return swap(own, "dp", 2, what + "_x1"), swap(own, "dp", 4, what + "_y1")


def gather_far(one, two, what):
    half = one.shape[0] // 2
    return swap(one[:half], "dp", 4, what + "_y2"), swap(two[half:], "dp", 2, what + "_x2")


def scatter_reach(grads, what):
    if len(grads) == 1:
        return (scatter_plane(grads[0], what),)
    _, to_x, to_y, _, _ = grads
    return swap(to_x, "dp", 2, what + "_x1"), swap(to_y, "dp", 4, what + "_y1")


def scatter_last(grads, reach, what):
    if len(grads) == 1:
        return ()
    from_x, from_y = reach
    _, _, _, keep_x, keep_y = grads
    on_x, on_y = add(keep_x, from_y[0::2]), add(keep_y, from_x[0::2])
    return swap(on_x, "dp", 2, what + "_x2"), swap(on_y, "dp", 4, what + "_y2")


def scatter_sum(grads, reach, last):
    if len(grads) == 1:
        return [reach[0][i] for i in range(reach[0].shape[0])]
    own = grads[0]
    return [
        add(own[i], reach[1 - i % 2][i + 1 - i % 2], last[i % 2][i // 2]) for i in range(own.shape[0])
    ]


def gather_z(own, what):
    two = swap(own, "mp", 2, what + "_z2")
    one = swap(own, "mp", 1, what + "_z1")
    return one, two, swap(two, "mp", 1, what + "_z3")


def scatter_z(zero, one, two, three, what):
    two = add(two, swap(three, "mp", 1, what + "_z3"))
    return add(zero, swap(one, "mp", 1, what + "_z1"), swap(two, "mp", 2, what + "_z2"))


def ordered_pair(own, other, core, axis=0):
    return jnp.stack(
        [jnp.where(core == 0, own, other), jnp.where(core == 0, other, own)], axis
    )


def image_routes(n_dp, n_mp, odd):
    pairs = []
    for plane in range(n_dp // 2):
        for core in range(2):
            for z in range(n_mp):
                shift = 2 * core + odd
                worker = (plane * 2 + core) * n_mp + z
                holder = (plane * 2 + (z >> 1)) * n_mp + (z ^ shift)
                pairs.append((holder, worker))
    return pairs


def image_groups(x):
    slots, images, width = x.shape
    return jnp.transpose(x, (1, 0, 2)).reshape(2, images // 2, slots, width)


def for_route(groups, z, odd):
    return lax.dynamic_index_in_dim(groups, (z ^ odd) & 1, 0, False)


def to_image(send, odd, what):
    n_dp, n_mp = lax.axis_size("dp"), lax.axis_size("mp")
    with jax.named_scope(what + "_route" + str(odd)):
        return lax.ppermute(send, ("dp", "mp"), image_routes(n_dp, n_mp, odd))


def from_image(y, z, odd, what):
    n_dp, n_mp = lax.axis_size("dp"), lax.axis_size("mp")
    routes = [(b, a) for a, b in image_routes(n_dp, n_mp, odd)]
    with jax.named_scope(what + "_route" + str(odd)):
        return lax.ppermute(y[:, odd], ("dp", "mp"), routes)


def joined_images(back, z):
    flip = (z & 1) == 1
    groups = jnp.concatenate([jnp.where(flip, back[1], back[0]), jnp.where(flip, back[0], back[1])])
    return jnp.transpose(groups, (1, 0, 2))


def local(
    tokens,
    counts,
    norm_gains,
    norm_shifts,
    qkv_weight,
    qkv_bias,
    proj_weight,
    out_biases,
    up_weight,
    up_bias,
    down_weight,
    cotangent,
):
    slots, images, width = tokens.shape
    n_dp, n_mp = lax.axis_size("dp"), lax.axis_size("mp")
    n_q = n_dp // 2
    wq = width // n_q
    dp, z = lax.axis_index("dp"), lax.axis_index("mp")
    q, core = dp >> 1, dp & 1
    own_images = images // 2
    all_slots = slots * n_mp
    rows = own_images * all_slots

    def rel(v):
        blocks = [lax.dynamic_slice_in_dim(v, (q ^ j) * wq, wq, v.ndim - 1) for j in range(n_q)]
        return jnp.concatenate(blocks, -1)

    def half_of(v, which, axis):
        size = v.shape[axis] // 2
        return lax.dynamic_slice_in_dim(v, which * size, size, axis)

    att = jnp.concatenate([qkv_weight, jnp.transpose(proj_weight)[None]])
    ffn_w = jnp.stack([up_weight, jnp.transpose(down_weight)])
    he, fh = att.shape[-1] // 2, ffn_w.shape[-1] // 2

    count_rows = jnp.pad(counts.astype(BF)[None], ((0, 15), (0, he - images)))
    sent = jnp.concatenate([half_of(att, 1 - core, 2).reshape(-1, he), count_rows])
    got = swap(sent, "dp", 1, "att_w_core")
    other_counts = got[-16, :images].astype(jnp.int32)
    got = got[:-16].reshape(4, wq // 2, he)
    att_own = ordered_pair(half_of(att, core, 2), got, core, 1).reshape(-1, he)
    got = swap(half_of(ffn_w, 1 - core, 2), "dp", 1, "ffn_w_core")
    ffn_own = ordered_pair(half_of(ffn_w, core, 2), got, core, 1).reshape(2, wq, fh)
    left = jnp.concatenate(
        [half_of(qkv_bias, core, 1), half_of(up_bias, core, 0).reshape(-1, he)]
    )
    n_bias = left.shape[0]
    terms = []
    for _ in range(3):
        term = lax.reduce_precision(left, 8, 7)
        terms.append(term.astype(BF))
        left = left - term
    bias_pad = -(-3 * n_bias // 16) * 16
    bias_terms = jnp.pad(jnp.concatenate(terms), ((0, bias_pad - 3 * n_bias), (0, 0)))

    counts_here = jnp.where((z >> 1) == core, counts, other_counts)
    counts_here = lax.dynamic_slice_in_dim(counts_here, (z & 1) * own_images, own_images, 0)
    meta = jnp.concatenate([counts_here, z[None], q[None]])
    slot_ids = jnp.arange(slots, dtype=jnp.int32)
    keep_mine = ((z * slots + slot_ids)[:, None] < BUF + counts[None, :])[:, :, None]

    def whole_rows(got, what):
        return ordered_pair(got, swap(got, "dp", 1, what), core, 1).reshape(rows, width)

    n_i = n_mp
    gains, shifts, out_b = rel(norm_gains), rel(norm_shifts), rel(out_biases)
    square = n_q == 4
    pair_places = [(j, i, 0, 2, False) for j, i in ((0, 0), (1, 0), (2, 0), (3, 0), (3, 1))]
    both = lax.optimization_barrier

    def flat(v):
        return v.reshape(v.shape[:-3] + (-1, v.shape[-1]))

    row_half = lambda v, which: half_of(v.reshape(own_images, n_mp, slots, width), which, 1)

    att_mine = jnp.concatenate([att_own, bias_terms])
    two = swap(att_mine, "mp", 2, "att_w_z2")
    one = swap(att_mine, "mp", 1, "att_w_z1")
    token_groups = image_groups(rel(tokens))
    sends = [for_route(token_groups, z, odd) for odd in (0, 1)]
    one, two, sends, ffn_own = both((one, two, sends, ffn_own))
    three = swap(two, "mp", 1, "att_w_z3")
    far_one, far_two = swap(ffn_own, "mp", 1, "ffn_w_z1"), swap(ffn_own, "mp", 2, "ffn_w_z2")
    att_z = jnp.stack([att_mine, one, two, three])
    bias_all = att_z[:, 4 * wq : 4 * wq + 3 * n_bias].astype(F32).reshape(n_i, 3, n_bias, he)
    bias_all = bias_all[:, 0] + (bias_all[:, 1] + bias_all[:, 2])
    bias_three = jnp.stack([bias_all[:, 0], jnp.zeros((n_i, he), F32), bias_all[:, 1]])
    bias_rows = jnp.transpose(bias_three.reshape(3, 2, 2, he), (1, 0, 2, 3)).reshape(1, -1)
    att_near = gather_near(att_z, "att_w") if square else ()
    far_one, far_two, sends, bias_rows = both((far_one, far_two, sends, bias_rows))
    far_three = swap(far_two, "mp", 1, "ffn_w_z3")
    token_rows = [to_image(sends[odd], odd, "tokens") for odd in (0, 1)]

    if square:
        att_far = gather_far(*att_near, "att_w")
        att_places = [(j, i, 0, 4, False) for j, i in ((0, 0), (1, 0), (2, 0), (3, 0), (3, 2))]
    else:
        att_far, att_places = (gather_plane(att_z, "att_w"),), [(0, 0, 0, 4, True)]
    cot = rel(jnp.where(keep_mine, cotangent, jnp.zeros_like(cotangent)))
    cot_groups = image_groups(cot)
    sends = [for_route(cot_groups, z, odd) for odd in (0, 1)]
    token_rows, att_far, far_three, sends = both((token_rows, att_far, far_three, sends))
    att_parts = [v[None] for v in (att_z, *att_near, *att_far)] if square else list(att_far)
    x = whole_rows(jnp.stack(token_rows, 1), "tokens_core")
    ffn_far = flat(jnp.stack([far_two, far_three]))
    x, ffn_far, sends = both((x, ffn_far, sends))
    far_near = gather_near(ffn_far, "ffn_w2") if square else ()
    cot_rows = [to_image(sends[odd], odd, "cotangent") for odd in (0, 1)]
    n1, qkva, qkvb, mixa, mixb, part = att_forward(
        x.reshape(own_images, all_slots, width),
        gains[0:1],
        shifts[0:1],
        bias_rows,
        meta,
        att_places,
        att_parts,
    )
    part, n1, x, far_near, cot_rows = both((part, n1, x, far_near, cot_rows))
    part_other = swap(part, "dp", 1, "attended")
    if square:
        far_far = gather_far(*far_near, "ffn_w2")
        parts0 = [v[None] for v in (ffn_far, *far_near, *far_far)]
        places = pair_places
    else:
        parts0, places = [gather_plane(ffn_far, "ffn_w2")], [(0, 0, 0, 2, True)]
    go = whole_rows(jnp.stack(cot_rows, 1), "cotangent_core")
    ffn_here = flat(jnp.stack([ffn_own, far_one]))
    go, parts0, part_other, ffn_here = both((go, parts0, part_other, ffn_here))
    here_near = gather_near(ffn_here, "ffn_w0") if square else ()
    up_rows = bias_all[:, 2:].reshape(n_i, fh)
    hidden, n2, n2t, got, sum_b, sum_g, upg1, *ffn_g0 = ffn_call(
        [x, part, part_other, out_b[0:1], gains[1:2], shifts[1:2], go, up_rows[2:], meta],
        n_q,
        2,
        fh,
        places,
        parts0,
        True,
        not square,
    )
    n2, ffn_g0, here_near = both((n2, ffn_g0, here_near))
    if square:
        parts1 = [v[None] for v in (ffn_here, *here_near, *gather_far(*here_near, "ffn_w0"))]
    else:
        parts1 = [gather_plane(ffn_here, "ffn_w0")]
    n2, parts1, ffn_g0 = both((n2, parts1, ffn_g0))
    reach_f0 = scatter_reach(ffn_g0, "ffn_g0")
    branch, gn2, upg0, *ffn_g1 = ffn_call(
        [n2, n2t, got, sum_b, sum_g, go, up_rows[:2], meta],
        n_q,
        2,
        fh,
        places,
        parts1,
        False,
        not square,
    )
    branch, gn2, ffn_g1, reach_f0 = both((branch, gn2, ffn_g1, reach_f0))

    last_f0 = scatter_last(ffn_g0, reach_f0, "ffn_g0")
    reach_f1 = scatter_reach(ffn_g1, "ffn_g1")
    gn2_other = swap(gn2, "dp", 1, "grad_norm_two")
    theirs = swap(row_half(branch, 1 - core), "dp", 1, "branch")
    gn2_other, theirs = both((gn2_other, theirs))
    out_half = row_half(hidden, core) + row_half(branch, core).astype(F32) + theirs.astype(F32) + out_b[1]
    gn2_other, out_half = both((gn2_other, rel(out_half.astype(BF))))
    out_first = from_image(out_half, z, 0, "block_out")
    gh, ght, gmixa, gmixb, sums = hidden_backward(
        meta, hidden, gn2, gn2_other, gains[1:2], go, n_q, att_places, att_parts
    )
    gmixa, last_f0, out_first, out_half = both((gmixa, last_f0, out_first, out_half))
    ffn2, ffn3 = scatter_sum(ffn_g0, reach_f0, last_f0)
    ffn_three = swap(ffn3, "mp", 1, "ffn_g_z3")
    out_last = from_image(out_half, z, 1, "block_out")
    gmixa, ffn2 = both((gmixa, ffn2))
    n1t, gqa, bias_a, *att_ga = att_backward_first(
        meta, gmixa, ght, n1, qkva, mixa, n_q, not square
    )
    n1t, gqa, reach_f1, ffn_three, out_last, att_ga = both(
        (n1t, gqa, reach_f1, ffn_three, out_last, att_ga)
    )
    reach_aa = scatter_reach(att_ga, "att_ga")
    last_f1 = scatter_last(ffn_g1, reach_f1, "ffn_g1")
    ffn_two = swap(add(ffn2, ffn_three), "mp", 2, "ffn_g_z2")
    gn1, bias_b, more_sums, *att_gb = att_backward_last(
        meta, x, gmixb, ght, n1t, gqa, qkvb, mixb, n_q, att_places, att_parts, not square
    )
    gn1, last_f1, att_gb, x, ffn_two, reach_aa = both((gn1, last_f1, att_gb, x, ffn_two, reach_aa))

    reach_ab = scatter_reach(att_gb, "att_gb")
    gn1_other = swap(row_half(gn1, 1 - core), "dp", 1, "grad_norm_one")
    ffn0, ffn1 = scatter_sum(ffn_g1, reach_f1, last_f1)
    ffn_one = swap(ffn1, "mp", 1, "ffn_g_z1")
    gn1 = row_half(gn1, core).astype(F32) + gn1_other.astype(F32)
    hat1, inv1 = normalise(after(row_half(x, core), gn1_other).astype(F32))
    input_half = row_half(gh, core) + norm_back(hat1, inv1, gains[0], gn1)
    input_half = rel(input_half.astype(BF))
    in_first = from_image(input_half, z, 0, "input_grad")
    reach_ab, input_half, in_first, upg0, upg1, bias_a, bias_b, sums, more_sums, reach_aa = both(
        (reach_ab, input_half, in_first, upg0, upg1, bias_a, bias_b, sums, more_sums, reach_aa)
    )
    in_last = from_image(input_half, z, 1, "input_grad")
    last_ab = scatter_last(att_gb, reach_ab, "att_gb")
    last_aa = scatter_last(att_ga, reach_aa, "att_ga")

    def placed(values):
        mine = jnp.concatenate([lax.dynamic_slice_in_dim(values, z ^ i, 1, 0) for i in range(n_i)])
        return jnp.stack([jnp.where(core == c, mine, jnp.zeros_like(mine)) for c in range(2)], 1)

    bias_a, bias_b = (v.reshape(3, 2, he) for v in (bias_a, bias_b))
    wide = [placed(jnp.concatenate([bias_a[t], bias_b[t]])) for t in (0, 2)]
    wide.append(placed(jnp.concatenate([upg0, upg1])))
    values = [*wide, rel(sums), rel(more_sums)]
    vector = jnp.concatenate([v.reshape(-1, 128) for v in values])
    last_ab, last_aa, vector, ffn_one = both((last_ab, last_aa, vector, ffn_one))
    att0, att1 = scatter_sum(att_ga, reach_aa, last_aa)
    att2, att3 = scatter_sum(att_gb, reach_ab, last_ab)
    att_three = swap(att3, "mp", 1, "att_g_z3")
    att_one = swap(att1, "mp", 1, "att_g_z1")
    vector = vector + swap(vector, "dp", 2, "sums_dp2")
    bit = 4
    while bit < n_dp:
        vector = vector + swap(vector, "dp", bit, "sums_dp" + str(bit))
        bit *= 2
    ffn_grad = add(ffn0, ffn_one, ffn_two)
    att_three, vector, in_last, ffn_grad = both((att_three, vector, in_last, ffn_grad))
    att_two = swap(add(att2, att_three), "mp", 2, "att_g_z2")
    vector = vector + swap(vector, "dp", 1, "sums_core")
    for bit in (1, 2):
        vector = vector + swap(vector, "mp", bit, "sums_z" + str(bit))
    att_grad = add(att0, att_one, att_two)
    in_routes = [in_first, in_last]
    block_out = joined_images([out_first, out_last], z)
    block_out = jnp.where(keep_mine, block_out, jnp.zeros_like(block_out))
    input_grad = joined_images(in_routes, z)

    def own_shard(grad, what):
        kinds, _, last = grad.shape
        pair = grad.reshape(kinds, 2, wq // 2, last)
        keep = lax.dynamic_index_in_dim(pair, core, 1, False)
        got = swap(lax.dynamic_index_in_dim(pair, 1 - core, 1, False), "dp", 1, what)
        return ordered_pair(keep, got, core, 2).reshape(kinds, wq // 2, 2 * last).astype(F32)

    att_shard, ffn_shard = own_shard(att_grad, "att_g_core"), own_shard(ffn_grad, "ffn_g_core")
    qkv_owned, proj_owned = att_shard[:3], jnp.transpose(att_shard[3])
    up_owned, down_owned = ffn_shard[0], jnp.transpose(ffn_shard[1])

    ends = [0]
    for v in values:
        ends.append(ends[-1] + v.size // 128)
    *wide, sums, more_sums = [
        vector[start:end].reshape(v.shape) for v, start, end in zip(values, ends, ends[1:])
    ]
    wide = [lax.dynamic_index_in_dim(v, z, 0, False).reshape(-1) for v in wide]
    bias_grad, upbias_grad = jnp.stack(wide[:2]), wide[2]
    gains_grad = jnp.stack([more_sums[0], sums[0] * 0.5])
    shifts_grad = jnp.stack([more_sums[1], sums[1] * 0.5])
    outbias_grad = sums[2:4] * 0.5
    return (
        block_out,
        input_grad,
        gains_grad,
        shifts_grad,
        qkv_owned,
        bias_grad,
        proj_owned,
        outbias_grad,
        up_owned,
        upbias_grad,
        down_owned,
    )


def solution(mesh):
    split = P("mp", "dp", None)
    return jax.shard_map(
        local,
        mesh=mesh,
        in_specs=(
            split,
            P("dp"),
            P(),
            P(),
            P(None, "dp", "mp"),
            P(None, "mp"),
            P("mp", "dp"),
            P(),
            P("dp", "mp"),
            P("mp"),
            P("mp", "dp"),
            split,
        ),
        out_specs=(
            split,
            split,
            P(),
            P(),
            P(None, "dp", "mp"),
            P(None, "mp"),
            P("mp", "dp"),
            P(),
            P("dp", "mp"),
            P("mp"),
            P("mp", "dp"),
        ),
        check_vma=False,
    )
```

```python
import functools

import jax
import jax.numpy as jnp
from jax import lax
from jax.experimental import pallas as pl
from jax.experimental.pallas import tpu as pltpu
from jax.sharding import PartitionSpec as P

HEAD = 64
BUF = 64
BF = jnp.bfloat16
F32 = jnp.float32
epsilon = 1e-06
masked_score = -1e30
MIB = 1 << 20
NT = (((1,), (1,)), ((), ()))
NN = (((1,), (0,)), ((), ()))
TN = (((0,), (0,)), ((), ()))
factor = HEAD ** (-0.5)
VMEM_SPEC = pl.BlockSpec(memory_space=pltpu.VMEM)
ANY_SPEC = pl.BlockSpec(memory_space=pl.ANY)
SMEM_SPEC = pl.BlockSpec(memory_space=pltpu.SMEM)


def mm(a, b, dims=NN):
    return lax.dot_general(a, b, dims, preferred_element_type=F32)


def normalise(values):
    average = jnp.mean(values, axis=-1, keepdims=True)
    centred = values - average
    spread = jnp.mean(centred * centred, axis=-1, keepdims=True)
    inv = lax.rsqrt(spread + epsilon)
    return centred * inv, inv


def norm_back(n, inv, scales, grad):
    e = grad * scales
    mean_e = jnp.mean(e, axis=-1, keepdims=True)
    mean_en = jnp.mean(e * n, axis=-1, keepdims=True)
    return (e - mean_e - n * mean_en) * inv


def gelu_parts(inputs):
    normal_cdf = 0.5 + 0.5 * lax.erf(inputs * 0.7071067811865476)
    density = jnp.exp(-0.5 * inputs * inputs) * 0.3989422804014327
    return inputs * normal_cdf, normal_cdf + inputs * density


def for_each(count, step):
    if count <= 4:
        for index in range(count):
            step(index)
    else:
        pl.loop(0, count)(step)


def valid_slots(meta_ref, image, slots, axis):
    shape = (slots, 1) if axis == 0 else (1, slots)
    row = lax.broadcasted_iota(jnp.int32, shape, axis)
    n = slots // 4
    k = (row >= n).astype(jnp.int32) + (row >= 2 * n) + (row >= 3 * n)
    slot = (k ^ meta_ref[3]) * n + (row - k * n)
    return slot < BUF + meta_ref[image]


def block_rows(jj, size):
    start = jj * size
    return pl.ds(start if isinstance(jj, int) else pl.multiple_of(start, size), size)


def load_blocks(parts, refs, q, kinds, wq, wanted, place, sem):
    for (j0, i0, t0, count, absolute), ref in zip(parts, refs):
        nj, ni = ref.shape[:2]

        def one(jj, ref=ref, j0=j0, i0=i0, t0=t0, count=count, absolute=absolute, ni=ni):
            source = jj ^ q if absolute else jj
            for ii in range(ni):
                if i0 + ii not in wanted:
                    continue
                for t in range(t0, t0 + count):
                    if t in kinds:
                        pltpu.make_async_copy(
                            ref.at[source, ii, pl.ds((t - t0) * wq, wq)],
                            place(block_rows(j0 + jj, wq), i0 + ii, t),
                            sem,
                        ).start()

        for_each(nj, one)


def store_blocks(refs, q, n_j, block, i, sem):
    def start(views, target):
        for t, view in enumerate(views):
            pltpu.make_async_copy(view, target.at[t], sem).start()

    if len(refs) == 1:
        for_each(n_j, lambda jj: start(block(jj), refs[0].at[jj ^ q, i]))
        return
    own, to_x, to_y, keep_x, keep_y = refs
    start(block(0), own.at[i])
    if i == 0:
        start(block(1), keep_x.at[0])
        start(block(2), to_y.at[1])
        start(block(3), to_y.at[0])
    else:
        start(block(1), to_x.at[1])
        start(block(2), keep_y.at[0])
        start(block(3), to_x.at[0])


def grad_shapes(n_j, n_i, absolute, block):
    shape = lambda *lead: jax.ShapeDtypeStruct(lead + block, BF)
    if absolute:
        return [shape(n_j, n_i)]
    return [shape(2), shape(2), shape(2), shape(1), shape(1)]


def att_column(n_i, i, t):
    he = 2 * HEAD
    if t == 3:
        return 3 * n_i * he + i * he
    return (i // 2) * 6 * he + (t * 2 + i % 2) * he


def att_fwd_kernel(parts, n_i, x_ref, g_ref, c_ref, bias_ref, meta_ref, *rest):
    w_refs = rest[: len(parts)]
    n1_ref, qkva_ref, qkvb_ref, mixa_ref, mixb_ref, part_ref, w_scr, m_scr, sem = rest[len(parts) :]
    he = 2 * HEAD
    width = w_scr.shape[0]
    image = pl.program_id(0)

    @pl.when(image == 0)
    def _():
        place = lambda rows, i, t: w_scr.at[rows, pl.ds(att_column(n_i, i, t), he)]
        wq = width // max(p[0] + r.shape[0] for p, r in zip(parts, w_refs))
        load_blocks(parts, w_refs, meta_ref[4], range(4), wq, range(n_i), place, sem)
        pltpu.make_async_copy(w_scr, w_scr, sem).wait()

    hat, _ = normalise(x_ref[0].astype(F32))
    n1 = (hat * g_ref[...] + c_ref[...]).astype(BF)
    n1_ref[...] = n1
    qkv_refs = (qkva_ref, qkvb_ref)
    for half in range(2):
        cols = pl.ds(half * 6 * he, 6 * he)
        res = (mm(n1, w_scr[:, cols]) + bias_ref[:, cols]).astype(BF)
        for n in range(6):
            qkv_refs[half][n] = res[:, n * he : (n + 1) * he]
    bias = jnp.where(valid_slots(meta_ref, image, x_ref.shape[1], 1), 0.0, masked_score)
    lane = lax.broadcasted_iota(jnp.int32, (1, he), 1)
    low_half = lane < HEAD
    for i in range(n_i):
        ref = qkv_refs[i // 2]
        q2, k2, v2 = (ref[t * 2 + i % 2] for t in range(3))
        outs = []
        for h in range(2):
            qm = jnp.where(low_half if h == 0 else ~low_half, q2, jnp.zeros_like(q2))
            s = mm(qm, k2, NT) * factor + bias
            top = jnp.max(s, axis=-1, keepdims=True)
            p = jnp.exp(s - top)
            w = (p / jnp.sum(p, axis=-1, keepdims=True)).astype(BF)
            outs.append(mm(w, v2))
        mixed = jnp.where(low_half, outs[0], outs[1]).astype(BF)
        m_scr[:, i * he : (i + 1) * he] = mixed
    mixa_ref[...] = m_scr[:, : 2 * he]
    mixb_ref[...] = m_scr[:, 2 * he :]
    part_ref[...] = mm(m_scr[...], w_scr[:, 3 * n_i * he :], NT).astype(BF)


def att_forward(x, gain, shift, bias, meta, parts, arrays):
    images, slots, width = x.shape
    n_i = 4
    he = 2 * HEAD
    rows = images * slots
    row_block = lambda last: pl.BlockSpec((slots, last), lambda a: (a, 0))
    whole = lambda *shape: pl.BlockSpec(shape, lambda a: (0,) * len(shape))
    qkv_block = pl.BlockSpec((6, slots, he), lambda a: (0, a, 0))
    return pl.pallas_call(
        functools.partial(att_fwd_kernel, parts, n_i),
        grid=(images,),
        in_specs=[
            pl.BlockSpec((1, slots, width), lambda a: (a, 0, 0)),
            whole(1, width),
            whole(1, width),
            whole(1, 3 * n_i * he),
            SMEM_SPEC,
        ]
        + [ANY_SPEC] * len(arrays),
        out_specs=[row_block(width), qkv_block, qkv_block, row_block(2 * he), row_block(2 * he), row_block(width)],
        out_shape=[
            jax.ShapeDtypeStruct((rows, width), BF),
            jax.ShapeDtypeStruct((6, rows, he), BF),
            jax.ShapeDtypeStruct((6, rows, he), BF),
            jax.ShapeDtypeStruct((rows, 2 * he), BF),
            jax.ShapeDtypeStruct((rows, 2 * he), BF),
            jax.ShapeDtypeStruct((rows, width), BF),
        ],
        scratch_shapes=[
            pltpu.VMEM((width, 4 * n_i * he), BF),
            pltpu.VMEM((slots, n_i * he), BF),
            pltpu.SemaphoreType.DMA,
        ],
        compiler_params=pltpu.CompilerParams(vmem_limit_bytes=48 * MIB),
        cost_estimate=pl.CostEstimate(flops=16_000_000_000, bytes_accessed=20_000_000, transcendentals=2_500_000),
        name="att_forward",
    )(x, gain, shift, bias, meta, *arrays)


def ffn_kernel(parts, n_i, n_j, n_out, first, *refs):
    if first:
        x_ref, pa_ref, pb_ref, b_ref, g_ref, c_ref = refs[:6]
        refs = refs[6:]
    else:
        kept, refs = refs[:5], refs[5:]
    go_ref, upb_ref, meta_ref = refs[:3]
    w_refs, refs = refs[3 : 3 + len(parts)], refs[3 + len(parts) :]
    q = meta_ref[4]
    if first:
        hidden_out, refs = refs[0], refs[1:]
        kept, refs = refs[:5], refs[5:]
        sum_outs = kept[3:]
    else:
        sum_outs, refs = refs[:2], refs[2:]
    upg_ref, refs = refs[0], refs[1:]
    grad_refs, refs = refs[:n_out], refs[n_out:]
    n2, n2t, got, run_b, run_g, wbuf, gbuf, act_s, pre_s, wsem, gsem, ksem, ssem = refs[:13]
    held = (n2, n2t, got, run_b, run_g)
    if first:
        hidden, hsem = refs[13:]
        low_sums = (run_b, run_g)
    else:
        low_sums = refs[13:]
    rows, width = go_ref.shape
    wq = width // n_j
    rb = rows // 3

    def fetch(i, slot):
        place = lambda rws, _, t: wbuf.at[slot, t, rws]
        load_blocks(parts, w_refs, q, range(2), wq, (i,), place, wsem.at[slot])

    def fetched(slot):
        pltpu.make_async_copy(wbuf.at[slot], wbuf.at[slot], wsem.at[slot]).wait()

    def put(i, slot):
        block = lambda jj: [gbuf.at[slot, t, block_rows(jj, wq)] for t in range(2)]
        store_blocks(grad_refs, q, n_j, block, i, gsem.at[slot])

    def stored(slot):
        pltpu.make_async_copy(gbuf.at[slot], gbuf.at[slot], gsem.at[slot]).wait()

    def keep(n):
        if first:
            return pltpu.make_async_copy(held[n], kept[n], ksem.at[n])
        return pltpu.make_async_copy(kept[n], held[n], ksem.at[n])

    fetch(0, 0)
    if first:
        block = 192

        @pl.loop(0, rows // block)
        def _(r):
            rw = pl.ds(pl.multiple_of(r * block, block), block)
            h = (
                x_ref[rw, :].astype(F32)
                + (pa_ref[rw, :].astype(F32) + pb_ref[rw, :].astype(F32))
                + b_ref[...]
            )
            hidden[rw, :] = h
            hat, _ = normalise(h)
            n2[rw, :] = (hat * g_ref[...] + c_ref[...]).astype(BF)

        pltpu.make_async_copy(hidden, hidden_out, hsem).start()
        keep(0).start()
        n2t[...] = n2[...].T
        keep(1).start()
        got[...] = go_ref[...].T
        keep(2).start()
    else:
        for n in (0, 3, 4, 1, 2):
            keep(n).start()
        keep(0).wait()
    for i in range(n_i):
        slot = i % 2
        if i + 1 < n_i:
            fetch(i + 1, 1 - slot)
        fetched(slot)
        if i == 0 and not first:
            keep(3).wait()
            keep(4).wait()

        @pl.loop(0, 3)
        def _(r, i=i, slot=slot):
            rw = pl.ds(pl.multiple_of(r * rb, rb), rb)
            u, w = wbuf[slot, 0], wbuf[slot, 1]
            up = mm(n2[rw, :], u) + upb_ref[i : i + 1, :]
            act, slope = gelu_parts(up)
            act = act.astype(BF)
            act_s[rw, :] = act
            pre = (mm(go_ref[rw, :], w) * slope).astype(BF)
            pre_s[rw, :] = pre
            down = mm(act, w, NT)
            back = mm(pre, u, NT)
            if i > 0 or not first:
                down += run_b[rw, :]
                back += run_g[rw, :]
            if i < n_i - 1:
                run_b[rw, :] = down
                run_g[rw, :] = back
            else:
                for n, total in enumerate((down, back)):
                    low_sums[n][rw, :] = total.astype(low_sums[n].dtype)
                    pltpu.make_async_copy(low_sums[n].at[rw], sum_outs[n].at[rw], ssem.at[n]).start()

        if i == 0 and not first:
            keep(1).wait()
            keep(2).wait()
        upg_ref[i : i + 1, :] = jnp.sum(pre_s[...].astype(F32), axis=0, keepdims=True)
        if i >= 2:
            stored(slot)
        gbuf[slot, 0] = mm(n2t[...], pre_s[...]).astype(BF)
        gbuf[slot, 1] = mm(got[...], act_s[...]).astype(BF)
        put(i, slot)
    for n in range(2):
        pltpu.make_async_copy(low_sums[n], sum_outs[n], ssem.at[n]).wait()
    if first:
        pltpu.make_async_copy(hidden, hidden_out, hsem).wait()
        for n in range(3):
            keep(n).wait()
    for i in range(max(n_i - 2, 0), n_i):
        stored(i % 2)


def ffn_call(ins, n_j, n_i, fh, parts, arrays, first, absolute):
    go = ins[-3]
    rows, width = go.shape
    wq = width // n_j
    wide, low, turned = (rows, width, F32), (rows, width, BF), (width, rows, BF)
    outs = [wide, low, turned, turned, wide, wide] if first else [low, low]
    grads = grad_shapes(n_j, n_i, absolute, (2, wq, fh))
    if first:
        in_specs = [VMEM_SPEC] * (len(ins) - 1)
    else:
        in_specs = [ANY_SPEC] * 5 + [VMEM_SPEC] * 2
    extra = (
        [pltpu.VMEM((rows, width), F32), pltpu.SemaphoreType.DMA]
        if first
        else [pltpu.VMEM((rows, width), BF)] * 2
    )
    return pl.pallas_call(
        functools.partial(ffn_kernel, parts, n_i, n_j, len(grads), first),
        in_specs=in_specs + [SMEM_SPEC] + [ANY_SPEC] * len(arrays),
        out_specs=[ANY_SPEC] * len(outs) + [VMEM_SPEC] + [ANY_SPEC] * len(grads),
        out_shape=[jax.ShapeDtypeStruct((m, n), kind) for m, n, kind in outs]
        + [jax.ShapeDtypeStruct((n_i, fh), F32)]
        + grads,
        scratch_shapes=[
            pltpu.VMEM((rows, width), BF),
            pltpu.VMEM((width, rows), BF),
            pltpu.VMEM((width, rows), BF),
            pltpu.VMEM((rows, width), F32),
            pltpu.VMEM((rows, width), F32),
            pltpu.VMEM((2, 2, width, fh), BF),
            pltpu.VMEM((2, 2, width, fh), BF),
            pltpu.VMEM((rows, fh), BF),
            pltpu.VMEM((rows, fh), BF),
            pltpu.SemaphoreType.DMA((2,)),
            pltpu.SemaphoreType.DMA((2,)),
            pltpu.SemaphoreType.DMA((5,)),
            pltpu.SemaphoreType.DMA((2,)),
        ]
        + extra,
        compiler_params=pltpu.CompilerParams(vmem_limit_bytes=56 * MIB),
        cost_estimate=pl.CostEstimate(
            flops=12_000_000_000 * n_i, bytes_accessed=30_000_000, transcendentals=1_000_000 * n_i
        ),
        name="ffn_first" if first else "ffn_last",
    )(*ins, *arrays)


def att_back_blocks(meta_ref, qkv_ref, gmix, gq, rows, which):
    he = 2 * HEAD
    images = 3
    slots = rows // images
    lane = lax.broadcasted_iota(jnp.int32, (1, he), 1)
    low_half = lane < HEAD

    @pl.loop(0, images)
    def _(a):
        rw = pl.ds(pl.multiple_of(a * slots, slots), slots)
        bias = jnp.where(valid_slots(meta_ref, a, slots, 0), 0.0, masked_score)
        for i in range(2):
            q2, k2, v2 = (qkv_ref[t * 2 + i, rw, :] for t in range(3))
            g2 = gmix[which + i, rw, :]
            dq, dk, dv = [], [], []
            for h in range(2):
                here = low_half if h == 0 else ~low_half
                qm = jnp.where(here, q2, jnp.zeros_like(q2))
                gm = jnp.where(here, g2, jnp.zeros_like(g2))
                st = mm(k2, qm, NT) * factor + bias
                top = jnp.max(st, axis=0, keepdims=True)
                p = jnp.exp(st - top)
                p = p / jnp.sum(p, axis=0, keepdims=True)
                dpt = mm(v2, gm, NT)
                dot = jnp.sum(p * dpt, axis=0, keepdims=True)
                ds = (p * (dpt - dot)).astype(BF)
                dk.append(mm(ds, q2))
                dv.append(mm(p.astype(BF), g2))
                dq.append(mm(ds, k2, TN))
            for t, (pair, scale) in enumerate(((dq, factor), (dk, factor), (dv, 1.0))):
                both = jnp.where(low_half, pair[0], pair[1])
                gq[rw, (t * 2 + i) * he : (t * 2 + i + 1) * he] = (both * scale).astype(BF)


def put_att_grads(grad_refs, q, n_j, wq, gbuf, gsem):
    he = 2 * HEAD
    for i in range(2):
        block = lambda jj, i=i: [
            gbuf.at[t, block_rows(jj, wq), pl.ds(i * he, he)] for t in range(4)
        ]
        store_blocks(grad_refs, q, n_j, block, i, gsem)


def hidden_back_kernel(
    parts, n_i, n_j, meta_ref, hid_ref, ga_ref, gb_ref, g_ref, go_ref, *rest
):
    w_refs = rest[: len(parts)]
    gh_ref, ght, gmixa, gmixb, sums_ref = rest[len(parts) : len(parts) + 5]
    ghb, w_scr, sem = rest[len(parts) + 5 :]
    rows, width = hid_ref.shape
    he = 2 * HEAD
    place = lambda rws, i, t: w_scr.at[rws, pl.ds(i * he, he)]
    load_blocks(parts, w_refs, meta_ref[4], (3,), width // n_j, range(n_i), place, sem)
    sums_ref[...] = jnp.zeros_like(sums_ref)
    pltpu.make_async_copy(w_scr, w_scr, sem).wait()
    block = 192

    @pl.loop(0, rows // block)
    def _(r):
        rw = pl.ds(pl.multiple_of(r * block, block), block)
        hat, inv = normalise(hid_ref[rw, :])
        grad = ga_ref[rw, :].astype(F32) + gb_ref[rw, :].astype(F32)
        gout = go_ref[rw, :].astype(F32)
        gh = gout + norm_back(hat, inv, g_ref[...], grad)
        gh_ref[rw, :] = gh
        low = gh.astype(BF)
        ghb[rw, :] = low
        sums_ref[0:1, :] += jnp.sum(grad * hat, axis=0, keepdims=True)
        sums_ref[1:2, :] += jnp.sum(grad, axis=0, keepdims=True)
        sums_ref[2:3, :] += jnp.sum(gh, axis=0, keepdims=True)
        sums_ref[3:4, :] += jnp.sum(gout, axis=0, keepdims=True)
        res = mm(low, w_scr[...]).astype(BF)
        for i in range(n_i):
            (gmixa, gmixb)[i // 2][i % 2, rw, :] = res[:, i * he : (i + 1) * he]

    ght[...] = ghb[...].T


def hidden_backward(meta, hidden, ga, gb, gain, go, n_j, parts, arrays):
    rows, width = hidden.shape
    n_i, he = 4, 2 * HEAD
    return pl.pallas_call(
        functools.partial(hidden_back_kernel, parts, n_i, n_j),
        in_specs=[SMEM_SPEC] + [VMEM_SPEC] * 5 + [ANY_SPEC] * len(arrays),
        out_specs=[VMEM_SPEC] * 5,
        out_shape=[
            jax.ShapeDtypeStruct((rows, width), F32),
            jax.ShapeDtypeStruct((width, rows), BF),
            jax.ShapeDtypeStruct((2, rows, he), BF),
            jax.ShapeDtypeStruct((2, rows, he), BF),
            jax.ShapeDtypeStruct((8, width), F32),
        ],
        scratch_shapes=[
            pltpu.VMEM((rows, width), BF),
            pltpu.VMEM((width, n_i * he), BF),
            pltpu.SemaphoreType.DMA,
        ],
        compiler_params=pltpu.CompilerParams(vmem_limit_bytes=48 * MIB),
        cost_estimate=pl.CostEstimate(flops=10_000_000_000, bytes_accessed=20_000_000, transcendentals=0),
        name="hidden_backward",
    )(meta, hidden, ga, gb, gain, go, *arrays)


def att_bwd_first_kernel(n_i, n_j, n_out, meta_ref, gmix, ght, n1_ref, qkv_ref, mix_ref, *rest):
    n1t, gq, bias_ref = rest[:3]
    grad_refs = rest[3 : 3 + n_out]
    gbuf, gsem = rest[3 + n_out :]
    width, rows = ght.shape
    he = 2 * HEAD
    gbuf[3] = mm(ght[...], mix_ref[...]).astype(BF)
    att_back_blocks(meta_ref, qkv_ref, gmix, gq, rows, 0)
    n1t[...] = n1_ref[...].T
    for t in range(3):
        gbuf[t] = mm(n1t[...], gq[:, 2 * t * he : 2 * (t + 1) * he]).astype(BF)
    put_att_grads(grad_refs, meta_ref[4], n_j, width // n_j, gbuf, gsem)
    bias_ref[...] = jnp.sum(gq[...].astype(F32), axis=0, keepdims=True)
    pltpu.make_async_copy(gbuf, gbuf, gsem).wait()


def att_backward_first(meta, gmix, ght, n1, qkv, mix, n_j, absolute):
    width, rows = ght.shape
    n_i, he = 4, 2 * HEAD
    wq = width // n_j
    grads = grad_shapes(n_j, 2, absolute, (4, wq, he))
    return pl.pallas_call(
        functools.partial(att_bwd_first_kernel, n_i, n_j, len(grads)),
        in_specs=[SMEM_SPEC] + [VMEM_SPEC] * 5,
        out_specs=[VMEM_SPEC] * 3 + [ANY_SPEC] * len(grads),
        out_shape=[
            jax.ShapeDtypeStruct((width, rows), BF),
            jax.ShapeDtypeStruct((rows, 6 * he), BF),
            jax.ShapeDtypeStruct((1, 6 * he), F32),
        ]
        + grads,
        scratch_shapes=[pltpu.VMEM((4, width, 2 * he), BF), pltpu.SemaphoreType.DMA],
        compiler_params=pltpu.CompilerParams(vmem_limit_bytes=48 * MIB),
        cost_estimate=pl.CostEstimate(flops=16_000_000_000, bytes_accessed=20_000_000, transcendentals=1_250_000),
        name="att_backward_first",
    )(meta, gmix, ght, n1, qkv, mix)


def att_bwd_last_kernel(
    parts, n_i, n_j, n_out, meta_ref, x_ref, gmix, ght, n1t, gqa_ref, qkv_ref, mix_ref, *rest
):
    w_refs = rest[: len(parts)]
    gn1_ref, bias_ref, sums_ref = rest[len(parts) : len(parts) + 3]
    rest = rest[len(parts) + 3 :]
    grad_refs = rest[:n_out]
    gq, w_scr, gbuf, sem, gsem = rest[n_out:]
    rows, width = x_ref.shape
    he = 2 * HEAD
    wq = width // n_j
    q = meta_ref[4]
    place = lambda rws, i, t: w_scr.at[rws, pl.ds(att_column(n_i, i, t), he)]
    load_blocks(parts, w_refs, q, (0, 1, 2), wq, range(n_i), place, sem)
    gbuf[3] = mm(ght[...], mix_ref[...]).astype(BF)
    att_back_blocks(meta_ref, qkv_ref, gmix, gq, rows, 0)
    for t in range(3):
        gbuf[t] = mm(n1t[...], gq[:, 2 * t * he : 2 * (t + 1) * he]).astype(BF)
    put_att_grads(grad_refs, q, n_j, wq, gbuf, gsem)
    bias_ref[...] = jnp.sum(gq[...].astype(F32), axis=0, keepdims=True)
    sums_ref[...] = jnp.zeros_like(sums_ref)
    pltpu.make_async_copy(w_scr, w_scr, sem).wait()
    rb = rows // 3

    @pl.loop(0, 3)
    def _(r):
        rw = pl.ds(pl.multiple_of(r * rb, rb), rb)
        grad = mm(gqa_ref[rw, :], w_scr[:, : 6 * he], NT) + mm(gq[rw, :], w_scr[:, 6 * he :], NT)
        gn1_ref[rw, :] = grad.astype(BF)
        hat, _ = normalise(x_ref[rw, :].astype(F32))
        sums_ref[0:1, :] += jnp.sum(grad * hat, axis=0, keepdims=True)
        sums_ref[1:2, :] += jnp.sum(grad, axis=0, keepdims=True)

    pltpu.make_async_copy(gbuf, gbuf, gsem).wait()


def att_backward_last(meta, x, gmix, ght, n1t, gqa, qkv, mix, n_j, parts, arrays, absolute):
    rows, width = x.shape
    n_i, he = 4, 2 * HEAD
    wq = width // n_j
    grads = grad_shapes(n_j, 2, absolute, (4, wq, he))
    return pl.pallas_call(
        functools.partial(att_bwd_last_kernel, parts, n_i, n_j, len(grads)),
        in_specs=[SMEM_SPEC] + [VMEM_SPEC] * 7 + [ANY_SPEC] * len(arrays),
        out_specs=[VMEM_SPEC] * 3 + [ANY_SPEC] * len(grads),
        out_shape=[
            jax.ShapeDtypeStruct((rows, width), BF),
            jax.ShapeDtypeStruct((1, 6 * he), F32),
            jax.ShapeDtypeStruct((8, width), F32),
        ]
        + grads,
        scratch_shapes=[
            pltpu.VMEM((rows, 6 * he), BF),
            pltpu.VMEM((width, 3 * n_i * he), BF),
            pltpu.VMEM((4, width, 2 * he), BF),
            pltpu.SemaphoreType.DMA,
            pltpu.SemaphoreType.DMA,
        ],
        compiler_params=pltpu.CompilerParams(vmem_limit_bytes=56 * MIB),
        cost_estimate=pl.CostEstimate(flops=20_000_000_000, bytes_accessed=30_000_000, transcendentals=1_250_000),
        name="att_backward_last",
    )(meta, x, gmix, ght, n1t, gqa, qkv, mix, *arrays)


def swap(x, axis, bits, what):
    n = lax.axis_size(axis)
    with jax.named_scope(what):
        return lax.ppermute(x, axis, [(i, i ^ bits) for i in range(n)])


def after(x, *deps):
    return lax.optimization_barrier((x,) + deps)[0] if deps else x


def add(*parts):
    total = parts[0].astype(F32)
    for part in parts[1:]:
        total = total + part.astype(F32)
    return total.astype(parts[0].dtype)


def planes():
    n_dp = lax.axis_size("dp")
    return [list(range(core, n_dp, 2)) for core in range(2)]


def gather_plane(block, what):
    with jax.named_scope(what):
        return lax.all_gather(block, "dp", axis_index_groups=planes())


def scatter_plane(blocks, what):
    flat = blocks.reshape(-1, blocks.shape[-1])
    with jax.named_scope(what):
        mine = lax.psum_scatter(
            flat, "dp", scatter_dimension=0, axis_index_groups=planes(), tiled=True
        )
    return mine.reshape(blocks.shape[1:])


def gather_near(own, what):
    return swap(own, "dp", 2, what + "_x1"), swap(own, "dp", 4, what + "_y1")


def gather_far(one, two, what):
    half = one.shape[0] // 2
    return swap(one[:half], "dp", 4, what + "_y2"), swap(two[half:], "dp", 2, what + "_x2")


def scatter_reach(grads, what):
    if len(grads) == 1:
        return (scatter_plane(grads[0], what),)
    _, to_x, to_y, _, _ = grads
    return swap(to_x, "dp", 2, what + "_x1"), swap(to_y, "dp", 4, what + "_y1")


def scatter_last(grads, reach, what):
    if len(grads) == 1:
        return ()
    from_x, from_y = reach
    _, _, _, keep_x, keep_y = grads
    on_x, on_y = add(keep_x, from_y[0::2]), add(keep_y, from_x[0::2])
    return swap(on_x, "dp", 2, what + "_x2"), swap(on_y, "dp", 4, what + "_y2")


def scatter_sum(grads, reach, last):
    if len(grads) == 1:
        return [reach[0][i] for i in range(reach[0].shape[0])]
    own = grads[0]
    return [
        add(own[i], reach[1 - i % 2][i + 1 - i % 2], last[i % 2][i // 2]) for i in range(own.shape[0])
    ]


def gather_z(own, what):
    two = swap(own, "mp", 2, what + "_z2")
    one = swap(own, "mp", 1, what + "_z1")
    return one, two, swap(two, "mp", 1, what + "_z3")


def scatter_z(zero, one, two, three, what):
    two = add(two, swap(three, "mp", 1, what + "_z3"))
    return add(zero, swap(one, "mp", 1, what + "_z1"), swap(two, "mp", 2, what + "_z2"))


def ordered_pair(own, other, core, axis=0):
    return jnp.stack(
        [jnp.where(core == 0, own, other), jnp.where(core == 0, other, own)], axis
    )


def image_routes(n_dp, n_mp, odd):
    pairs = []
    for plane in range(n_dp // 2):
        for core in range(2):
            for z in range(n_mp):
                shift = 2 * core + odd
                worker = (plane * 2 + core) * n_mp + z
                holder = (plane * 2 + (z >> 1)) * n_mp + (z ^ shift)
                pairs.append((holder, worker))
    return pairs


def image_groups(x):
    slots, images, width = x.shape
    return jnp.transpose(x, (1, 0, 2)).reshape(2, images // 2, slots, width)


def for_route(groups, z, odd):
    return lax.dynamic_index_in_dim(groups, (z ^ odd) & 1, 0, False)


def to_image(send, odd, what):
    n_dp, n_mp = lax.axis_size("dp"), lax.axis_size("mp")
    with jax.named_scope(what + "_route" + str(odd)):
        return lax.ppermute(send, ("dp", "mp"), image_routes(n_dp, n_mp, odd))


def from_image(y, z, odd, what):
    n_dp, n_mp = lax.axis_size("dp"), lax.axis_size("mp")
    routes = [(b, a) for a, b in image_routes(n_dp, n_mp, odd)]
    with jax.named_scope(what + "_route" + str(odd)):
        return lax.ppermute(y[:, odd], ("dp", "mp"), routes)


def joined_images(back, z):
    flip = (z & 1) == 1
    groups = jnp.concatenate([jnp.where(flip, back[1], back[0]), jnp.where(flip, back[0], back[1])])
    return jnp.transpose(groups, (1, 0, 2))


def local(
    tokens,
    counts,
    norm_gains,
    norm_shifts,
    qkv_weight,
    qkv_bias,
    proj_weight,
    out_biases,
    up_weight,
    up_bias,
    down_weight,
    cotangent,
):
    slots, images, width = tokens.shape
    n_dp, n_mp = lax.axis_size("dp"), lax.axis_size("mp")
    n_q = n_dp // 2
    wq = width // n_q
    dp, z = lax.axis_index("dp"), lax.axis_index("mp")
    q, core = dp >> 1, dp & 1
    own_images = images // 2
    all_slots = slots * n_mp
    rows = own_images * all_slots

    def rel(v):
        blocks = [lax.dynamic_slice_in_dim(v, (q ^ j) * wq, wq, v.ndim - 1) for j in range(n_q)]
        return jnp.concatenate(blocks, -1)

    def half_of(v, which, axis):
        size = v.shape[axis] // 2
        return lax.dynamic_slice_in_dim(v, which * size, size, axis)

    att = jnp.concatenate([qkv_weight, jnp.transpose(proj_weight)[None]])
    ffn_w = jnp.stack([up_weight, jnp.transpose(down_weight)])
    he, fh = att.shape[-1] // 2, ffn_w.shape[-1] // 2

    count_rows = jnp.pad(counts.astype(BF)[None], ((0, 15), (0, he - images)))
    sent = jnp.concatenate([half_of(att, 1 - core, 2).reshape(-1, he), count_rows])
    got = swap(sent, "dp", 1, "att_w_core")
    other_counts = got[-16, :images].astype(jnp.int32)
    got = got[:-16].reshape(4, wq // 2, he)
    att_own = ordered_pair(half_of(att, core, 2), got, core, 1).reshape(-1, he)
    got = swap(half_of(ffn_w, 1 - core, 2), "dp", 1, "ffn_w_core")
    ffn_own = ordered_pair(half_of(ffn_w, core, 2), got, core, 1).reshape(2, wq, fh)
    left = jnp.concatenate(
        [half_of(qkv_bias, core, 1), half_of(up_bias, core, 0).reshape(-1, he)]
    )
    n_bias = left.shape[0]
    terms = []
    for _ in range(3):
        term = lax.reduce_precision(left, 8, 7)
        terms.append(term.astype(BF))
        left = left - term
    bias_pad = -(-3 * n_bias // 16) * 16
    bias_terms = jnp.pad(jnp.concatenate(terms), ((0, bias_pad - 3 * n_bias), (0, 0)))

    counts_here = jnp.where((z >> 1) == core, counts, other_counts)
    counts_here = lax.dynamic_slice_in_dim(counts_here, (z & 1) * own_images, own_images, 0)
    meta = jnp.concatenate([counts_here, z[None], q[None]])
    slot_ids = jnp.arange(slots, dtype=jnp.int32)
    keep_mine = ((z * slots + slot_ids)[:, None] < BUF + counts[None, :])[:, :, None]

    def whole_rows(got, what):
        return ordered_pair(got, swap(got, "dp", 1, what), core, 1).reshape(rows, width)

    n_i = n_mp
    gains, shifts, out_b = rel(norm_gains), rel(norm_shifts), rel(out_biases)
    square = n_q == 4
    pair_places = [(j, i, 0, 2, False) for j, i in ((0, 0), (1, 0), (2, 0), (3, 0), (3, 1))]
    both = lax.optimization_barrier

    def flat(v):
        return v.reshape(v.shape[:-3] + (-1, v.shape[-1]))

    row_half = lambda v, which: half_of(v.reshape(own_images, n_mp, slots, width), which, 1)

    att_mine = jnp.concatenate([att_own, bias_terms])
    two = swap(att_mine, "mp", 2, "att_w_z2")
    one = swap(att_mine, "mp", 1, "att_w_z1")
    token_groups = image_groups(rel(tokens))
    sends = [for_route(token_groups, z, odd) for odd in (0, 1)]
    own_near = gather_near(ffn_own, "ffn_w0") if square else ()
    one, two, sends, ffn_own = both((one, two, sends, ffn_own))
    three = swap(two, "mp", 1, "att_w_z3")
    far_two = swap(ffn_own, "mp", 2, "ffn_w_z2")
    att_z = jnp.stack([att_mine, one, two, three])
    bias_all = att_z[:, 4 * wq : 4 * wq + 3 * n_bias].astype(F32).reshape(n_i, 3, n_bias, he)
    bias_all = bias_all[:, 0] + (bias_all[:, 1] + bias_all[:, 2])
    bias_three = jnp.stack([bias_all[:, 0], jnp.zeros((n_i, he), F32), bias_all[:, 1]])
    bias_rows = jnp.transpose(bias_three.reshape(3, 2, 2, he), (1, 0, 2, 3)).reshape(1, -1)
    att_near = gather_near(after(att_z, *own_near), "att_w") if square else ()
    own_far = gather_far(*own_near, "ffn_w0") if square else ()
    far_two, sends, bias_rows = both((far_two, sends, bias_rows))
    far_three = swap(far_two, "mp", 1, "ffn_w_z3")
    token_rows = [to_image(sends[odd], odd, "tokens") for odd in (0, 1)]

    if square:
        att_far = gather_far(*att_near, "att_w")
        att_places = [(j, i, 0, 4, False) for j, i in ((0, 0), (1, 0), (2, 0), (3, 0), (3, 2))]
    else:
        att_far, att_places = (gather_plane(att_z, "att_w"),), [(0, 0, 0, 4, True)]
    cot = rel(jnp.where(keep_mine, cotangent, jnp.zeros_like(cotangent)))
    cot_groups = image_groups(cot)
    sends = [for_route(cot_groups, z, odd) for odd in (0, 1)]
    token_rows, att_far, far_three, sends, own_far = both(
        (token_rows, att_far, far_three, sends, own_far)
    )
    far_one = swap(after(ffn_own, *token_rows), "mp", 1, "ffn_w_z1")
    att_parts = [v[None] for v in (att_z, *att_near, *att_far)] if square else list(att_far)
    x = whole_rows(jnp.stack(token_rows, 1), "tokens_core")
    ffn_far = flat(jnp.stack([far_two, far_three]))
    x, ffn_far, sends = both((x, ffn_far, sends))
    far_near = gather_near(ffn_far, "ffn_w2") if square else ()
    cot_rows = [to_image(sends[odd], odd, "cotangent") for odd in (0, 1)]
    n1, qkva, qkvb, mixa, mixb, part = att_forward(
        x.reshape(own_images, all_slots, width),
        gains[0:1],
        shifts[0:1],
        bias_rows,
        meta,
        att_places,
        att_parts,
    )
    part, n1, x, far_near, cot_rows, far_one = both((part, n1, x, far_near, cot_rows, far_one))
    part_other = swap(part, "dp", 1, "attended")
    if square:
        far_far = gather_far(*far_near, "ffn_w2")
        parts0 = [v[None] for v in (ffn_far, *far_near, *far_far)]
        places = pair_places
    else:
        parts0, places = [gather_plane(ffn_far, "ffn_w2")], [(0, 0, 0, 2, True)]
    go = whole_rows(jnp.stack(cot_rows, 1), "cotangent_core")
    go, parts0, part_other, far_one = both((go, parts0, part_other, far_one))
    here_near = gather_near(far_one, "ffn_w1") if square else ()
    up_rows = bias_all[:, 2:].reshape(n_i, fh)
    hidden, n2, n2t, got, sum_b, sum_g, upg1, *ffn_g0 = ffn_call(
        [x, part, part_other, out_b[0:1], gains[1:2], shifts[1:2], go, up_rows[2:], meta],
        n_q,
        2,
        fh,
        places,
        parts0,
        True,
        not square,
    )
    n2, ffn_g0, here_near = both((n2, ffn_g0, here_near))
    if square:
        here_far = gather_far(*here_near, "ffn_w1")
        parts1 = [ffn_own, *own_near, *own_far, far_one, *here_near, *here_far]
        parts1 = [flat(v)[None, None] for v in parts1]
        halves = ((0, 0, 2), (1, 0, 2), (2, 0, 2), (3, 0, 1), (3, 1, 1))
        places = [(j, i, t, n, False) for i in (0, 1) for j, t, n in halves]
    else:
        parts1 = [gather_plane(flat(jnp.stack([ffn_own, far_one])), "ffn_w0")]
    n2, parts1, ffn_g0 = both((n2, parts1, ffn_g0))
    reach_f0 = scatter_reach(ffn_g0, "ffn_g0")
    branch, gn2, upg0, *ffn_g1 = ffn_call(
        [n2, n2t, got, sum_b, sum_g, go, up_rows[:2], meta],
        n_q,
        2,
        fh,
        places,
        parts1,
        False,
        not square,
    )
    branch, gn2, ffn_g1, reach_f0 = both((branch, gn2, ffn_g1, reach_f0))

    last_f0 = scatter_last(ffn_g0, reach_f0, "ffn_g0")
    reach_f1 = scatter_reach(ffn_g1, "ffn_g1")
    gn2_other = swap(gn2, "dp", 1, "grad_norm_two")
    theirs = swap(row_half(branch, 1 - core), "dp", 1, "branch")
    gn2_other, theirs = both((gn2_other, theirs))
    out_half = row_half(hidden, core) + row_half(branch, core).astype(F32) + theirs.astype(F32) + out_b[1]
    gn2_other, out_half = both((gn2_other, rel(out_half.astype(BF))))
    out_first = from_image(out_half, z, 0, "block_out")
    gh, ght, gmixa, gmixb, sums = hidden_backward(
        meta, hidden, gn2, gn2_other, gains[1:2], go, n_q, att_places, att_parts
    )
    gmixa, last_f0, out_first, out_half = both((gmixa, last_f0, out_first, out_half))
    ffn2, ffn3 = scatter_sum(ffn_g0, reach_f0, last_f0)
    ffn_three = swap(ffn3, "mp", 1, "ffn_g_z3")
    out_last = from_image(out_half, z, 1, "block_out")
    gmixa, ffn2 = both((gmixa, ffn2))
    n1t, gqa, bias_a, *att_ga = att_backward_first(
        meta, gmixa, ght, n1, qkva, mixa, n_q, not square
    )
    n1t, gqa, reach_f1, ffn_three, out_last, att_ga = both(
        (n1t, gqa, reach_f1, ffn_three, out_last, att_ga)
    )
    reach_aa = scatter_reach(att_ga, "att_ga")
    last_f1 = scatter_last(ffn_g1, reach_f1, "ffn_g1")
    ffn_two = swap(add(ffn2, ffn_three), "mp", 2, "ffn_g_z2")
    gn1, bias_b, more_sums, *att_gb = att_backward_last(
        meta, x, gmixb, ght, n1t, gqa, qkvb, mixb, n_q, att_places, att_parts, not square
    )
    gn1, last_f1, att_gb, x, ffn_two, reach_aa = both((gn1, last_f1, att_gb, x, ffn_two, reach_aa))

    reach_ab = scatter_reach(att_gb, "att_gb")
    gn1_other = swap(row_half(gn1, 1 - core), "dp", 1, "grad_norm_one")
    ffn0, ffn1 = scatter_sum(ffn_g1, reach_f1, last_f1)
    ffn_one = swap(ffn1, "mp", 1, "ffn_g_z1")
    gn1 = row_half(gn1, core).astype(F32) + gn1_other.astype(F32)
    hat1, inv1 = normalise(after(row_half(x, core), gn1_other).astype(F32))
    input_half = row_half(gh, core) + norm_back(hat1, inv1, gains[0], gn1)
    input_half = rel(input_half.astype(BF))
    in_first = from_image(input_half, z, 0, "input_grad")
    reach_ab, input_half, in_first, upg0, upg1, bias_a, bias_b, sums, more_sums, reach_aa = both(
        (reach_ab, input_half, in_first, upg0, upg1, bias_a, bias_b, sums, more_sums, reach_aa)
    )
    in_last = from_image(input_half, z, 1, "input_grad")
    last_ab = scatter_last(att_gb, reach_ab, "att_gb")
    last_aa = scatter_last(att_ga, reach_aa, "att_ga")

    def placed(values):
        mine = jnp.concatenate([lax.dynamic_slice_in_dim(values, z ^ i, 1, 0) for i in range(n_i)])
        return jnp.stack([jnp.where(core == c, mine, jnp.zeros_like(mine)) for c in range(2)], 1)

    bias_a, bias_b = (v.reshape(3, 2, he) for v in (bias_a, bias_b))
    wide = [placed(jnp.concatenate([bias_a[t], bias_b[t]])) for t in (0, 2)]
    wide.append(placed(jnp.concatenate([upg0, upg1])))
    values = [*wide, rel(sums), rel(more_sums)]
    vector = jnp.concatenate([v.reshape(-1, 128) for v in values])
    last_ab, last_aa, vector, ffn_one = both((last_ab, last_aa, vector, ffn_one))
    att0, att1 = scatter_sum(att_ga, reach_aa, last_aa)
    att2, att3 = scatter_sum(att_gb, reach_ab, last_ab)
    att_three = swap(att3, "mp", 1, "att_g_z3")
    att_one = swap(att1, "mp", 1, "att_g_z1")
    vector = vector + swap(vector, "dp", 2, "sums_dp2")
    bit = 4
    while bit < n_dp:
        vector = vector + swap(vector, "dp", bit, "sums_dp" + str(bit))
        bit *= 2
    ffn_grad = add(ffn0, ffn_one, ffn_two)
    att_three, vector, in_last, ffn_grad = both((att_three, vector, in_last, ffn_grad))
    att_two = swap(add(att2, att_three), "mp", 2, "att_g_z2")
    vector = vector + swap(vector, "dp", 1, "sums_core")
    for bit in (1, 2):
        vector = vector + swap(vector, "mp", bit, "sums_z" + str(bit))
    att_grad = add(att0, att_one, att_two)
    in_routes = [in_first, in_last]
    block_out = joined_images([out_first, out_last], z)
    block_out = jnp.where(keep_mine, block_out, jnp.zeros_like(block_out))
    input_grad = joined_images(in_routes, z)

    def own_shard(grad, what):
        kinds, _, last = grad.shape
        pair = grad.reshape(kinds, 2, wq // 2, last)
        keep = lax.dynamic_index_in_dim(pair, core, 1, False)
        got = swap(lax.dynamic_index_in_dim(pair, 1 - core, 1, False), "dp", 1, what)
        return ordered_pair(keep, got, core, 2).reshape(kinds, wq // 2, 2 * last).astype(F32)

    att_shard, ffn_shard = own_shard(att_grad, "att_g_core"), own_shard(ffn_grad, "ffn_g_core")
    qkv_owned, proj_owned = att_shard[:3], jnp.transpose(att_shard[3])
    up_owned, down_owned = ffn_shard[0], jnp.transpose(ffn_shard[1])

    ends = [0]
    for v in values:
        ends.append(ends[-1] + v.size // 128)
    *wide, sums, more_sums = [
        vector[start:end].reshape(v.shape) for v, start, end in zip(values, ends, ends[1:])
    ]
    wide = [lax.dynamic_index_in_dim(v, z, 0, False).reshape(-1) for v in wide]
    bias_grad, upbias_grad = jnp.stack(wide[:2]), wide[2]
    gains_grad = jnp.stack([more_sums[0], sums[0] * 0.5])
    shifts_grad = jnp.stack([more_sums[1], sums[1] * 0.5])
    outbias_grad = sums[2:4] * 0.5
    return (
        block_out,
        input_grad,
        gains_grad,
        shifts_grad,
        qkv_owned,
        bias_grad,
        proj_owned,
        outbias_grad,
        up_owned,
        upbias_grad,
        down_owned,
    )


def solution(mesh):
    split = P("mp", "dp", None)
    return jax.shard_map(
        local,
        mesh=mesh,
        in_specs=(
            split,
            P("dp"),
            P(),
            P(),
            P(None, "dp", "mp"),
            P(None, "mp"),
            P("mp", "dp"),
            P(),
            P("dp", "mp"),
            P("mp"),
            P("mp", "dp"),
            split,
        ),
        out_specs=(
            split,
            split,
            P(),
            P(),
            P(None, "dp", "mp"),
            P(None, "mp"),
            P("mp", "dp"),
            P(),
            P("dp", "mp"),
            P("mp"),
            P("mp", "dp"),
        ),
        check_vma=False,
    )
```

```python
import functools

import jax
import jax.numpy as jnp
from jax import lax
from jax.experimental import pallas as pl
from jax.experimental.pallas import tpu as pltpu
from jax.sharding import PartitionSpec as P

HEAD = 64
BUF = 64
BF = jnp.bfloat16
F32 = jnp.float32
epsilon = 1e-06
masked_score = -1e30
MIB = 1 << 20
NT = (((1,), (1,)), ((), ()))
NN = (((1,), (0,)), ((), ()))
TN = (((0,), (0,)), ((), ()))
factor = HEAD ** (-0.5)
VMEM_SPEC = pl.BlockSpec(memory_space=pltpu.VMEM)
ANY_SPEC = pl.BlockSpec(memory_space=pl.ANY)
SMEM_SPEC = pl.BlockSpec(memory_space=pltpu.SMEM)


def mm(a, b, dims=NN):
    return lax.dot_general(a, b, dims, preferred_element_type=F32)


def normalise(values):
    average = jnp.mean(values, axis=-1, keepdims=True)
    centred = values - average
    spread = jnp.mean(centred * centred, axis=-1, keepdims=True)
    inv = lax.rsqrt(spread + epsilon)
    return centred * inv, inv


def norm_back(n, inv, scales, grad):
    e = grad * scales
    mean_e = jnp.mean(e, axis=-1, keepdims=True)
    mean_en = jnp.mean(e * n, axis=-1, keepdims=True)
    return (e - mean_e - n * mean_en) * inv


def gelu_parts(inputs):
    normal_cdf = 0.5 + 0.5 * lax.erf(inputs * 0.7071067811865476)
    density = jnp.exp(-0.5 * inputs * inputs) * 0.3989422804014327
    return inputs * normal_cdf, normal_cdf + inputs * density


def for_each(count, step):
    if count <= 4:
        for index in range(count):
            step(index)
    else:
        pl.loop(0, count)(step)


def valid_slots(meta_ref, image, slots, axis):
    shape = (slots, 1) if axis == 0 else (1, slots)
    row = lax.broadcasted_iota(jnp.int32, shape, axis)
    n = slots // 4
    k = (row >= n).astype(jnp.int32) + (row >= 2 * n) + (row >= 3 * n)
    slot = (k ^ meta_ref[3]) * n + (row - k * n)
    return slot < BUF + meta_ref[image]


def block_rows(jj, size):
    start = jj * size
    return pl.ds(start if isinstance(jj, int) else pl.multiple_of(start, size), size)


def load_blocks(parts, refs, q, kinds, wq, wanted, place, sem):
    for (j0, i0, t0, count, absolute), ref in zip(parts, refs):
        nj, ni = ref.shape[:2]

        def one(jj, ref=ref, j0=j0, i0=i0, t0=t0, count=count, absolute=absolute, ni=ni):
            source = jj ^ q if absolute else jj
            for ii in range(ni):
                if i0 + ii not in wanted:
                    continue
                for t in range(t0, t0 + count):
                    if t in kinds:
                        pltpu.make_async_copy(
                            ref.at[source, ii, pl.ds((t - t0) * wq, wq)],
                            place(block_rows(j0 + jj, wq), i0 + ii, t),
                            sem,
                        ).start()

        for_each(nj, one)


def store_blocks(refs, q, n_j, block, i, sem):
    def start(views, target):
        for t, view in enumerate(views):
            pltpu.make_async_copy(view, target.at[t], sem).start()

    if len(refs) == 1:
        for_each(n_j, lambda jj: start(block(jj), refs[0].at[jj ^ q, i]))
        return
    own, to_x, to_y, keep_x, keep_y = refs
    start(block(0), own.at[i])
    if i == 0:
        start(block(1), keep_x.at[0])
        start(block(2), to_y.at[1])
        start(block(3), to_y.at[0])
    else:
        start(block(1), to_x.at[1])
        start(block(2), keep_y.at[0])
        start(block(3), to_x.at[0])


def grad_shapes(n_j, n_i, absolute, block):
    shape = lambda *lead: jax.ShapeDtypeStruct(lead + block, BF)
    if absolute:
        return [shape(n_j, n_i)]
    return [shape(2), shape(2), shape(2), shape(1), shape(1)]


def att_column(n_i, i, t):
    he = 2 * HEAD
    if t == 3:
        return 3 * n_i * he + i * he
    return (i // 2) * 6 * he + (t * 2 + i % 2) * he


def att_fwd_kernel(parts, n_i, x_ref, g_ref, c_ref, bias_ref, meta_ref, *rest):
    w_refs = rest[: len(parts)]
    n1_ref, qkva_ref, qkvb_ref, mixa_ref, mixb_ref, part_ref, w_scr, m_scr, sem = rest[len(parts) :]
    he = 2 * HEAD
    width = w_scr.shape[0]
    image = pl.program_id(0)

    @pl.when(image == 0)
    def _():
        place = lambda rows, i, t: w_scr.at[rows, pl.ds(att_column(n_i, i, t), he)]
        wq = width // max(p[0] + r.shape[0] for p, r in zip(parts, w_refs))
        load_blocks(parts, w_refs, meta_ref[4], range(4), wq, range(n_i), place, sem)
        pltpu.make_async_copy(w_scr, w_scr, sem).wait()

    hat, _ = normalise(x_ref[0].astype(F32))
    n1 = (hat * g_ref[...] + c_ref[...]).astype(BF)
    n1_ref[...] = n1
    qkv_refs = (qkva_ref, qkvb_ref)
    for half in range(2):
        cols = pl.ds(half * 6 * he, 6 * he)
        res = (mm(n1, w_scr[:, cols]) + bias_ref[:, cols]).astype(BF)
        for n in range(6):
            qkv_refs[half][n] = res[:, n * he : (n + 1) * he]
    bias = jnp.where(valid_slots(meta_ref, image, x_ref.shape[1], 1), 0.0, masked_score)
    lane = lax.broadcasted_iota(jnp.int32, (1, he), 1)
    low_half = lane < HEAD
    for i in range(n_i):
        ref = qkv_refs[i // 2]
        q2, k2, v2 = (ref[t * 2 + i % 2] for t in range(3))
        outs = []
        for h in range(2):
            qm = jnp.where(low_half if h == 0 else ~low_half, q2, jnp.zeros_like(q2))
            s = mm(qm, k2, NT) * factor + bias
            top = jnp.max(s, axis=-1, keepdims=True)
            p = jnp.exp(s - top)
            w = (p / jnp.sum(p, axis=-1, keepdims=True)).astype(BF)
            outs.append(mm(w, v2))
        mixed = jnp.where(low_half, outs[0], outs[1]).astype(BF)
        m_scr[:, i * he : (i + 1) * he] = mixed
    mixa_ref[...] = m_scr[:, : 2 * he]
    mixb_ref[...] = m_scr[:, 2 * he :]
    part_ref[...] = mm(m_scr[...], w_scr[:, 3 * n_i * he :], NT).astype(BF)


def att_forward(x, gain, shift, bias, meta, parts, arrays):
    images, slots, width = x.shape
    n_i = 4
    he = 2 * HEAD
    rows = images * slots
    row_block = lambda last: pl.BlockSpec((slots, last), lambda a: (a, 0))
    whole = lambda *shape: pl.BlockSpec(shape, lambda a: (0,) * len(shape))
    qkv_block = pl.BlockSpec((6, slots, he), lambda a: (0, a, 0))
    return pl.pallas_call(
        functools.partial(att_fwd_kernel, parts, n_i),
        grid=(images,),
        in_specs=[
            pl.BlockSpec((1, slots, width), lambda a: (a, 0, 0)),
            whole(1, width),
            whole(1, width),
            whole(1, 3 * n_i * he),
            SMEM_SPEC,
        ]
        + [ANY_SPEC] * len(arrays),
        out_specs=[row_block(width), qkv_block, qkv_block, row_block(2 * he), row_block(2 * he), row_block(width)],
        out_shape=[
            jax.ShapeDtypeStruct((rows, width), BF),
            jax.ShapeDtypeStruct((6, rows, he), BF),
            jax.ShapeDtypeStruct((6, rows, he), BF),
            jax.ShapeDtypeStruct((rows, 2 * he), BF),
            jax.ShapeDtypeStruct((rows, 2 * he), BF),
            jax.ShapeDtypeStruct((rows, width), BF),
        ],
        scratch_shapes=[
            pltpu.VMEM((width, 4 * n_i * he), BF),
            pltpu.VMEM((slots, n_i * he), BF),
            pltpu.SemaphoreType.DMA,
        ],
        compiler_params=pltpu.CompilerParams(vmem_limit_bytes=48 * MIB),
        cost_estimate=pl.CostEstimate(flops=16_000_000_000, bytes_accessed=20_000_000, transcendentals=2_500_000),
        name="att_forward",
    )(x, gain, shift, bias, meta, *arrays)


def ffn_kernel(parts, n_i, n_j, n_out, first, *refs):
    if first:
        x_ref, pa_ref, pb_ref, b_ref, g_ref, c_ref = refs[:6]
        refs = refs[6:]
    else:
        kept, refs = refs[:5], refs[5:]
    go_ref, upb_ref, meta_ref = refs[:3]
    w_refs, refs = refs[3 : 3 + len(parts)], refs[3 + len(parts) :]
    q = meta_ref[4]
    if first:
        hidden_out, refs = refs[0], refs[1:]
        kept, refs = refs[:5], refs[5:]
        sum_outs = kept[3:]
    else:
        sum_outs, refs = refs[:2], refs[2:]
    upg_ref, refs = refs[0], refs[1:]
    grad_refs, refs = refs[:n_out], refs[n_out:]
    n2, n2t, got, run_b, run_g, wbuf, gbuf, act_s, pre_s, wsem, gsem, ksem, ssem = refs[:13]
    held = (n2, n2t, got, run_b, run_g)
    if first:
        hidden, hsem = refs[13:]
        low_sums = (run_b, run_g)
    else:
        low_sums = refs[13:]
    rows, width = go_ref.shape
    wq = width // n_j
    rb = rows // 3

    def fetch(i, slot):
        place = lambda rws, _, t: wbuf.at[slot, t, rws]
        load_blocks(parts, w_refs, q, range(2), wq, (i,), place, wsem.at[slot])

    def fetched(slot):
        pltpu.make_async_copy(wbuf.at[slot], wbuf.at[slot], wsem.at[slot]).wait()

    def put(i, slot):
        block = lambda jj: [gbuf.at[slot, t, block_rows(jj, wq)] for t in range(2)]
        store_blocks(grad_refs, q, n_j, block, i, gsem.at[slot])

    def stored(slot):
        pltpu.make_async_copy(gbuf.at[slot], gbuf.at[slot], gsem.at[slot]).wait()

    def keep(n):
        if first:
            return pltpu.make_async_copy(held[n], kept[n], ksem.at[n])
        return pltpu.make_async_copy(kept[n], held[n], ksem.at[n])

    fetch(0, 0)
    if first:
        block = 192

        @pl.loop(0, rows // block)
        def _(r):
            rw = pl.ds(pl.multiple_of(r * block, block), block)
            h = (
                x_ref[rw, :].astype(F32)
                + (pa_ref[rw, :].astype(F32) + pb_ref[rw, :].astype(F32))
                + b_ref[...]
            )
            hidden[rw, :] = h
            hat, _ = normalise(h)
            n2[rw, :] = (hat * g_ref[...] + c_ref[...]).astype(BF)

        pltpu.make_async_copy(hidden, hidden_out, hsem).start()
        keep(0).start()
        n2t[...] = n2[...].T
        keep(1).start()
        got[...] = go_ref[...].T
        keep(2).start()
    else:
        for n in (0, 3, 4, 1, 2):
            keep(n).start()
        keep(0).wait()
    for i in range(n_i):
        slot = i % 2
        if i + 1 < n_i:
            fetch(i + 1, 1 - slot)
        fetched(slot)
        if i == 0 and not first:
            keep(3).wait()
            keep(4).wait()

        @pl.loop(0, 3)
        def _(r, i=i, slot=slot):
            rw = pl.ds(pl.multiple_of(r * rb, rb), rb)
            u, w = wbuf[slot, 0], wbuf[slot, 1]
            up = mm(n2[rw, :], u) + upb_ref[i : i + 1, :]
            act, slope = gelu_parts(up)
            act = act.astype(BF)
            act_s[rw, :] = act
            pre = (mm(go_ref[rw, :], w) * slope).astype(BF)
            pre_s[rw, :] = pre
            down = mm(act, w, NT)
            back = mm(pre, u, NT)
            if i > 0 or not first:
                down += run_b[rw, :]
                back += run_g[rw, :]
            if i < n_i - 1:
                run_b[rw, :] = down
                run_g[rw, :] = back
            else:
                for n, total in enumerate((down, back)):
                    low_sums[n][rw, :] = total.astype(low_sums[n].dtype)
                    pltpu.make_async_copy(low_sums[n].at[rw], sum_outs[n].at[rw], ssem.at[n]).start()

        if i == 0 and not first:
            keep(1).wait()
            keep(2).wait()
        upg_ref[i : i + 1, :] = jnp.sum(pre_s[...].astype(F32), axis=0, keepdims=True)
        if i >= 2:
            stored(slot)
        gbuf[slot, 0] = mm(n2t[...], pre_s[...]).astype(BF)
        gbuf[slot, 1] = mm(got[...], act_s[...]).astype(BF)
        put(i, slot)
    for n in range(2):
        pltpu.make_async_copy(low_sums[n], sum_outs[n], ssem.at[n]).wait()
    if first:
        pltpu.make_async_copy(hidden, hidden_out, hsem).wait()
        for n in range(3):
            keep(n).wait()
    for i in range(max(n_i - 2, 0), n_i):
        stored(i % 2)


def ffn_call(ins, n_j, n_i, fh, parts, arrays, first, absolute):
    go = ins[-3]
    rows, width = go.shape
    wq = width // n_j
    wide, low, turned = (rows, width, F32), (rows, width, BF), (width, rows, BF)
    outs = [wide, low, turned, turned, wide, wide] if first else [low, low]
    grads = grad_shapes(n_j, n_i, absolute, (2, wq, fh))
    if first:
        in_specs = [VMEM_SPEC] * (len(ins) - 1)
    else:
        in_specs = [ANY_SPEC] * 5 + [VMEM_SPEC] * 2
    extra = (
        [pltpu.VMEM((rows, width), F32), pltpu.SemaphoreType.DMA]
        if first
        else [pltpu.VMEM((rows, width), BF)] * 2
    )
    return pl.pallas_call(
        functools.partial(ffn_kernel, parts, n_i, n_j, len(grads), first),
        in_specs=in_specs + [SMEM_SPEC] + [ANY_SPEC] * len(arrays),
        out_specs=[ANY_SPEC] * len(outs) + [VMEM_SPEC] + [ANY_SPEC] * len(grads),
        out_shape=[jax.ShapeDtypeStruct((m, n), kind) for m, n, kind in outs]
        + [jax.ShapeDtypeStruct((n_i, fh), F32)]
        + grads,
        scratch_shapes=[
            pltpu.VMEM((rows, width), BF),
            pltpu.VMEM((width, rows), BF),
            pltpu.VMEM((width, rows), BF),
            pltpu.VMEM((rows, width), F32),
            pltpu.VMEM((rows, width), F32),
            pltpu.VMEM((2, 2, width, fh), BF),
            pltpu.VMEM((2, 2, width, fh), BF),
            pltpu.VMEM((rows, fh), BF),
            pltpu.VMEM((rows, fh), BF),
            pltpu.SemaphoreType.DMA((2,)),
            pltpu.SemaphoreType.DMA((2,)),
            pltpu.SemaphoreType.DMA((5,)),
            pltpu.SemaphoreType.DMA((2,)),
        ]
        + extra,
        compiler_params=pltpu.CompilerParams(vmem_limit_bytes=56 * MIB),
        cost_estimate=pl.CostEstimate(
            flops=12_000_000_000 * n_i, bytes_accessed=30_000_000, transcendentals=1_000_000 * n_i
        ),
        name="ffn_first" if first else "ffn_last",
    )(*ins, *arrays)


def att_back_blocks(meta_ref, qkv_ref, gmix, gq, rows, which):
    he = 2 * HEAD
    images = 3
    slots = rows // images
    lane = lax.broadcasted_iota(jnp.int32, (1, he), 1)
    low_half = lane < HEAD

    @pl.loop(0, images)
    def _(a):
        rw = pl.ds(pl.multiple_of(a * slots, slots), slots)
        bias = jnp.where(valid_slots(meta_ref, a, slots, 0), 0.0, masked_score)
        for i in range(2):
            q2, k2, v2 = (qkv_ref[t * 2 + i, rw, :] for t in range(3))
            g2 = gmix[which + i, rw, :]
            dq, dk, dv = [], [], []
            for h in range(2):
                here = low_half if h == 0 else ~low_half
                qm = jnp.where(here, q2, jnp.zeros_like(q2))
                gm = jnp.where(here, g2, jnp.zeros_like(g2))
                st = mm(k2, qm, NT) * factor + bias
                top = jnp.max(st, axis=0, keepdims=True)
                p = jnp.exp(st - top)
                p = p / jnp.sum(p, axis=0, keepdims=True)
                dpt = mm(v2, gm, NT)
                dot = jnp.sum(p * dpt, axis=0, keepdims=True)
                ds = (p * (dpt - dot)).astype(BF)
                dk.append(mm(ds, q2))
                dv.append(mm(p.astype(BF), g2))
                dq.append(mm(ds, k2, TN))
            for t, (pair, scale) in enumerate(((dq, factor), (dk, factor), (dv, 1.0))):
                both = jnp.where(low_half, pair[0], pair[1])
                gq[rw, (t * 2 + i) * he : (t * 2 + i + 1) * he] = (both * scale).astype(BF)


def put_att_grads(grad_refs, q, n_j, wq, gbuf, gsem):
    he = 2 * HEAD
    for i in range(2):
        block = lambda jj, i=i: [
            gbuf.at[t, block_rows(jj, wq), pl.ds(i * he, he)] for t in range(4)
        ]
        store_blocks(grad_refs, q, n_j, block, i, gsem)


def hidden_back_kernel(
    parts, n_i, n_j, meta_ref, hid_ref, ga_ref, gb_ref, g_ref, go_ref, *rest
):
    w_refs = rest[: len(parts)]
    gh_ref, ght, gmixa, gmixb, sums_ref = rest[len(parts) : len(parts) + 5]
    ghb, w_scr, sem = rest[len(parts) + 5 :]
    rows, width = hid_ref.shape
    he = 2 * HEAD
    place = lambda rws, i, t: w_scr.at[rws, pl.ds(i * he, he)]
    load_blocks(parts, w_refs, meta_ref[4], (3,), width // n_j, range(n_i), place, sem)
    sums_ref[...] = jnp.zeros_like(sums_ref)
    pltpu.make_async_copy(w_scr, w_scr, sem).wait()
    block = 192

    @pl.loop(0, rows // block)
    def _(r):
        rw = pl.ds(pl.multiple_of(r * block, block), block)
        hat, inv = normalise(hid_ref[rw, :])
        grad = ga_ref[rw, :].astype(F32) + gb_ref[rw, :].astype(F32)
        gout = go_ref[rw, :].astype(F32)
        gh = gout + norm_back(hat, inv, g_ref[...], grad)
        gh_ref[rw, :] = gh
        low = gh.astype(BF)
        ghb[rw, :] = low
        sums_ref[0:1, :] += jnp.sum(grad * hat, axis=0, keepdims=True)
        sums_ref[1:2, :] += jnp.sum(grad, axis=0, keepdims=True)
        sums_ref[2:3, :] += jnp.sum(gh, axis=0, keepdims=True)
        sums_ref[3:4, :] += jnp.sum(gout, axis=0, keepdims=True)
        res = mm(low, w_scr[...]).astype(BF)
        for i in range(n_i):
            (gmixa, gmixb)[i // 2][i % 2, rw, :] = res[:, i * he : (i + 1) * he]

    ght[...] = ghb[...].T


def hidden_backward(meta, hidden, ga, gb, gain, go, n_j, parts, arrays):
    rows, width = hidden.shape
    n_i, he = 4, 2 * HEAD
    return pl.pallas_call(
        functools.partial(hidden_back_kernel, parts, n_i, n_j),
        in_specs=[SMEM_SPEC] + [VMEM_SPEC] * 5 + [ANY_SPEC] * len(arrays),
        out_specs=[VMEM_SPEC] * 5,
        out_shape=[
            jax.ShapeDtypeStruct((rows, width), F32),
            jax.ShapeDtypeStruct((width, rows), BF),
            jax.ShapeDtypeStruct((2, rows, he), BF),
            jax.ShapeDtypeStruct((2, rows, he), BF),
            jax.ShapeDtypeStruct((8, width), F32),
        ],
        scratch_shapes=[
            pltpu.VMEM((rows, width), BF),
            pltpu.VMEM((width, n_i * he), BF),
            pltpu.SemaphoreType.DMA,
        ],
        compiler_params=pltpu.CompilerParams(vmem_limit_bytes=48 * MIB),
        cost_estimate=pl.CostEstimate(flops=10_000_000_000, bytes_accessed=20_000_000, transcendentals=0),
        name="hidden_backward",
    )(meta, hidden, ga, gb, gain, go, *arrays)


def att_bwd_first_kernel(n_i, n_j, n_out, meta_ref, gmix, ght, n1_ref, qkv_ref, mix_ref, *rest):
    n1t, gq, bias_ref = rest[:3]
    grad_refs = rest[3 : 3 + n_out]
    gbuf, gsem = rest[3 + n_out :]
    width, rows = ght.shape
    he = 2 * HEAD
    gbuf[3] = mm(ght[...], mix_ref[...]).astype(BF)
    att_back_blocks(meta_ref, qkv_ref, gmix, gq, rows, 0)
    n1t[...] = n1_ref[...].T
    for t in range(3):
        gbuf[t] = mm(n1t[...], gq[:, 2 * t * he : 2 * (t + 1) * he]).astype(BF)
    put_att_grads(grad_refs, meta_ref[4], n_j, width // n_j, gbuf, gsem)
    bias_ref[...] = jnp.sum(gq[...].astype(F32), axis=0, keepdims=True)
    pltpu.make_async_copy(gbuf, gbuf, gsem).wait()


def att_backward_first(meta, gmix, ght, n1, qkv, mix, n_j, absolute):
    width, rows = ght.shape
    n_i, he = 4, 2 * HEAD
    wq = width // n_j
    grads = grad_shapes(n_j, 2, absolute, (4, wq, he))
    return pl.pallas_call(
        functools.partial(att_bwd_first_kernel, n_i, n_j, len(grads)),
        in_specs=[SMEM_SPEC] + [VMEM_SPEC] * 5,
        out_specs=[VMEM_SPEC] * 3 + [ANY_SPEC] * len(grads),
        out_shape=[
            jax.ShapeDtypeStruct((width, rows), BF),
            jax.ShapeDtypeStruct((rows, 6 * he), BF),
            jax.ShapeDtypeStruct((1, 6 * he), F32),
        ]
        + grads,
        scratch_shapes=[pltpu.VMEM((4, width, 2 * he), BF), pltpu.SemaphoreType.DMA],
        compiler_params=pltpu.CompilerParams(vmem_limit_bytes=48 * MIB),
        cost_estimate=pl.CostEstimate(flops=16_000_000_000, bytes_accessed=20_000_000, transcendentals=1_250_000),
        name="att_backward_first",
    )(meta, gmix, ght, n1, qkv, mix)


def att_bwd_last_kernel(
    parts, n_i, n_j, n_out, meta_ref, x_ref, gmix, ght, n1t, gqa_ref, qkv_ref, mix_ref, *rest
):
    w_refs = rest[: len(parts)]
    gn1_ref, bias_ref, sums_ref = rest[len(parts) : len(parts) + 3]
    rest = rest[len(parts) + 3 :]
    grad_refs = rest[:n_out]
    gq, w_scr, gbuf, sem, gsem = rest[n_out:]
    rows, width = x_ref.shape
    he = 2 * HEAD
    wq = width // n_j
    q = meta_ref[4]
    place = lambda rws, i, t: w_scr.at[rws, pl.ds(att_column(n_i, i, t), he)]
    load_blocks(parts, w_refs, q, (0, 1, 2), wq, range(n_i), place, sem)
    gbuf[3] = mm(ght[...], mix_ref[...]).astype(BF)
    att_back_blocks(meta_ref, qkv_ref, gmix, gq, rows, 0)
    for t in range(3):
        gbuf[t] = mm(n1t[...], gq[:, 2 * t * he : 2 * (t + 1) * he]).astype(BF)
    put_att_grads(grad_refs, q, n_j, wq, gbuf, gsem)
    bias_ref[...] = jnp.sum(gq[...].astype(F32), axis=0, keepdims=True)
    sums_ref[...] = jnp.zeros_like(sums_ref)
    pltpu.make_async_copy(w_scr, w_scr, sem).wait()
    rb = rows // 3

    @pl.loop(0, 3)
    def _(r):
        rw = pl.ds(pl.multiple_of(r * rb, rb), rb)
        grad = mm(gqa_ref[rw, :], w_scr[:, : 6 * he], NT) + mm(gq[rw, :], w_scr[:, 6 * he :], NT)
        gn1_ref[rw, :] = grad.astype(BF)
        hat, _ = normalise(x_ref[rw, :].astype(F32))
        sums_ref[0:1, :] += jnp.sum(grad * hat, axis=0, keepdims=True)
        sums_ref[1:2, :] += jnp.sum(grad, axis=0, keepdims=True)

    pltpu.make_async_copy(gbuf, gbuf, gsem).wait()


def att_backward_last(meta, x, gmix, ght, n1t, gqa, qkv, mix, n_j, parts, arrays, absolute):
    rows, width = x.shape
    n_i, he = 4, 2 * HEAD
    wq = width // n_j
    grads = grad_shapes(n_j, 2, absolute, (4, wq, he))
    return pl.pallas_call(
        functools.partial(att_bwd_last_kernel, parts, n_i, n_j, len(grads)),
        in_specs=[SMEM_SPEC] + [VMEM_SPEC] * 7 + [ANY_SPEC] * len(arrays),
        out_specs=[VMEM_SPEC] * 3 + [ANY_SPEC] * len(grads),
        out_shape=[
            jax.ShapeDtypeStruct((rows, width), BF),
            jax.ShapeDtypeStruct((1, 6 * he), F32),
            jax.ShapeDtypeStruct((8, width), F32),
        ]
        + grads,
        scratch_shapes=[
            pltpu.VMEM((rows, 6 * he), BF),
            pltpu.VMEM((width, 3 * n_i * he), BF),
            pltpu.VMEM((4, width, 2 * he), BF),
            pltpu.SemaphoreType.DMA,
            pltpu.SemaphoreType.DMA,
        ],
        compiler_params=pltpu.CompilerParams(vmem_limit_bytes=56 * MIB),
        cost_estimate=pl.CostEstimate(flops=20_000_000_000, bytes_accessed=30_000_000, transcendentals=1_250_000),
        name="att_backward_last",
    )(meta, x, gmix, ght, n1t, gqa, qkv, mix, *arrays)


def swap(x, axis, bits, what):
    n = lax.axis_size(axis)
    with jax.named_scope(what):
        return lax.ppermute(x, axis, [(i, i ^ bits) for i in range(n)])


def after(x, *deps):
    return lax.optimization_barrier((x,) + deps)[0] if deps else x


def add(*parts):
    total = parts[0].astype(F32)
    for part in parts[1:]:
        total = total + part.astype(F32)
    return total.astype(parts[0].dtype)


def planes():
    n_dp = lax.axis_size("dp")
    return [list(range(core, n_dp, 2)) for core in range(2)]


def gather_plane(block, what):
    with jax.named_scope(what):
        return lax.all_gather(block, "dp", axis_index_groups=planes())


def scatter_plane(blocks, what):
    flat = blocks.reshape(-1, blocks.shape[-1])
    with jax.named_scope(what):
        mine = lax.psum_scatter(
            flat, "dp", scatter_dimension=0, axis_index_groups=planes(), tiled=True
        )
    return mine.reshape(blocks.shape[1:])


def gather_near(own, what):
    return swap(own, "dp", 2, what + "_x1"), swap(own, "dp", 4, what + "_y1")


def gather_far(one, two, what):
    half = one.shape[0] // 2
    return swap(one[:half], "dp", 4, what + "_y2"), swap(two[half:], "dp", 2, what + "_x2")


def scatter_reach(grads, what):
    if len(grads) == 1:
        return (scatter_plane(grads[0], what),)
    _, to_x, to_y, _, _ = grads
    return swap(to_x, "dp", 2, what + "_x1"), swap(to_y, "dp", 4, what + "_y1")


def scatter_last(grads, reach, what):
    if len(grads) == 1:
        return ()
    from_x, from_y = reach
    _, _, _, keep_x, keep_y = grads
    on_x, on_y = add(keep_x, from_y[0::2]), add(keep_y, from_x[0::2])
    return swap(on_x, "dp", 2, what + "_x2"), swap(on_y, "dp", 4, what + "_y2")


def scatter_sum(grads, reach, last):
    if len(grads) == 1:
        return [reach[0][i] for i in range(reach[0].shape[0])]
    own = grads[0]
    return [
        add(own[i], reach[1 - i % 2][i + 1 - i % 2], last[i % 2][i // 2]) for i in range(own.shape[0])
    ]


def gather_z(own, what):
    two = swap(own, "mp", 2, what + "_z2")
    one = swap(own, "mp", 1, what + "_z1")
    return one, two, swap(two, "mp", 1, what + "_z3")


def scatter_z(zero, one, two, three, what):
    two = add(two, swap(three, "mp", 1, what + "_z3"))
    return add(zero, swap(one, "mp", 1, what + "_z1"), swap(two, "mp", 2, what + "_z2"))


def ordered_pair(own, other, core, axis=0):
    return jnp.stack(
        [jnp.where(core == 0, own, other), jnp.where(core == 0, other, own)], axis
    )


def image_routes(n_dp, n_mp, odd):
    pairs = []
    for plane in range(n_dp // 2):
        for core in range(2):
            for z in range(n_mp):
                shift = 2 * core + odd
                worker = (plane * 2 + core) * n_mp + z
                holder = (plane * 2 + (z >> 1)) * n_mp + (z ^ shift)
                pairs.append((holder, worker))
    return pairs


def image_groups(x):
    slots, images, width = x.shape
    return jnp.transpose(x, (1, 0, 2)).reshape(2, images // 2, slots, width)


def for_route(groups, z, odd):
    return lax.dynamic_index_in_dim(groups, (z ^ odd) & 1, 0, False)


def to_image(send, odd, what):
    n_dp, n_mp = lax.axis_size("dp"), lax.axis_size("mp")
    with jax.named_scope(what + "_route" + str(odd)):
        return lax.ppermute(send, ("dp", "mp"), image_routes(n_dp, n_mp, odd))


def from_image(y, z, odd, what):
    n_dp, n_mp = lax.axis_size("dp"), lax.axis_size("mp")
    routes = [(b, a) for a, b in image_routes(n_dp, n_mp, odd)]
    with jax.named_scope(what + "_route" + str(odd)):
        return lax.ppermute(y[:, odd], ("dp", "mp"), routes)


def joined_images(back, z):
    flip = (z & 1) == 1
    groups = jnp.concatenate([jnp.where(flip, back[1], back[0]), jnp.where(flip, back[0], back[1])])
    return jnp.transpose(groups, (1, 0, 2))


def local(
    tokens,
    counts,
    norm_gains,
    norm_shifts,
    qkv_weight,
    qkv_bias,
    proj_weight,
    out_biases,
    up_weight,
    up_bias,
    down_weight,
    cotangent,
):
    slots, images, width = tokens.shape
    n_dp, n_mp = lax.axis_size("dp"), lax.axis_size("mp")
    n_q = n_dp // 2
    wq = width // n_q
    dp, z = lax.axis_index("dp"), lax.axis_index("mp")
    q, core = dp >> 1, dp & 1
    own_images = images // 2
    all_slots = slots * n_mp
    rows = own_images * all_slots

    def rel(v):
        blocks = [lax.dynamic_slice_in_dim(v, (q ^ j) * wq, wq, v.ndim - 1) for j in range(n_q)]
        return jnp.concatenate(blocks, -1)

    def half_of(v, which, axis):
        size = v.shape[axis] // 2
        return lax.dynamic_slice_in_dim(v, which * size, size, axis)

    att = jnp.concatenate([qkv_weight, jnp.transpose(proj_weight)[None]])
    ffn_w = jnp.stack([up_weight, jnp.transpose(down_weight)])
    he, fh = att.shape[-1] // 2, ffn_w.shape[-1] // 2

    count_rows = jnp.pad(counts.astype(BF)[None], ((0, 15), (0, he - images)))
    sent = jnp.concatenate([half_of(att, 1 - core, 2).reshape(-1, he), count_rows])
    got = swap(sent, "dp", 1, "att_w_core")
    other_counts = got[-16, :images].astype(jnp.int32)
    got = got[:-16].reshape(4, wq // 2, he)
    att_own = ordered_pair(half_of(att, core, 2), got, core, 1).reshape(-1, he)
    got = swap(half_of(ffn_w, 1 - core, 2), "dp", 1, "ffn_w_core")
    ffn_own = ordered_pair(half_of(ffn_w, core, 2), got, core, 1).reshape(2, wq, fh)
    left = jnp.concatenate(
        [half_of(qkv_bias, core, 1), half_of(up_bias, core, 0).reshape(-1, he)]
    )
    n_bias = left.shape[0]
    terms = []
    for _ in range(3):
        term = lax.reduce_precision(left, 8, 7)
        terms.append(term.astype(BF))
        left = left - term
    bias_pad = -(-3 * n_bias // 16) * 16
    bias_terms = jnp.pad(jnp.concatenate(terms), ((0, bias_pad - 3 * n_bias), (0, 0)))

    counts_here = jnp.where((z >> 1) == core, counts, other_counts)
    counts_here = lax.dynamic_slice_in_dim(counts_here, (z & 1) * own_images, own_images, 0)
    meta = jnp.concatenate([counts_here, z[None], q[None]])
    slot_ids = jnp.arange(slots, dtype=jnp.int32)
    keep_mine = ((z * slots + slot_ids)[:, None] < BUF + counts[None, :])[:, :, None]

    def whole_rows(got, what):
        return ordered_pair(got, swap(got, "dp", 1, what), core, 1).reshape(rows, width)

    n_i = n_mp
    gains, shifts, out_b = rel(norm_gains), rel(norm_shifts), rel(out_biases)
    square = n_q == 4
    pair_places = [(j, i, 0, 2, False) for j, i in ((0, 0), (1, 0), (2, 0), (3, 0), (3, 1))]
    both = lax.optimization_barrier

    def flat(v):
        return v.reshape(v.shape[:-3] + (-1, v.shape[-1]))

    row_half = lambda v, which: half_of(v.reshape(own_images, n_mp, slots, width), which, 1)

    att_mine = jnp.concatenate([att_own, bias_terms])
    two = swap(att_mine, "mp", 2, "att_w_z2")
    one = swap(att_mine, "mp", 1, "att_w_z1")
    token_groups = image_groups(rel(tokens))
    sends = [for_route(token_groups, z, odd) for odd in (0, 1)]
    own_near = gather_near(ffn_own, "ffn_w0") if square else ()
    one, two, sends, ffn_own = both((one, two, sends, ffn_own))
    three = swap(two, "mp", 1, "att_w_z3")
    far_two = swap(ffn_own, "mp", 2, "ffn_w_z2")
    att_z = jnp.stack([att_mine, one, two, three])
    bias_all = att_z[:, 4 * wq : 4 * wq + 3 * n_bias].astype(F32).reshape(n_i, 3, n_bias, he)
    bias_all = bias_all[:, 0] + (bias_all[:, 1] + bias_all[:, 2])
    bias_three = jnp.stack([bias_all[:, 0], jnp.zeros((n_i, he), F32), bias_all[:, 1]])
    bias_rows = jnp.transpose(bias_three.reshape(3, 2, 2, he), (1, 0, 2, 3)).reshape(1, -1)
    att_near = gather_near(after(att_z, *own_near), "att_w") if square else ()
    own_far = gather_far(*own_near, "ffn_w0") if square else ()
    far_two, sends, bias_rows = both((far_two, sends, bias_rows))
    far_three = swap(far_two, "mp", 1, "ffn_w_z3")
    token_rows = [to_image(sends[odd], odd, "tokens") for odd in (0, 1)]

    if square:
        att_far = gather_far(*att_near, "att_w")
        att_places = [(j, i, 0, 4, False) for j, i in ((0, 0), (1, 0), (2, 0), (3, 0), (3, 2))]
    else:
        att_far, att_places = (gather_plane(att_z, "att_w"),), [(0, 0, 0, 4, True)]
    cot = rel(jnp.where(keep_mine, cotangent, jnp.zeros_like(cotangent)))
    cot_groups = image_groups(cot)
    sends = [for_route(cot_groups, z, odd) for odd in (0, 1)]
    token_rows, att_far, far_three, sends, own_far = both(
        (token_rows, att_far, far_three, sends, own_far)
    )
    far_one = swap(after(ffn_own, *token_rows), "mp", 1, "ffn_w_z1")
    att_parts = [v[None] for v in (att_z, *att_near, *att_far)] if square else list(att_far)
    x = whole_rows(jnp.stack(token_rows, 1), "tokens_core")
    ffn_far = flat(jnp.stack([far_two, far_three]))
    x, ffn_far, sends = both((x, ffn_far, sends))
    far_near = gather_near(ffn_far, "ffn_w2") if square else ()
    cot_rows = [to_image(sends[odd], odd, "cotangent") for odd in (0, 1)]
    n1, qkva, qkvb, mixa, mixb, part = att_forward(
        x.reshape(own_images, all_slots, width),
        gains[0:1],
        shifts[0:1],
        bias_rows,
        meta,
        att_places,
        att_parts,
    )
    part, n1, x, far_near, cot_rows, far_one = both((part, n1, x, far_near, cot_rows, far_one))
    part_other = swap(part, "dp", 1, "attended")
    if square:
        far_far = gather_far(*far_near, "ffn_w2")
        parts0 = [v[None] for v in (ffn_far, *far_near, *far_far)]
        places = pair_places
    else:
        parts0, places = [gather_plane(ffn_far, "ffn_w2")], [(0, 0, 0, 2, True)]
    go = whole_rows(jnp.stack(cot_rows, 1), "cotangent_core")
    go, parts0, part_other, far_one = both((go, parts0, part_other, far_one))
    here_near = gather_near(far_one, "ffn_w1") if square else ()
    up_rows = bias_all[:, 2:].reshape(n_i, fh)
    hidden, n2, n2t, got, sum_b, sum_g, upg1, *ffn_g0 = ffn_call(
        [x, part, part_other, out_b[0:1], gains[1:2], shifts[1:2], go, up_rows[2:], meta],
        n_q,
        2,
        fh,
        places,
        parts0,
        True,
        not square,
    )
    n2, ffn_g0, here_near = both((n2, ffn_g0, here_near))
    if square:
        here_far = gather_far(*here_near, "ffn_w1")
        parts1 = [ffn_own, *own_near, *own_far, far_one, *here_near, *here_far]
        parts1 = [flat(v)[None, None] for v in parts1]
        halves = ((0, 0, 2), (1, 0, 2), (2, 0, 2), (3, 0, 1), (3, 1, 1))
        places = [(j, i, t, n, False) for i in (0, 1) for j, t, n in halves]
    else:
        parts1 = [gather_plane(flat(jnp.stack([ffn_own, far_one])), "ffn_w0")]
    n2, parts1, ffn_g0 = both((n2, parts1, ffn_g0))
    reach_f0 = scatter_reach(ffn_g0, "ffn_g0")
    branch, gn2, upg0, *ffn_g1 = ffn_call(
        [n2, n2t, got, sum_b, sum_g, go, up_rows[:2], meta],
        n_q,
        2,
        fh,
        places,
        parts1,
        False,
        not square,
    )
    branch, gn2, ffn_g1, reach_f0 = both((branch, gn2, ffn_g1, reach_f0))

    last_f0 = scatter_last(ffn_g0, reach_f0, "ffn_g0")
    reach_f1 = scatter_reach(ffn_g1, "ffn_g1")
    gn2_other = swap(gn2, "dp", 1, "grad_norm_two")
    theirs = swap(row_half(branch, 1 - core), "dp", 1, "branch")
    gn2_other, theirs = both((gn2_other, theirs))
    out_half = row_half(hidden, core) + row_half(branch, core).astype(F32) + theirs.astype(F32) + out_b[1]
    gn2_other, out_half = both((gn2_other, rel(out_half.astype(BF))))
    out_first = from_image(out_half, z, 0, "block_out")
    gh, ght, gmixa, gmixb, sums = hidden_backward(
        meta, hidden, gn2, gn2_other, gains[1:2], go, n_q, att_places, att_parts
    )
    gmixa, last_f0, out_first, out_half = both((gmixa, last_f0, out_first, out_half))
    ffn2, ffn3 = scatter_sum(ffn_g0, reach_f0, last_f0)
    ffn_three = swap(ffn3, "mp", 1, "ffn_g_z3")
    out_last = from_image(out_half, z, 1, "block_out")
    gmixa, ffn2 = both((gmixa, ffn2))
    n1t, gqa, bias_a, *att_ga = att_backward_first(
        meta, gmixa, ght, n1, qkva, mixa, n_q, not square
    )
    n1t, gqa, reach_f1, ffn_three, out_last, att_ga = both(
        (n1t, gqa, reach_f1, ffn_three, out_last, att_ga)
    )
    reach_aa = scatter_reach(att_ga, "att_ga")
    last_f1 = scatter_last(ffn_g1, reach_f1, "ffn_g1")
    ffn_two = swap(add(ffn2, ffn_three), "mp", 2, "ffn_g_z2")
    gn1, bias_b, more_sums, *att_gb = att_backward_last(
        meta, x, gmixb, ght, n1t, gqa, qkvb, mixb, n_q, att_places, att_parts, not square
    )
    gn1, last_f1, att_gb, x, ffn_two, reach_aa = both((gn1, last_f1, att_gb, x, ffn_two, reach_aa))

    reach_ab = scatter_reach(att_gb, "att_gb")
    gn1_other = swap(row_half(gn1, 1 - core), "dp", 1, "grad_norm_one")
    ffn0, ffn1 = scatter_sum(ffn_g1, reach_f1, last_f1)
    ffn_one = swap(ffn1, "mp", 1, "ffn_g_z1")
    gn1 = row_half(gn1, core).astype(F32) + gn1_other.astype(F32)
    hat1, inv1 = normalise(after(row_half(x, core), gn1_other).astype(F32))
    input_half = row_half(gh, core) + norm_back(hat1, inv1, gains[0], gn1)
    input_half = rel(input_half.astype(BF))
    in_first = from_image(input_half, z, 0, "input_grad")
    reach_ab, input_half, in_first, upg0, upg1, bias_a, bias_b, sums, more_sums, reach_aa = both(
        (reach_ab, input_half, in_first, upg0, upg1, bias_a, bias_b, sums, more_sums, reach_aa)
    )
    in_last = from_image(input_half, z, 1, "input_grad")
    last_ab = scatter_last(att_gb, reach_ab, "att_gb")
    last_aa = scatter_last(att_ga, reach_aa, "att_ga")

    def placed(values):
        mine = jnp.concatenate([lax.dynamic_slice_in_dim(values, z ^ i, 1, 0) for i in range(n_i)])
        return jnp.stack([jnp.where(core == c, mine, jnp.zeros_like(mine)) for c in range(2)], 1)

    bias_a, bias_b = (v.reshape(3, 2, he) for v in (bias_a, bias_b))
    wide = [placed(jnp.concatenate([bias_a[t], bias_b[t]])) for t in (0, 2)]
    wide.append(placed(jnp.concatenate([upg0, upg1])))
    values = [*wide, rel(sums), rel(more_sums)]
    vector = jnp.concatenate([v.reshape(-1, 128) for v in values])
    last_ab, last_aa, vector, ffn_one = both((last_ab, last_aa, vector, ffn_one))
    att0, att1 = scatter_sum(att_ga, reach_aa, last_aa)
    att2, att3 = scatter_sum(att_gb, reach_ab, last_ab)
    att_three = swap(att3, "mp", 1, "att_g_z3")
    att_one = swap(att1, "mp", 1, "att_g_z1")
    vector = vector + swap(vector, "dp", 2, "sums_dp2")
    bit = 4
    while bit < n_dp:
        vector = vector + swap(vector, "dp", bit, "sums_dp" + str(bit))
        bit *= 2
    ffn_grad = add(ffn0, ffn_one, ffn_two)
    att_three, vector, in_last, ffn_grad, out_first, out_last = both(
        (att_three, vector, in_last, ffn_grad, out_first, out_last)
    )
    att_two = swap(add(att2, att_three), "mp", 2, "att_g_z2")
    vector = vector + swap(vector, "dp", 1, "sums_core")
    vector, ffn_grad = both((vector, ffn_grad))
    for bit in (1, 2):
        vector = vector + swap(vector, "mp", bit, "sums_z" + str(bit))
    att_grad = add(att0, att_one, att_two)
    in_routes = [in_first, in_last]
    block_out = joined_images([out_first, out_last], z)
    block_out = jnp.where(keep_mine, block_out, jnp.zeros_like(block_out))
    input_grad = joined_images(in_routes, z)

    def own_shard(grad, what):
        kinds, _, last = grad.shape
        pair = grad.reshape(kinds, 2, wq // 2, last)
        keep = lax.dynamic_index_in_dim(pair, core, 1, False)
        got = swap(lax.dynamic_index_in_dim(pair, 1 - core, 1, False), "dp", 1, what)
        return ordered_pair(keep, got, core, 2).reshape(kinds, wq // 2, 2 * last).astype(F32)

    att_shard, ffn_shard = own_shard(att_grad, "att_g_core"), own_shard(ffn_grad, "ffn_g_core")
    qkv_owned, proj_owned = att_shard[:3], jnp.transpose(att_shard[3])
    up_owned, down_owned = ffn_shard[0], jnp.transpose(ffn_shard[1])

    ends = [0]
    for v in values:
        ends.append(ends[-1] + v.size // 128)
    *wide, sums, more_sums = [
        vector[start:end].reshape(v.shape) for v, start, end in zip(values, ends, ends[1:])
    ]
    wide = [lax.dynamic_index_in_dim(v, z, 0, False).reshape(-1) for v in wide]
    bias_grad, upbias_grad = jnp.stack(wide[:2]), wide[2]
    gains_grad = jnp.stack([more_sums[0], sums[0] * 0.5])
    shifts_grad = jnp.stack([more_sums[1], sums[1] * 0.5])
    outbias_grad = sums[2:4] * 0.5
    return (
        block_out,
        input_grad,
        gains_grad,
        shifts_grad,
        qkv_owned,
        bias_grad,
        proj_owned,
        outbias_grad,
        up_owned,
        upbias_grad,
        down_owned,
    )


def solution(mesh):
    split = P("mp", "dp", None)
    return jax.shard_map(
        local,
        mesh=mesh,
        in_specs=(
            split,
            P("dp"),
            P(),
            P(),
            P(None, "dp", "mp"),
            P(None, "mp"),
            P("mp", "dp"),
            P(),
            P("dp", "mp"),
            P("mp"),
            P("mp", "dp"),
            split,
        ),
        out_specs=(
            split,
            split,
            P(),
            P(),
            P(None, "dp", "mp"),
            P(None, "mp"),
            P("mp", "dp"),
            P(),
            P("dp", "mp"),
            P("mp"),
            P("mp", "dp"),
        ),
        check_vma=False,
    )
```
